32 devices in a mesh: dp: 8 (over z, x), expert: 4 (over y, core).
Axes of the slice: x: 2, y: 2, z: 4, core: 2. Of those that a mesh axis runs over, the one named last changes fastest.
Arguments:
- out_grad: bfloat16 [512, 3072], P('expert'), may hold values from -1.1953125 to 1.1953125
- routes: int32 [512, 4], P('expert'), may hold values from 0 to 7, all different within a row; in each aligned block of 128 rows (0 to 127, 128 to 255, ...) at most 80 rows name the same one
- gate_values: float32 [512, 4], P('expert'), may hold values from 0.1 to 0.5
- layer_input: bfloat16 [512, 3072], P('expert'), may hold values from -6 to 6
- w_gate: bfloat16 [8, 3072, 8192], P('expert', None, 'dp'), may hold values from -0.109375 to 0.109375
- w_up: bfloat16 [8, 3072, 8192], P('expert', None, 'dp'), may hold values from -0.109375 to 0.109375
- w_down: bfloat16 [8, 3072, 8192], P('expert', None, 'dp'), may hold values from -0.109375 to 0.109375
Outputs:
- input_grad: bfloat16 [512, 3072], P('expert')
- grad_gate: float32 [8, 3072, 8192], P('expert', None, 'dp')
- grad_up: float32 [8, 3072, 8192], P('expert', None, 'dp')
The draws below stay inside these ranges and needn't reach their ends.
Inputs may be any that keep to these rules, and one draw needn't show every extreme that they name: In every aligned block of 128 tokens (the tokens of one index of expert) no expert is named by more than 80 routes, a bound that some block reaches; the 4 experts of a token differ.
All inputs are finite; a program needn't handle non-finite values.
Results may differ from the reference program's by a relative error of at most 0.024.
Values may be sent and summed in bfloat16 or wider, within the bound.
No kernel may reach another device: no remote copies, remote signals or barrier semaphores. Data moves between devices by JAX's collectives and lax.ppermute only.
A program may use at most 192 MiB of HBM per device.

```python
import math
import jax
import jax.numpy as jnp
import numpy as np
from jax import lax

D = 3072
TOP = 4
FW = 8192
EXPERTS = 8
TOK_DEV = 128
MOST = 80
TOKENS = 512
N_DP = 8
N_EXPERT = 4


def block_scale(key, shape, pieces, least, largest):
    def one(position, parts):
        steps = jax.random.uniform(jax.random.fold_in(jax.random.fold_in(key, 6), position), (parts,), jnp.float32, least / len(pieces), largest / len(pieces))
        return jnp.repeat(jnp.exp(steps), shape[position] // parts).reshape((-1,) + (1,) * (len(shape) - position - 1))

    level = one(*pieces[0])
    for cut in pieces[1:]:
        level = level * one(*cut)
    return level


def assign_block(stream_key, own, number, rows, amount, top, reach, skew):
    order = jax.random.permutation(stream_key, amount)
    packed, usual = load_shares(amount, rows * top, reach, skew, True), load_shares(amount, rows * top, reach, skew, False)
    places = jnp.arange(amount)

    def named(lengths, rotation):
        used = int((lengths > 0).sum())
        fixed = max(1, used // 4)
        passed = fixed + (places - fixed + rotation * (used - fixed)) % max(1, amount - fixed)
        return jnp.zeros((amount,), jnp.int32).at[order[jnp.where(places < fixed, places, passed)]].set(jnp.asarray(lengths, jnp.int32))

    lengths = jnp.where(number % 4 == 0, named(packed, number // 4), named(usual, number - number // 4 - 1))
    mixed = jax.random.permutation(jax.random.fold_in(own, 3), amount)
    source_of, sink = mixed[0:amount // 2 * 2:2], mixed[1:amount // 2 * 2:2]
    slack = jnp.minimum(lengths[source_of] - 1, reach - lengths[sink]) // 2
    slack = jnp.where((source_of == order[0]) | (sink == order[0]) | (lengths[sink] == 0), 0, jnp.maximum(slack, 0))
    passed = jax.random.randint(jax.random.fold_in(own, 4), (amount // 2,), 0, 1 << 20) % (slack + 1)
    lengths = lengths.at[source_of].add(-passed).at[sink].add(passed)
    items = jnp.searchsorted(jnp.cumsum(lengths), jnp.arange(rows * top), side="right").astype(jnp.int32)
    grid = items.reshape(top, rows).T
    grid = grid[jax.random.permutation(jax.random.fold_in(own, 1), rows)]
    rotation = jax.random.randint(jax.random.fold_in(own, 2), (rows, 1), 0, top)
    return jnp.take_along_axis(grid, (jnp.arange(top)[None, :] + rotation) % top, axis=1)


def load_shares(number_of, total, bound, slope, full):
    weights = [(1 << 20) // math.isqrt(rank ** slope) + 1 for rank in range(1, number_of + 1)]
    largest = bound if full else min(bound, max(-(-total // number_of), total * weights[0] // sum(weights)))
    least = 1 if total - largest >= number_of - 1 else 0
    given, surplus = [largest] + [least] * (number_of - 1), total - largest - least * (number_of - 1)
    while surplus > 0:
        free = [i for i in range(1, number_of) if given[i] < largest] or [i for i in range(1, number_of) if given[i] < bound]
        pool, left = sum([weights[i] for i in free]), surplus
        for i in free:
            addition = min(bound - given[i], max(1, left * weights[i] // pool), surplus)
            given[i] = given[i] + addition
            surplus = surplus - addition
    return np.array(given)


def scatter_about(rng, dims, spread, bound, shards=(), kind=jnp.bfloat16):
    result = jax.random.normal(rng, dims, jnp.float32) * spread
    if len(shards) > 0:
        result = block_scale(rng, dims, shards, -0.22, 0.18) * result
    return jnp.clip(result, min=-bound, max=bound).astype(kind)


def setup_inputs(seed: int = 0) -> dict:
    keys = jax.random.split(jax.random.key(seed), 8)
    out_grad = scatter_about(keys[0], (TOKENS, D), 0.2, 1.1953125, ((0, 4),))
    routes_keys = jax.random.split(jax.random.fold_in(keys[1], 1), TOKENS // TOK_DEV)
    routes_turns = jax.random.permutation(jax.random.fold_in(keys[1], 3), TOKENS // TOK_DEV)
    routes = jax.vmap(lambda own, number: assign_block(jax.random.fold_in(keys[1], 2), own, number, TOK_DEV, EXPERTS, TOP, MOST, 1))(routes_keys, routes_turns).reshape((TOKENS, TOP))
    gate_values = jnp.clip(0.1 + 0.4 * jax.random.uniform(keys[2], (TOKENS, TOP), jnp.float32) ** block_scale(keys[2], (TOKENS, TOP), ((0, 4),), -0.2, 0.2), 0.1, 0.5)
    layer_input = scatter_about(keys[3], (TOKENS, D), 1.0, 6.0, ((0, 4),))
    w_gate = scatter_about(keys[4], (EXPERTS, D, FW), D ** -0.5, 0.109375, ((0, 4), (2, 8)))
    w_up = scatter_about(keys[5], (EXPERTS, D, FW), D ** -0.5, 0.109375, ((0, 4), (2, 8)))
    w_down = scatter_about(keys[6], (EXPERTS, D, FW), D ** -0.5, 0.109375, ((0, 4), (2, 8)))
    return dict(out_grad=out_grad, routes=routes, gate_values=gate_values, layer_input=layer_input, w_gate=w_gate, w_up=w_up, w_down=w_down)


def slot_numbers(block_routes):
    experts_row = jnp.arange(EXPERTS, dtype=jnp.int32)[None, :]
    onehot = (block_routes[:, None] == experts_row).astype(jnp.int32)
    earlier = jnp.cumsum(onehot, axis=0) - onehot
    return jnp.sum(earlier * onehot, axis=1).astype(jnp.int32)


def one_expert(inputs_one):
    rows_in, grads_in, weight_gate, weight_up, weight_down = inputs_one
    highest = lax.Precision.HIGHEST
    rows_float = rows_in.reshape(-1, D).astype(jnp.float32)
    grads_float = grads_in.reshape(-1, D).astype(jnp.float32)
    gate_float = weight_gate.astype(jnp.float32)
    up_float = weight_up.astype(jnp.float32)
    down_float = weight_down.astype(jnp.float32)
    gate_pre = jnp.dot(rows_float, gate_float, precision=highest, preferred_element_type=jnp.float32)
    up_pre = jnp.dot(rows_float, up_float, precision=highest, preferred_element_type=jnp.float32)
    sigmoid_gate = jax.nn.sigmoid(gate_pre)
    activated = gate_pre * sigmoid_gate
    hidden_grad = jnp.dot(grads_float, down_float, precision=highest, preferred_element_type=jnp.float32)
    up_grad = (hidden_grad * activated).astype(jnp.bfloat16)
    gate_grad = (hidden_grad * up_pre * sigmoid_gate * (1.0 + gate_pre * (1.0 - sigmoid_gate))).astype(jnp.bfloat16)
    gate_grad_float = gate_grad.astype(jnp.float32)
    up_grad_float = up_grad.astype(jnp.float32)
    units = FW // N_DP

    def group_term(group, total):
        first = (group * units).astype(jnp.int32)
        part_gate = lax.dynamic_slice_in_dim(gate_grad_float, first, units, 1)
        part_up = lax.dynamic_slice_in_dim(up_grad_float, first, units, 1)
        cols_gate = lax.dynamic_slice_in_dim(gate_float, first, units, 1)
        cols_up = lax.dynamic_slice_in_dim(up_float, first, units, 1)
        partial_value = jnp.dot(part_gate, cols_gate.T, precision=highest, preferred_element_type=jnp.float32)
        partial_value = partial_value + jnp.dot(part_up, cols_up.T, precision=highest, preferred_element_type=jnp.float32)
        rounded = lax.optimization_barrier(partial_value.astype(jnp.bfloat16))
        return total + rounded.astype(jnp.float32)

    start_total = jnp.zeros((rows_float.shape[0], D), jnp.float32)
    route_sum = lax.fori_loop(jnp.int32(0), jnp.int32(N_DP), group_term, start_total)
    route_sum = route_sum.astype(jnp.bfloat16).reshape(N_EXPERT, MOST, D)
    term_gate = jnp.dot(rows_float.T, gate_grad_float, precision=highest, preferred_element_type=jnp.float32)
    term_up = jnp.dot(rows_float.T, up_grad_float, precision=highest, preferred_element_type=jnp.float32)
    return route_sum, term_gate, term_up


def reference(out_grad, routes, gate_values, layer_input, w_gate, w_up, w_down):
    blocks = N_EXPERT
    flat_routes = routes.reshape(blocks, TOK_DEV * TOP)
    slot_index = jax.vmap(slot_numbers)(flat_routes)
    target = (flat_routes * MOST + slot_index).astype(jnp.int32)
    scaled = gate_values.reshape(blocks, TOK_DEV, TOP, 1) * out_grad.reshape(blocks, TOK_DEV, 1, D).astype(jnp.float32)
    scaled = scaled.reshape(blocks, TOK_DEV * TOP, D).astype(jnp.bfloat16)
    copies = jnp.broadcast_to(layer_input.reshape(blocks, TOK_DEV, 1, D), (blocks, TOK_DEV, TOP, D))
    copies = copies.reshape(blocks, TOK_DEV * TOP, D)
    block_index = jnp.broadcast_to(jnp.arange(blocks, dtype=jnp.int32)[:, None], target.shape)
    blank_slots = jnp.zeros((blocks, EXPERTS * MOST, D), jnp.bfloat16)
    sent_grads = blank_slots.at[block_index, target].set(scaled)
    sent_grads = sent_grads.reshape(blocks, EXPERTS, MOST, D).transpose(1, 0, 2, 3)
    sent_rows = blank_slots.at[block_index, target].set(copies)
    sent_rows = sent_rows.reshape(blocks, EXPERTS, MOST, D).transpose(1, 0, 2, 3)
    route_all, grad_gate, grad_up = lax.map(one_expert, (sent_rows, sent_grads, w_gate, w_up, w_down))
    returned = route_all.transpose(1, 0, 2, 3).reshape(blocks, EXPERTS * MOST, D)
    picked = jnp.take_along_axis(returned, target[:, :, None], axis=1).astype(jnp.float32)
    input_grad = jnp.sum(picked.reshape(TOKENS, TOP, D), axis=1).astype(jnp.bfloat16)
    return input_grad, grad_gate, grad_up
```

```python
import functools

import jax
import jax.numpy as jnp
from jax import lax
from jax.experimental import pallas as pl
from jax.experimental.pallas import tpu as pltpu
from jax.sharding import PartitionSpec as P

EXPERTS = 8
MOST = 80
UNIT_TILE = 256
FEATURE_TILE = 512
VMEM_BYTES = 52 * 1024 * 1024
BF16 = jnp.bfloat16
F32 = jnp.float32
NN = (((1,), (0,)), ((), ()))
NT = (((1,), (1,)), ((), ()))
TN = (((0,), (0,)), ((), ()))


def dot(a, b, dims=NN):
    return lax.dot_general(a, b, dims, preferred_element_type=F32)


def params(count):
    return pltpu.CompilerParams(
        dimension_semantics=("arbitrary",) * count, vmem_limit_bytes=VMEM_BYTES
    )


def whole(shape):
    return pl.BlockSpec(
        shape, lambda *_: (0,) * len(shape), pipeline_mode=pl.Buffered(buffer_count=1)
    )


def one_hot(slot_row):
    slots = lax.broadcasted_iota(jnp.int32, (MOST, slot_row.shape[1]), 0)
    return slots == slot_row.astype(jnp.int32)


def pick(chosen, pieces, block, tokens, columns):
    first, total, at = block * tokens, None, 0
    for piece in pieces:
        low, high = max(first, at), min(first + tokens, at + piece.shape[0])
        if low < high:
            term = dot(chosen[:, low - first : high - first], piece[low - at : high - at, columns])
            total = term if total is None else total + term
        at += piece.shape[0]
    return total


def column_chunks(features):
    step = 768 if features % 768 == 0 else features
    return [slice(c, c + step) for c in range(0, features, step)]


def forward_kernel(count, *refs):
    pieces, (slot, w_gate, w_up, rows, act, slope) = refs[:count], refs[count:]
    blocks, tokens = slot.shape[1:]

    @pl.when(pl.program_id(1) == 0)
    def _():
        for b in range(blocks):
            chosen = one_hot(slot[0, b : b + 1, :]).astype(BF16)
            for cols in column_chunks(rows.shape[2]):
                rows[0, b * MOST : (b + 1) * MOST, cols] = pick(
                    chosen, pieces, b, tokens, cols
                ).astype(BF16)

    x = rows[0]
    gate = dot(x, w_gate[0])
    up = dot(x, w_up[0])
    sig = jax.nn.sigmoid(gate)
    act[0] = gate * sig
    slope[0] = up * sig * (1.0 + gate * (1.0 - sig))


def forward(pieces, slot, w_gate, w_up):
    experts, blocks, tokens = slot.shape
    _, features, units = w_gate.shape
    tile = min(UNIT_TILE, units)
    slots = blocks * MOST
    weight = pl.BlockSpec((1, features, tile), lambda l, f: (l, 0, f))
    unit = pl.BlockSpec((1, slots, tile), lambda l, f: (l, 0, f))
    return pl.pallas_call(
        functools.partial(forward_kernel, len(pieces)),
        grid=(experts, units // tile),
        in_specs=[whole(p.shape) for p in pieces]
        + [pl.BlockSpec((1, blocks, tokens), lambda l, f: (l, 0, 0)), weight, weight],
        out_specs=[pl.BlockSpec((1, slots, features), lambda l, f: (l, 0, 0)), unit, unit],
        out_shape=[
            jax.ShapeDtypeStruct((experts, slots, features), BF16),
            jax.ShapeDtypeStruct((experts, slots, units), F32),
            jax.ShapeDtypeStruct((experts, slots, units), F32),
        ],
        compiler_params=params(2),
        cost_estimate=pl.CostEstimate(
            flops=4 * experts * slots * features * units,
            bytes_accessed=4 * experts * features * units,
            transcendentals=experts * slots * units,
        ),
    )(*pieces, slot, w_gate, w_up)


def backward_kernel(count, groups, unit_steps, *refs):
    pieces = refs[:count]
    slot, weight, act, slope, w_down, w_gate, w_up = refs[count : count + 7]
    gate_grad, up_grad = refs[count + 7 : count + 9]
    sums = refs[count + 9 : count + 9 + len(groups)]
    grads, all_gate, all_up = refs[count + 9 + len(groups) :]
    experts, blocks, tokens = slot.shape
    tile = w_down.shape[2]
    tiles = unit_steps // experts
    step = pl.program_id(0)

    @pl.when(step < unit_steps)
    def _():
        expert, place = step // tiles, step % tiles

        @pl.when(place == 0)
        def _():
            for b in range(blocks):
                mask = one_hot(slot[expert, b : b + 1, :])
                scale = jnp.sum(
                    jnp.where(mask, weight[expert, b : b + 1, :], 0.0), axis=1, keepdims=True
                )
                chosen = mask.astype(BF16)
                for cols in column_chunks(grads.shape[1]):
                    taken = pick(chosen, pieces, b, tokens, cols)
                    grads[b * MOST : (b + 1) * MOST, cols] = (taken * scale).astype(BF16)

        hidden = dot(grads[...], w_down[0])
        up_part = (hidden * act[0]).astype(BF16)
        gate_part = (hidden * slope[0]).astype(BF16)
        up_grad[0] = up_part
        gate_grad[0] = gate_part
        cols = pl.ds(pl.multiple_of(place * tile, tile), tile)
        all_up[expert, :, cols] = up_part
        all_gate[expert, :, cols] = gate_part

    @pl.when(step >= unit_steps)
    def _():
        partial = [
            (
                dot(all_gate[l], w_gate[l], NT) + dot(all_up[l], w_up[l], NT)
            ).astype(BF16)
            for l in range(experts)
        ]
        for out, members in zip(sums, groups):
            for place, b in enumerate(members):
                total = None
                for l in range(experts):
                    chosen = one_hot(slot[l, b : b + 1, :]).astype(BF16)
                    term = dot(chosen, partial[l][b * MOST : (b + 1) * MOST], TN)
                    total = term if total is None else total + term
                out[place * tokens : (place + 1) * tokens] = total.astype(BF16)


def backward(pieces, slot, weight, act, slope, w_down, w_gate, w_up, groups):
    experts, blocks, tokens = slot.shape
    _, features, units = w_gate.shape
    tile = min(UNIT_TILE, units)
    wide = FEATURE_TILE
    tiles = units // tile
    slots = blocks * MOST
    unit_steps = experts * tiles
    first = lambda i: jnp.minimum(i, unit_steps - 1)
    second = lambda i: jnp.maximum(i - unit_steps, 0)
    unit = pl.BlockSpec((1, slots, tile), lambda i: (first(i) // tiles, 0, first(i) % tiles))
    down = pl.BlockSpec((1, features, tile), lambda i: (first(i) // tiles, 0, first(i) % tiles))
    across = pl.BlockSpec((experts, wide, units), lambda i: (0, second(i), 0))
    return pl.pallas_call(
        functools.partial(backward_kernel, len(pieces), groups, unit_steps),
        grid=(unit_steps + features // wide,),
        in_specs=[whole(p.shape) for p in pieces]
        + [whole(slot.shape), whole(slot.shape), unit, unit, down, across, across],
        out_specs=[unit, unit]
        + [pl.BlockSpec((len(g) * tokens, wide), lambda i: (0, second(i))) for g in groups],
        out_shape=[jax.ShapeDtypeStruct((experts, slots, units), BF16)] * 2
        + [jax.ShapeDtypeStruct((len(g) * tokens, features), BF16) for g in groups],
        scratch_shapes=[
            pltpu.VMEM((slots, features), BF16),
            pltpu.VMEM((experts, slots, units), BF16),
            pltpu.VMEM((experts, slots, units), BF16),
        ],
        compiler_params=params(1),
        cost_estimate=pl.CostEstimate(
            flops=6 * experts * slots * features * units,
            bytes_accessed=6 * experts * features * units,
            transcendentals=0,
        ),
    )(*pieces, slot, weight, act, slope, w_down, w_gate, w_up)


def weights_kernel(rows, gate_grad, up_grad, *refs):
    grad_gate, grad_up = refs[-2:]
    grad_gate[0] = dot(rows[0], gate_grad[0], TN)
    grad_up[0] = dot(rows[0], up_grad[0], TN)


def weight_grads(rows, gate_grad, up_grad, expert, before):
    experts, slots, features = rows.shape
    units = gate_grad.shape[2]
    wide = FEATURE_TILE
    unit = pl.BlockSpec((1, slots, units), lambda d: (expert, 0, 0))
    out = pl.BlockSpec((1, wide, units), lambda d: (expert, d, 0))
    kept = [] if before is None else list(before)
    return pl.pallas_call(
        weights_kernel,
        grid=(features // wide,),
        in_specs=[pl.BlockSpec((1, slots, wide), lambda d: (expert, 0, d)), unit, unit]
        + [pl.BlockSpec(memory_space=pl.ANY)] * len(kept),
        out_specs=[out, out],
        out_shape=[jax.ShapeDtypeStruct((experts, features, units), F32)] * 2,
        input_output_aliases={3 + i: i for i in range(len(kept))},
        compiler_params=params(1),
        cost_estimate=pl.CostEstimate(
            flops=4 * slots * features * units,
            bytes_accessed=8 * features * units,
            transcendentals=0,
        ),
    )(rows, gate_grad, up_grad, *kept)


def route_table(routes, gate_values):
    tokens = routes.shape[0]
    experts = jnp.arange(EXPERTS, dtype=jnp.int32)[:, None, None]
    match = routes.T[None] == experts
    member = jnp.any(match, axis=1)
    gate = jnp.sum(jnp.where(match, gate_values.T[None], 0.0), axis=1)
    place = jnp.arange(tokens, dtype=jnp.int32)
    earlier = (place[:, None] < place[None, :]).astype(BF16)
    slot = jnp.where(member, dot(member.astype(BF16), earlier), -1.0)
    return jnp.stack([slot, gate], axis=1)


def flip(value, axis, bit):
    count = lax.axis_size(axis)
    return lax.ppermute(value, axis, [(i, i ^ bit) for i in range(count)])


def fetch_near(block):
    side = lax.axis_index("dp") % 2
    half = block.shape[0] // 2
    mine = lax.dynamic_slice_in_dim(block, side * half, half, 0)
    across = flip(mine, "expert", 2)
    sibling = flip(block, "expert", 1)
    beside = flip(across, "dp", 1)
    return [
        block, sibling, across, beside, flip(across, "expert", 1), flip(beside, "expert", 1)
    ]


def local_near(out_grad, routes, gate_values, layer_input, w_gate, w_up, w_down):
    experts = w_gate.shape[0]
    me = lax.axis_index("expert")
    side = lax.axis_index("dp") % 2
    tokens = out_grad.shape[0]
    rows_in = fetch_near(layer_input)
    grads_in = fetch_near(out_grad)
    table = route_table(routes, gate_values)
    tables = []
    for r in range(4):
        part = lax.dynamic_slice_in_dim(table, (me ^ r) * experts, experts, 0)
        if r > 0:
            part = flip(part, "expert", r)
        if r > 1:
            part = jnp.where(side == 1, jnp.roll(part, tokens // 2, axis=2), part)
        tables.append(part)
    table = jnp.stack(tables, axis=2)
    slot, weight = table[:, 0], table[:, 1]
    rows, act, slope = forward(rows_in, slot, w_gate, w_up)
    gate_grad, up_grad, kept, sent = backward(
        grads_in, slot, weight, act, slope, w_down, w_gate, w_up, ((0, 2), (1, 3))
    )
    grads = None
    for l in range(experts):
        grads = weight_grads(rows, gate_grad, up_grad, l, grads)
    chip = kept.astype(F32) + flip(sent, "expert", 1).astype(F32)
    own, far = chip[:tokens], chip[tokens:].astype(BF16)
    got = flip(far, "expert", 2)
    got = jnp.where(side == 1, jnp.roll(got, tokens // 2, axis=0), got)
    total = (own + got.astype(F32)).astype(BF16)
    return (lax.psum(total, "dp"), *grads)


def local_any(out_grad, routes, gate_values, layer_input, w_gate, w_up, w_down):
    experts = w_gate.shape[0]
    me = lax.axis_index("expert")
    rows_in = lax.all_gather(layer_input, "expert", tiled=True)
    grads_in = lax.all_gather(out_grad, "expert", tiled=True)
    table = lax.all_gather(route_table(routes, gate_values), "expert")
    table = lax.dynamic_slice_in_dim(table, me * experts, experts, 1)
    slot, weight = table[:, :, 0].swapaxes(0, 1), table[:, :, 1].swapaxes(0, 1)
    rows, act, slope = forward([rows_in], slot, w_gate, w_up)
    groups = (tuple(range(slot.shape[1])),)
    gate_grad, up_grad, sums = backward(
        [grads_in], slot, weight, act, slope, w_down, w_gate, w_up, groups
    )
    grads = None
    for l in range(experts):
        grads = weight_grads(rows, gate_grad, up_grad, l, grads)
    own = lax.psum_scatter(sums, "expert", scatter_dimension=0, tiled=True)
    return (lax.psum(own, "dp"), *grads)


def solution(mesh):
    near = mesh.shape["dp"] == 8 and mesh.shape["expert"] == 4
    placed = (
        P("expert", None),
        P("expert", None),
        P("expert", None),
        P("expert", None),
        P("expert", None, "dp"),
        P("expert", None, "dp"),
        P("expert", None, "dp"),
    )
    return jax.shard_map(
        local_near if near else local_any,
        mesh=mesh,
        in_specs=placed,
        out_specs=(P("expert", None), P("expert", None, "dp"), P("expert", None, "dp")),
        check_vma=False,
    )
```

```python
import functools

import jax
import jax.numpy as jnp
from jax import lax
from jax.experimental import pallas as pl
from jax.experimental.pallas import tpu as pltpu
from jax.sharding import PartitionSpec as P

EXPERTS = 8
MOST = 80
UNIT_TILE = 512
FEATURE_TILE = 256
VMEM_BYTES = 52 * 1024 * 1024
BF16 = jnp.bfloat16
F32 = jnp.float32
NN = (((1,), (0,)), ((), ()))
NT = (((1,), (1,)), ((), ()))
TN = (((0,), (0,)), ((), ()))


def dot(a, b, dims=NN):
    return lax.dot_general(a, b, dims, preferred_element_type=F32)


def params(count):
    return pltpu.CompilerParams(
        dimension_semantics=("arbitrary",) * count, vmem_limit_bytes=VMEM_BYTES
    )


def whole(shape):
    return pl.BlockSpec(
        shape, lambda *_: (0,) * len(shape), pipeline_mode=pl.Buffered(buffer_count=1)
    )


def one_hot(slot_row):
    slots = lax.broadcasted_iota(jnp.int32, (MOST, slot_row.shape[1]), 0)
    return slots == slot_row.astype(jnp.int32)


def pick(chosen, pieces, block, tokens, columns):
    first, total, at = block * tokens, None, 0
    for piece in pieces:
        low, high = max(first, at), min(first + tokens, at + piece.shape[0])
        if low < high:
            term = dot(chosen[:, low - first : high - first], piece[low - at : high - at, columns])
            total = term if total is None else total + term
        at += piece.shape[0]
    return total


def column_chunks(features):
    step = 768 if features % 768 == 0 else features
    return [slice(c, c + step) for c in range(0, features, step)]


def forward_kernel(count, *refs):
    pieces, (slot, w_gate, w_up, rows, act, slope) = refs[:count], refs[count:]
    blocks, tokens = slot.shape[1:]

    @pl.when(pl.program_id(1) == 0)
    def _():
        for b in range(blocks):
            chosen = one_hot(slot[0, b : b + 1, :]).astype(BF16)
            for cols in column_chunks(rows.shape[2]):
                rows[0, b * MOST : (b + 1) * MOST, cols] = pick(
                    chosen, pieces, b, tokens, cols
                ).astype(BF16)

    x = rows[0]
    gate = dot(x, w_gate[0])
    up = dot(x, w_up[0])
    sig = jax.nn.sigmoid(gate)
    act[0] = gate * sig
    slope[0] = up * sig * (1.0 + gate * (1.0 - sig))


def forward(pieces, slot, w_gate, w_up):
    experts, blocks, tokens = slot.shape
    _, features, units = w_gate.shape
    tile = min(UNIT_TILE, units)
    slots = blocks * MOST
    weight = pl.BlockSpec((1, features, tile), lambda l, f: (l, 0, f))
    unit = pl.BlockSpec((1, slots, tile), lambda l, f: (l, 0, f))
    return pl.pallas_call(
        functools.partial(forward_kernel, len(pieces)),
        grid=(experts, units // tile),
        in_specs=[whole(p.shape) for p in pieces]
        + [pl.BlockSpec((1, blocks, tokens), lambda l, f: (l, 0, 0)), weight, weight],
        out_specs=[pl.BlockSpec((1, slots, features), lambda l, f: (l, 0, 0)), unit, unit],
        out_shape=[
            jax.ShapeDtypeStruct((experts, slots, features), BF16),
            jax.ShapeDtypeStruct((experts, slots, units), F32),
            jax.ShapeDtypeStruct((experts, slots, units), F32),
        ],
        compiler_params=params(2),
        cost_estimate=pl.CostEstimate(
            flops=4 * experts * slots * features * units,
            bytes_accessed=4 * experts * features * units,
            transcendentals=experts * slots * units,
        ),
    )(*pieces, slot, w_gate, w_up)


def hidden_kernel(count, *refs):
    pieces, (slot, weight, act, slope, w_down, gate_grad, up_grad, grads) = (
        refs[:count],
        refs[count:],
    )
    blocks, tokens = slot.shape[1:]

    @pl.when(pl.program_id(1) == 0)
    def _():
        for b in range(blocks):
            mask = one_hot(slot[0, b : b + 1, :])
            scale = jnp.sum(
                jnp.where(mask, weight[0, b : b + 1, :], 0.0), axis=1, keepdims=True
            )
            chosen = mask.astype(BF16)
            for cols in column_chunks(grads.shape[1]):
                taken = pick(chosen, pieces, b, tokens, cols)
                grads[b * MOST : (b + 1) * MOST, cols] = (taken * scale).astype(BF16)

    hidden = dot(grads[...], w_down[0])
    up_grad[0] = (hidden * act[0]).astype(BF16)
    gate_grad[0] = (hidden * slope[0]).astype(BF16)


def hidden_grads(pieces, slot, weight, act, slope, w_down):
    experts, blocks, tokens = slot.shape
    _, features, units = w_down.shape
    tile = min(UNIT_TILE, units)
    slots = blocks * MOST
    unit = pl.BlockSpec((1, slots, tile), lambda l, f: (l, 0, f))
    table = pl.BlockSpec((1, blocks, tokens), lambda l, f: (l, 0, 0))
    return pl.pallas_call(
        functools.partial(hidden_kernel, len(pieces)),
        grid=(experts, units // tile),
        in_specs=[whole(p.shape) for p in pieces]
        + [table, table, unit, unit]
        + [pl.BlockSpec((1, features, tile), lambda l, f: (l, 0, f))],
        out_specs=[unit, unit],
        out_shape=[jax.ShapeDtypeStruct((experts, slots, units), BF16)] * 2,
        scratch_shapes=[pltpu.VMEM((slots, features), BF16)],
        compiler_params=params(2),
        cost_estimate=pl.CostEstimate(
            flops=2 * experts * slots * features * units,
            bytes_accessed=2 * experts * features * units,
            transcendentals=0,
        ),
    )(*pieces, slot, weight, act, slope, w_down)


def inputs_kernel(groups, slot, gate_grad, up_grad, w_gate, w_up, *sums):
    experts, _, tokens = slot.shape
    partial = [
        (dot(gate_grad[l], w_gate[l], NT) + dot(up_grad[l], w_up[l], NT)).astype(BF16)
        for l in range(experts)
    ]
    for out, members in zip(sums, groups):
        for place, b in enumerate(members):
            total = None
            for l in range(experts):
                chosen = one_hot(slot[l, b : b + 1, :]).astype(BF16)
                term = dot(chosen, partial[l][b * MOST : (b + 1) * MOST], TN)
                total = term if total is None else total + term
            out[place * tokens : (place + 1) * tokens] = total.astype(BF16)


def input_sums(slot, gate_grad, up_grad, w_gate, w_up, groups, part, parts):
    experts, blocks, tokens = slot.shape
    _, features, units = w_gate.shape
    wide = FEATURE_TILE
    steps = features // parts // wide
    slots = blocks * MOST
    across = pl.BlockSpec((experts, wide, units), lambda i: (0, part * steps + i, 0))
    return pl.pallas_call(
        functools.partial(inputs_kernel, groups),
        grid=(steps,),
        in_specs=[whole(slot.shape), whole(gate_grad.shape), whole(up_grad.shape), across, across],
        out_specs=[pl.BlockSpec((len(g) * tokens, wide), lambda i: (0, i)) for g in groups],
        out_shape=[
            jax.ShapeDtypeStruct((len(g) * tokens, features // parts), BF16) for g in groups
        ],
        compiler_params=params(1),
        cost_estimate=pl.CostEstimate(
            flops=4 * experts * slots * features * units // parts,
            bytes_accessed=4 * experts * features * units // parts,
            transcendentals=0,
        ),
    )(slot, gate_grad, up_grad, w_gate, w_up)


def weights_kernel(rows, gate_grad, up_grad, *refs):
    grad_gate, grad_up = refs[-2:]
    grad_gate[0] = dot(rows[0], gate_grad[0], TN)
    grad_up[0] = dot(rows[0], up_grad[0], TN)


def weight_grads(rows, gate_grad, up_grad, before, expert, part=0, parts=1):
    experts, slots, features = rows.shape
    units = gate_grad.shape[2]
    wide = FEATURE_TILE
    steps = features // parts // wide
    unit = pl.BlockSpec((1, slots, units), lambda d: (expert, 0, 0))
    out = pl.BlockSpec((1, wide, units), lambda d: (expert, part * steps + d, 0))
    kept = [] if before is None else list(before)
    return pl.pallas_call(
        weights_kernel,
        grid=(steps,),
        in_specs=[
            pl.BlockSpec((1, slots, wide), lambda d: (expert, 0, part * steps + d)), unit, unit
        ]
        + [pl.BlockSpec(memory_space=pl.ANY)] * len(kept),
        out_specs=[out, out],
        out_shape=[jax.ShapeDtypeStruct((experts, features, units), F32)] * 2,
        input_output_aliases={3 + i: i for i in range(len(kept))},
        compiler_params=params(1),
        cost_estimate=pl.CostEstimate(
            flops=4 * slots * features * units // parts,
            bytes_accessed=8 * features * units // parts,
            transcendentals=0,
        ),
    )(rows, gate_grad, up_grad, *kept)


def route_table(routes, gate_values):
    tokens = routes.shape[0]
    experts = jnp.arange(EXPERTS, dtype=jnp.int32)[:, None, None]
    match = routes.T[None] == experts
    member = jnp.any(match, axis=1)
    gate = jnp.sum(jnp.where(match, gate_values.T[None], 0.0), axis=1)
    place = jnp.arange(tokens, dtype=jnp.int32)
    earlier = (place[:, None] < place[None, :]).astype(BF16)
    slot = jnp.where(member, dot(member.astype(BF16), earlier), -1.0)
    return jnp.stack([slot, gate], axis=1)


def flip(value, axis, bit):
    count = lax.axis_size(axis)
    return lax.ppermute(value, axis, [(i, i ^ bit) for i in range(count)])


def swap_order(value, side, pair, dim):
    shape = value.shape
    value = value.reshape(shape[:dim] + (2, 2, shape[dim] // 4) + shape[dim + 1 :])
    value = jnp.where(side == 1, jnp.flip(value, dim), value)
    return jnp.where(pair == 1, jnp.flip(value, dim + 1), value).reshape(shape)


def add(*terms):
    total = terms[0].astype(F32)
    for term in terms[1:]:
        total = total + term.astype(F32)
    return total.astype(BF16)


def fetch_near(block, mine):
    across = flip(mine, "expert", 2)
    sibling = flip(block, "expert", 1)
    beside = flip(across, "dp", 1)
    return [
        block, sibling, across, beside, flip(across, "expert", 1), flip(beside, "expert", 1)
    ]


def local_near(out_grad, routes, gate_values, layer_input, w_gate, w_up, w_down):
    experts, features, _ = w_gate.shape
    me = lax.axis_index("expert")
    position = lax.axis_index("dp")
    side, pair = position % 2, position // 2 % 2
    tokens = out_grad.shape[0]
    half, quarter = tokens // 2, tokens // 4
    x_mine = lax.dynamic_slice_in_dim(layer_input, side * half, half, 0)
    g_mine = lax.dynamic_slice_in_dim(out_grad, side * half, half, 0)
    x_mine, g_mine, layer_input, out_grad, routes = lax.optimization_barrier(
        (x_mine, g_mine, layer_input, out_grad, routes)
    )
    rows_in = fetch_near(layer_input, x_mine)
    grads_in = fetch_near(out_grad, g_mine)
    table = route_table(routes, gate_values)
    tables = []
    for r in range(4):
        part = lax.dynamic_slice_in_dim(table, (me ^ r) * experts, experts, 0)
        tables.append(flip(part, "expert", r) if r > 0 else part)
    table = jnp.stack(tables, axis=2)
    slot_out = swap_order(table[:, 0], side, pair, 2)
    far = jnp.where(side == 1, jnp.roll(table[:, :, 2:], half, axis=3), table[:, :, 2:])
    table = jnp.concatenate([table[:, :, :2], far], axis=2)
    slot, weight = table[:, 0], table[:, 1]
    rows, act, slope = forward(rows_in, slot, w_gate, w_up)
    gate_grad, up_grad = hidden_grads(grads_in, slot, weight, act, slope, w_down)

    groups = ((0, 2), (1, 3))
    kept_a, sent_a = input_sums(slot_out, gate_grad, up_grad, w_gate, w_up, groups, 0, 2)
    kept_b, sent_b = input_sums(slot_out, gate_grad, up_grad, w_gate, w_up, groups, 1, 2)

    def piece(after, before, expert, part):
        held, rows_now = lax.optimization_barrier((after, rows))
        return held, weight_grads(rows_now, gate_grad, up_grad, before, expert, part, 2)

    chip_a = add(kept_a, flip(sent_a, "expert", 1))
    sent_b, grads = piece(sent_b, None, 0, 0)
    far_a = flip(chip_a[tokens:], "expert", 2)
    got_b = flip(sent_b, "expert", 1)
    got_b, far_a, *grads = lax.optimization_barrier((got_b, far_a, *grads))
    own_a = add(chip_a[:tokens], far_a)
    mine_a, other_a = own_a[:half], own_a[half:]
    chip_b = [add(kept_b[i : i + half], got_b[i : i + half]) for i in range(0, 2 * tokens, half)]
    (mine_b, other_b, far_mine_b, far_other_b) = chip_b
    other_b = jnp.concatenate([other_b, far_other_b], axis=0)
    other_b, grads = piece(other_b, grads, 0, 1)
    got_a, got_b = flip(other_a, "dp", 1), flip(other_b, "dp", 1)
    got_a, got_b, *grads = lax.optimization_barrier((got_a, got_b, *grads))
    mine_a = add(mine_a, got_a)
    far_mine_b = add(far_mine_b, got_b[half:])
    far_mine_b, grads = piece(far_mine_b, grads, 1, 0)
    got_y = flip(far_mine_b, "expert", 2)
    got_z = flip(mine_a[quarter:], "dp", 2)
    got_y, got_z, *grads = lax.optimization_barrier((got_y, got_z, *grads))
    mine_b = add(mine_b, got_b[:half], got_y)
    mine_a = add(mine_a[:quarter], got_z)
    mine_a, grads = piece(mine_a, grads, 1, 1)
    got_b = flip(mine_b[quarter:], "dp", 2)
    got_a = flip(mine_a, "dp", 4)
    got_a, got_b, *grads = lax.optimization_barrier((got_a, got_b, *grads))
    mine_a = add(mine_a, got_a)
    mine_b = add(mine_b[:quarter], got_b)
    mine_b = add(mine_b, flip(mine_b, "dp", 4))
    halves = []
    for mine in (mine_a, mine_b):
        both = jnp.concatenate([mine, flip(mine, "dp", 2)], axis=0)
        halves.append(jnp.concatenate([both, flip(both, "dp", 1)], axis=0))
    total = swap_order(jnp.concatenate(halves, axis=1), side, pair, 0)
    return (total, *grads)


def local_any(out_grad, routes, gate_values, layer_input, w_gate, w_up, w_down):
    experts = w_gate.shape[0]
    me = lax.axis_index("expert")
    rows_in = lax.all_gather(layer_input, "expert", tiled=True)
    grads_in = lax.all_gather(out_grad, "expert", tiled=True)
    table = lax.all_gather(route_table(routes, gate_values), "expert")
    table = lax.dynamic_slice_in_dim(table, me * experts, experts, 1)
    slot, weight = table[:, :, 0].swapaxes(0, 1), table[:, :, 1].swapaxes(0, 1)
    rows, act, slope = forward([rows_in], slot, w_gate, w_up)
    groups = (tuple(range(slot.shape[1])),)
    gate_grad, up_grad = hidden_grads([grads_in], slot, weight, act, slope, w_down)
    (sums,) = input_sums(slot, gate_grad, up_grad, w_gate, w_up, groups, 0, 1)
    grads = None
    for l in range(experts):
        grads = weight_grads(rows, gate_grad, up_grad, grads, l)
    own = lax.psum_scatter(sums, "expert", scatter_dimension=0, tiled=True)
    return (lax.psum(own, "dp"), *grads)


def solution(mesh):
    near = mesh.shape["dp"] == 8 and mesh.shape["expert"] == 4
    placed = (
        P("expert", None),
        P("expert", None),
        P("expert", None),
        P("expert", None),
        P("expert", None, "dp"),
        P("expert", None, "dp"),
        P("expert", None, "dp"),
    )
    return jax.shard_map(
        local_near if near else local_any,
        mesh=mesh,
        in_specs=placed,
        out_specs=(P("expert", None), P("expert", None, "dp"), P("expert", None, "dp")),
        check_vma=False,
    )
```

```python
import functools

import jax
import jax.numpy as jnp
from jax import lax
from jax.experimental import pallas as pl
from jax.experimental.pallas import tpu as pltpu
from jax.sharding import PartitionSpec as P

EXPERTS = 8
MOST = 80
UNIT_TILE = 256
FEATURE_TILE = 512
VMEM_BYTES = 52 * 1024 * 1024
BF16 = jnp.bfloat16
F32 = jnp.float32
NN = (((1,), (0,)), ((), ()))
NT = (((1,), (1,)), ((), ()))
TN = (((0,), (0,)), ((), ()))


def dot(a, b, dims=NN):
    return lax.dot_general(a, b, dims, preferred_element_type=F32)


def params(count):
    return pltpu.CompilerParams(
        dimension_semantics=("arbitrary",) * count, vmem_limit_bytes=VMEM_BYTES
    )


def whole(shape):
    return pl.BlockSpec(
        shape, lambda *_: (0,) * len(shape), pipeline_mode=pl.Buffered(buffer_count=1)
    )


def one_hot(slot_row):
    slots = lax.broadcasted_iota(jnp.int32, (MOST, slot_row.shape[1]), 0)
    return slots == slot_row.astype(jnp.int32)


def gather_block(held, pieces, block):
    tokens = held.shape[0]
    first, at = block * tokens, 0
    for piece in pieces:
        low, high = max(first, at), min(first + tokens, at + piece.shape[0])
        if low < high:
            held[low - first : high - first] = piece[low - at : high - at]
        at += piece.shape[0]


def column_chunks(features):
    step = 768 if features % 768 == 0 else features
    return [slice(c, c + step) for c in range(0, features, step)]


def slots_kernel(count, *refs):
    x_pieces, g_pieces = refs[:count], refs[count : 2 * count]
    slot, weight, w_gate, w_up, w_down = refs[2 * count : 2 * count + 5]
    rows, gate_grad, up_grad, held, grads = refs[-5:]
    blocks = slot.shape[1]

    @pl.when(pl.program_id(1) == 0)
    def _():
        for b in range(blocks):
            mask = one_hot(slot[0, b : b + 1, :])
            scale = jnp.sum(
                jnp.where(mask, weight[0, b : b + 1, :], 0.0), axis=1, keepdims=True
            )
            chosen = mask.astype(BF16)
            span = slice(b * MOST, (b + 1) * MOST)
            gather_block(held, x_pieces, b)
            for cols in column_chunks(held.shape[1]):
                rows[0, span, cols] = dot(chosen, held[:, cols]).astype(BF16)
            gather_block(held, g_pieces, b)
            for cols in column_chunks(held.shape[1]):
                grads[span, cols] = (dot(chosen, held[:, cols]) * scale).astype(BF16)

    gate = dot(rows[0], w_gate[0])
    up = dot(rows[0], w_up[0])
    hidden = dot(grads[...], w_down[0])
    sig = jax.nn.sigmoid(gate)
    up_grad[0] = (hidden * (gate * sig)).astype(BF16)
    gate_grad[0] = (hidden * up * sig * (1.0 + gate * (1.0 - sig))).astype(BF16)


def slot_grads(x_pieces, g_pieces, slot, weight, w_gate, w_up, w_down, before, first, last, part, parts):
    experts, blocks, tokens = slot.shape
    _, features, units = w_gate.shape
    tile = min(UNIT_TILE, units)
    slots = blocks * MOST
    count = last - first
    table = pl.BlockSpec((1, blocks, tokens), lambda l, f: (first + l, 0, 0))
    matrix = pl.BlockSpec((1, features, tile), lambda l, f: (first + l, 0, f))
    unit = pl.BlockSpec((1, slots, tile), lambda l, f: (first + l, part, f))
    pieces = [*x_pieces, *g_pieces]
    kept = [] if before is None else list(before)
    return pl.pallas_call(
        functools.partial(slots_kernel, len(x_pieces)),
        grid=(count, units // tile),
        in_specs=[whole(p.shape) for p in pieces]
        + [table, table, matrix, matrix, matrix]
        + [pl.BlockSpec(memory_space=pl.ANY)] * len(kept),
        out_specs=[
            pl.BlockSpec((1, slots, features), lambda l, f: (first + l, part, 0)), unit, unit
        ],
        out_shape=[
            jax.ShapeDtypeStruct((experts, parts * slots, features), BF16),
            jax.ShapeDtypeStruct((experts, parts * slots, units), BF16),
            jax.ShapeDtypeStruct((experts, parts * slots, units), BF16),
        ],
        scratch_shapes=[pltpu.VMEM((tokens, features), BF16), pltpu.VMEM((slots, features), BF16)],
        input_output_aliases={len(pieces) + 5 + i: i for i in range(len(kept))},
        compiler_params=params(2),
        cost_estimate=pl.CostEstimate(
            flops=6 * count * slots * features * units,
            bytes_accessed=6 * count * features * units,
            transcendentals=count * slots * units,
        ),
    )(*pieces, slot, weight, w_gate, w_up, w_down, *kept)


def inputs_kernel(groups, back, gate_grad, up_grad, w_gate, w_up, *refs):
    sums, held = refs[:-1], refs[-1]
    blocks, tokens, _ = back.shape
    for l in range(gate_grad.shape[0]):
        partial = dot(gate_grad[l], w_gate[l], NT) + dot(up_grad[l], w_up[l], NT)
        for b in range(blocks):
            held[b, l * MOST : (l + 1) * MOST] = partial[b * MOST : (b + 1) * MOST].astype(BF16)
    for out, members in zip(sums, groups):
        for place, b in enumerate(members):
            out[place * tokens : (place + 1) * tokens] = dot(back[b], held[b]).astype(BF16)


def input_sums(back, gate_grad, up_grad, w_gate, w_up, groups, part, parts):
    blocks, tokens, _ = back.shape
    experts, features, units = w_gate.shape
    wide = FEATURE_TILE
    steps = features // parts // wide
    slots = blocks * MOST
    across = pl.BlockSpec((experts, wide, units), lambda i: (0, part * steps + i, 0))
    return pl.pallas_call(
        functools.partial(inputs_kernel, groups),
        grid=(steps,),
        in_specs=[whole(back.shape), whole(gate_grad.shape), whole(up_grad.shape), across, across],
        out_specs=[pl.BlockSpec((len(g) * tokens, wide), lambda i: (0, i)) for g in groups],
        out_shape=[
            jax.ShapeDtypeStruct((len(g) * tokens, features // parts), BF16) for g in groups
        ],
        scratch_shapes=[pltpu.VMEM((blocks, experts * MOST, wide), BF16)],
        compiler_params=params(1),
        cost_estimate=pl.CostEstimate(
            flops=4 * experts * slots * features * units // parts,
            bytes_accessed=4 * experts * features * units // parts,
            transcendentals=0,
        ),
    )(back, gate_grad, up_grad, w_gate, w_up)


def back_matrix(slot):
    places = jnp.arange(MOST, dtype=F32)
    chosen = slot.transpose(1, 2, 0)[..., None] == places
    return chosen.reshape(slot.shape[1], slot.shape[2], -1).astype(BF16)


def weights_kernel(rows, gate_grad, up_grad, *refs):
    grad_gate, grad_up = refs[-2:]
    grad_gate[0] = dot(rows[0], gate_grad[0], TN)
    grad_up[0] = dot(rows[0], up_grad[0], TN)


def weight_grads(rows, gate_grad, up_grad, before, expert, part=0, parts=1):
    experts, slots, features = rows.shape
    units = gate_grad.shape[2]
    wide = FEATURE_TILE
    steps = features // parts // wide
    unit = pl.BlockSpec((1, slots, units), lambda d: (expert, 0, 0))
    out = pl.BlockSpec((1, wide, units), lambda d: (expert, part * steps + d, 0))
    kept = [] if before is None else list(before)
    return pl.pallas_call(
        weights_kernel,
        grid=(steps,),
        in_specs=[
            pl.BlockSpec((1, slots, wide), lambda d: (expert, 0, part * steps + d)), unit, unit
        ]
        + [pl.BlockSpec(memory_space=pl.ANY)] * len(kept),
        out_specs=[out, out],
        out_shape=[jax.ShapeDtypeStruct((experts, features, units), F32)] * 2,
        input_output_aliases={3 + i: i for i in range(len(kept))},
        compiler_params=params(1),
        cost_estimate=pl.CostEstimate(
            flops=4 * slots * features * units // parts,
            bytes_accessed=8 * features * units // parts,
            transcendentals=0,
        ),
    )(rows, gate_grad, up_grad, *kept)


def route_table(routes, gate_values):
    tokens = routes.shape[0]
    experts = jnp.arange(EXPERTS, dtype=jnp.int32)[:, None, None]
    match = routes.T[None] == experts
    member = jnp.any(match, axis=1)
    gate = jnp.sum(jnp.where(match, gate_values.T[None], 0.0), axis=1)
    place = jnp.arange(tokens, dtype=jnp.int32)
    earlier = (place[:, None] < place[None, :]).astype(BF16)
    slot = jnp.where(member, dot(member.astype(BF16), earlier), -1.0)
    return jnp.stack([slot, gate], axis=1)


def flip(value, axis, bit):
    count = lax.axis_size(axis)
    return lax.ppermute(value, axis, [(i, i ^ bit) for i in range(count)])


def swap_order(value, side, pair, dim):
    shape = value.shape
    value = value.reshape(shape[:dim] + (2, 2, shape[dim] // 4) + shape[dim + 1 :])
    value = jnp.where(side == 1, jnp.flip(value, dim), value)
    return jnp.where(pair == 1, jnp.flip(value, dim + 1), value).reshape(shape)


def add(*terms):
    total = terms[0].astype(F32)
    for term in terms[1:]:
        total = total + term.astype(F32)
    return total.astype(BF16)


def quarters(value, count, at):
    return lax.dynamic_slice_in_dim(value, at * (count // 4), count // 4, 0)


def local_near(out_grad, routes, gate_values, layer_input, w_gate, w_up, w_down):
    experts, features, _ = w_gate.shape
    me = lax.axis_index("expert")
    position = lax.axis_index("dp")
    side, pair = position % 2, position // 2 % 2
    tokens = out_grad.shape[0]
    half, quarter = tokens // 2, tokens // 4
    corner = side * 2 + pair

    def fetched(block):
        return jnp.concatenate(
            [quarters(block, tokens, corner), quarters(block, tokens, 3 - corner)], axis=0
        )

    x_mine, g_mine = fetched(layer_input), fetched(out_grad)
    x_mine, g_mine, layer_input, out_grad, routes = lax.optimization_barrier(
        (x_mine, g_mine, layer_input, out_grad, routes)
    )
    table = route_table(routes, gate_values)
    x_sibling, g_sibling = flip(layer_input, "expert", 1), flip(out_grad, "expert", 1)
    x_across, g_across = flip(x_mine, "expert", 2), flip(g_mine, "expert", 2)

    def for_expert(value, owner):
        return lax.dynamic_slice_in_dim(value, owner * experts, experts, 0)

    beside = flip(for_expert(table, me ^ 1), "expert", 1)
    near = jnp.stack([for_expert(table, me), beside], axis=2)
    every = lax.all_gather(table, "expert")
    weights = (w_gate, w_up, w_down)
    x_near, g_near = (layer_input, x_sibling), (out_grad, g_sibling)
    made = slot_grads(x_near, g_near, near[:, 0], near[:, 1], *weights, None, 0, 1, 0, 2)
    x_across, every, near, *made = lax.optimization_barrier((x_across, every, near, *made))
    x_side, x_pair = flip(x_across[:quarter], "dp", 1), flip(x_across[:quarter], "dp", 2)
    made = slot_grads(x_near, g_near, near[:, 0], near[:, 1], *weights, made, 1, experts, 0, 2)
    g_across, *made = lax.optimization_barrier((g_across, *made))
    g_side, g_pair = flip(g_across[:quarter], "dp", 1), flip(g_across[:quarter], "dp", 2)
    far = jnp.stack(
        [
            for_expert(lax.dynamic_index_in_dim(every, me ^ r, 0, keepdims=False), me)
            for r in (2, 3)
        ],
        axis=2,
    )
    slot_back = swap_order(jnp.concatenate([near[:, 0], far[:, 0]], axis=1), side, pair, 2)
    back = back_matrix(slot_back)
    far = swap_order(far, side, pair, 3).reshape(experts, 2, 2, 4, quarter)
    far = jnp.stack([far[:, :, :, q] for q in (0, 3, 2, 1)], axis=3)
    far = far.reshape(experts, 2, 2, tokens)

    x_far = (x_across, x_side, x_pair)
    g_far = (g_across, g_side, g_pair)
    x_far = (*x_far, *(flip(v, "expert", 1) for v in x_far))
    g_far = (*g_far, *(flip(v, "expert", 1) for v in g_far))
    rows, gate_grad, up_grad = slot_grads(
        x_far, g_far, far[:, 0], far[:, 1], *weights, made, 0, experts, 1, 2
    )

    groups = ((0, 2), (1, 3))
    kept_a, sent_a = input_sums(back, gate_grad, up_grad, w_gate, w_up, groups, 0, 2)
    kept_b, sent_b = input_sums(back, gate_grad, up_grad, w_gate, w_up, groups, 1, 2)

    def piece(after, before, expert, part):
        held, rows_now = lax.optimization_barrier((after, rows))
        return held, weight_grads(rows_now, gate_grad, up_grad, before, expert, part, 2)

    chip_a = add(kept_a, flip(sent_a, "expert", 1))
    got = flip(sent_b, "expert", 1)
    chip_b = [add(kept_b[i : i + half], got[i : i + half]) for i in range(0, 2 * tokens, half)]
    (mine_b, other_b, far_mine_b, far_other_b) = chip_b
    other_b = jnp.concatenate([other_b, far_other_b], axis=0)
    far_a = chip_a[tokens:]
    (far_a, other_b), grads = piece((far_a, other_b), None, 0, 0)
    got_a, got_b = flip(far_a, "expert", 2), flip(other_b, "dp", 1)
    got_a, got_b, *grads = lax.optimization_barrier((got_a, got_b, *grads))
    own_a = [add(chip_a[i : i + half], got_a[i : i + half]) for i in (0, half)]
    mine_a, other_a = own_a
    far_mine_b = add(far_mine_b, got_b[half:])
    (other_a, far_mine_b), grads = piece((other_a, far_mine_b), grads, 0, 1)
    got_a, got_y = flip(other_a, "dp", 1), flip(far_mine_b, "expert", 2)
    got_a, got_y, *grads = lax.optimization_barrier((got_a, got_y, *grads))
    mine = jnp.concatenate([add(mine_a, got_a), add(mine_b, got_b[:half], got_y)], axis=1)
    mine = add(mine[:quarter], flip(mine[quarter:], "dp", 2))
    mine, grads = piece(mine, grads, 1, 0)
    got = flip(mine, "dp", 4)
    got, *grads = lax.optimization_barrier((got, *grads))
    mine = add(mine, got)
    mine = jnp.concatenate([mine, flip(mine, "dp", 2)], axis=0)
    mine, grads = piece(mine, grads, 1, 1)
    got = flip(mine, "dp", 1)
    got, *grads = lax.optimization_barrier((got, *grads))
    total = swap_order(jnp.concatenate([mine, got], axis=0), side, pair, 0)
    return (total, *grads)


def local_any(out_grad, routes, gate_values, layer_input, w_gate, w_up, w_down):
    experts = w_gate.shape[0]
    me = lax.axis_index("expert")
    rows_in = lax.all_gather(layer_input, "expert", tiled=True)
    grads_in = lax.all_gather(out_grad, "expert", tiled=True)
    table = lax.all_gather(route_table(routes, gate_values), "expert")
    table = lax.dynamic_slice_in_dim(table, me * experts, experts, 1)
    slot, weight = table[:, :, 0].swapaxes(0, 1), table[:, :, 1].swapaxes(0, 1)
    rows, gate_grad, up_grad = slot_grads(
        [rows_in], [grads_in], slot, weight, w_gate, w_up, w_down, None, 0, experts, 0, 1
    )
    groups = (tuple(range(slot.shape[1])),)
    (sums,) = input_sums(back_matrix(slot), gate_grad, up_grad, w_gate, w_up, groups, 0, 1)
    grads = None
    for l in range(experts):
        grads = weight_grads(rows, gate_grad, up_grad, grads, l)
    own = lax.psum_scatter(sums, "expert", scatter_dimension=0, tiled=True)
    return (lax.psum(own, "dp"), *grads)


def solution(mesh):
    near = mesh.shape["dp"] == 8 and mesh.shape["expert"] == 4
    placed = (
        P("expert", None),
        P("expert", None),
        P("expert", None),
        P("expert", None),
        P("expert", None, "dp"),
        P("expert", None, "dp"),
        P("expert", None, "dp"),
    )
    return jax.shard_map(
        local_near if near else local_any,
        mesh=mesh,
        in_specs=placed,
        out_specs=(P("expert", None), P("expert", None, "dp"), P("expert", None, "dp")),
        check_vma=False,
    )
```

```python
import functools

import jax
import jax.numpy as jnp
from jax import lax
from jax.experimental import pallas as pl
from jax.experimental.pallas import tpu as pltpu
from jax.sharding import PartitionSpec as P

EXPERTS = 8
MOST = 80
UNIT_TILE = 256
FEATURE_TILE = 512
VMEM_BYTES = 52 * 1024 * 1024
BF16 = jnp.bfloat16
F32 = jnp.float32
NN = (((1,), (0,)), ((), ()))
NT = (((1,), (1,)), ((), ()))
TN = (((0,), (0,)), ((), ()))


def dot(a, b, dims=NN):
    return lax.dot_general(a, b, dims, preferred_element_type=F32)


def params(count):
    return pltpu.CompilerParams(
        dimension_semantics=("arbitrary",) * count, vmem_limit_bytes=VMEM_BYTES
    )


def whole(shape):
    return pl.BlockSpec(
        shape, lambda *_: (0,) * len(shape), pipeline_mode=pl.Buffered(buffer_count=1)
    )


def one_hot(slot_row):
    slots = lax.broadcasted_iota(jnp.int32, (MOST, slot_row.shape[1]), 0)
    return slots == slot_row.astype(jnp.int32)


def lay_out(held, pieces, first):
    rows, at = held.shape[0], 0
    for piece in pieces:
        low, high = max(first, at), min(first + rows, at + piece.shape[0])
        if low < high:
            held[low - first : high - first] = piece[low - at : high - at]
        at += piece.shape[0]


def column_chunks(features):
    step = 768 if features % 768 == 0 else features
    return [slice(c, c + step) for c in range(0, features, step)]


def slots_kernel(count, *refs):
    x_pieces, g_pieces = refs[:count], refs[count : 2 * count]
    slot, weight, w_gate, w_up, w_down = refs[2 * count : 2 * count + 5]
    rows, gate_grad, up_grad, held, chosen, grads = refs[-6:]
    experts, blocks, tokens = slot.shape
    group = held.shape[0] // tokens
    expert = pl.program_id(0)

    @pl.when((expert == 0) & (pl.program_id(1) == 0))
    def _():
        for start in range(0, blocks, group):
            chosen[...] = jnp.zeros_like(chosen)
            scales = []
            places = [(l, b) for l in range(experts) for b in range(group)]
            for i, (l, b) in enumerate(places):
                at = slice(start + b, start + b + 1)
                mask = one_hot(slot[l, at, :])
                chosen[i * MOST : (i + 1) * MOST, b * tokens : (b + 1) * tokens] = mask.astype(BF16)
                scales.append(
                    jnp.sum(jnp.where(mask, weight[l, at, :], 0.0), axis=1, keepdims=True)
                )
            for pieces, out in ((x_pieces, rows), (g_pieces, grads)):
                lay_out(held, pieces, start * tokens)
                for cols in column_chunks(held.shape[1]):
                    taken = dot(chosen[...], held[:, cols])
                    for i, (l, b) in enumerate(places):
                        part = taken[i * MOST : (i + 1) * MOST]
                        if out is grads:
                            part = part * scales[i]
                        span = slice((start + b) * MOST, (start + b + 1) * MOST)
                        out[l, span, cols] = part.astype(BF16)

    x = rows[expert]
    gate = dot(x, w_gate[0])
    up = dot(x, w_up[0])
    hidden = dot(grads[expert], w_down[0])
    sig = jax.nn.sigmoid(gate)
    up_grad[0] = (hidden * (gate * sig)).astype(BF16)
    gate_grad[0] = (hidden * up * sig * (1.0 + gate * (1.0 - sig))).astype(BF16)


def slot_grads(x_pieces, g_pieces, table, weights, before, first, last, part, parts, share=(0, 1)):
    slot, weight = table[:, 0], table[:, 1]
    experts, blocks, tokens = slot.shape
    _, features, units = weights[0].shape
    tile = min(UNIT_TILE, units)
    tiles = units // tile // share[1]
    skip = share[0] * tiles
    slots = blocks * MOST
    count = last - first
    group = 2 if blocks % 2 == 0 else 1
    routes = pl.BlockSpec((count, blocks, tokens), lambda l, f: (first // count, 0, 0))
    matrix = pl.BlockSpec((1, features, tile), lambda l, f: (first + l, 0, skip + f))
    unit = pl.BlockSpec((1, slots, tile), lambda l, f: (first + l, part, skip + f))
    pieces = [*x_pieces, *g_pieces]
    kept = [] if before is None else list(before)
    return pl.pallas_call(
        functools.partial(slots_kernel, len(x_pieces)),
        grid=(count, tiles),
        in_specs=[whole(p.shape) for p in pieces]
        + [routes, routes, matrix, matrix, matrix]
        + [pl.BlockSpec(memory_space=pl.ANY)] * len(kept),
        out_specs=[
            pl.BlockSpec((count, slots, features), lambda l, f: (first // count, part, 0)),
            unit,
            unit,
        ],
        out_shape=[
            jax.ShapeDtypeStruct((experts, parts * slots, features), BF16),
            jax.ShapeDtypeStruct((experts, parts * slots, units), BF16),
            jax.ShapeDtypeStruct((experts, parts * slots, units), BF16),
        ],
        scratch_shapes=[
            pltpu.VMEM((group * tokens, features), BF16),
            pltpu.VMEM((count * group * MOST, group * tokens), BF16),
            pltpu.VMEM((count, slots, features), BF16),
        ],
        input_output_aliases={len(pieces) + 5 + i: i for i in range(len(kept))},
        compiler_params=params(2),
        cost_estimate=pl.CostEstimate(
            flops=6 * count * slots * features * tiles * tile,
            bytes_accessed=6 * count * features * tiles * tile,
            transcendentals=count * slots * tiles * tile,
        ),
    )(*pieces, slot, weight, *weights, *kept)


def inputs_kernel(groups, back, gate_grad, up_grad, w_gate, w_up, *refs):
    sums, held = refs[:-1], refs[-1]
    blocks, tokens, _ = back.shape
    for l in range(gate_grad.shape[0]):
        partial = dot(gate_grad[l], w_gate[l], NT) + dot(up_grad[l], w_up[l], NT)
        for b in range(blocks):
            held[b, l * MOST : (l + 1) * MOST] = partial[b * MOST : (b + 1) * MOST].astype(BF16)
    for out, members in zip(sums, groups):
        for place, b in enumerate(members):
            out[place * tokens : (place + 1) * tokens] = dot(back[b], held[b]).astype(BF16)


def input_sums(back, gate_grad, up_grad, w_gate, w_up, groups, part, parts):
    blocks, tokens, _ = back.shape
    experts, features, units = w_gate.shape
    wide = FEATURE_TILE
    steps = features // parts // wide
    slots = blocks * MOST
    across = pl.BlockSpec((experts, wide, units), lambda i: (0, part * steps + i, 0))
    return pl.pallas_call(
        functools.partial(inputs_kernel, groups),
        grid=(steps,),
        in_specs=[whole(back.shape), whole(gate_grad.shape), whole(up_grad.shape), across, across],
        out_specs=[pl.BlockSpec((len(g) * tokens, wide), lambda i: (0, i)) for g in groups],
        out_shape=[
            jax.ShapeDtypeStruct((len(g) * tokens, features // parts), BF16) for g in groups
        ],
        scratch_shapes=[pltpu.VMEM((blocks, experts * MOST, wide), BF16)],
        compiler_params=params(1),
        cost_estimate=pl.CostEstimate(
            flops=4 * experts * slots * features * units // parts,
            bytes_accessed=4 * experts * features * units // parts,
            transcendentals=0,
        ),
    )(back, gate_grad, up_grad, w_gate, w_up)


def back_matrix(slot):
    places = jnp.arange(MOST, dtype=F32)
    chosen = slot.transpose(1, 2, 0)[..., None] == places
    return chosen.reshape(slot.shape[1], slot.shape[2], -1).astype(BF16)


def weights_kernel(rows, gate_grad, up_grad, *refs):
    grad_gate, grad_up = refs[-2:]
    grad_gate[0] = dot(rows[0], gate_grad[0], TN)
    grad_up[0] = dot(rows[0], up_grad[0], TN)


def weight_grads(rows, gate_grad, up_grad, before, expert, part=0, parts=1):
    experts, slots, features = rows.shape
    units = gate_grad.shape[2]
    wide = FEATURE_TILE
    steps = features // parts // wide
    unit = pl.BlockSpec((1, slots, units), lambda d: (expert, 0, 0))
    out = pl.BlockSpec((1, wide, units), lambda d: (expert, part * steps + d, 0))
    kept = [] if before is None else list(before)
    return pl.pallas_call(
        weights_kernel,
        grid=(steps,),
        in_specs=[
            pl.BlockSpec((1, slots, wide), lambda d: (expert, 0, part * steps + d)), unit, unit
        ]
        + [pl.BlockSpec(memory_space=pl.ANY)] * len(kept),
        out_specs=[out, out],
        out_shape=[jax.ShapeDtypeStruct((experts, features, units), F32)] * 2,
        input_output_aliases={3 + i: i for i in range(len(kept))},
        compiler_params=params(1),
        cost_estimate=pl.CostEstimate(
            flops=4 * slots * features * units // parts,
            bytes_accessed=8 * features * units // parts,
            transcendentals=0,
        ),
    )(rows, gate_grad, up_grad, *kept)


def route_table(routes, gate_values):
    tokens = routes.shape[0]
    experts = jnp.arange(EXPERTS, dtype=jnp.int32)[:, None, None]
    match = routes.T[None] == experts
    member = jnp.any(match, axis=1)
    gate = jnp.sum(jnp.where(match, gate_values.T[None], 0.0), axis=1)
    place = jnp.arange(tokens, dtype=jnp.int32)
    earlier = (place[:, None] < place[None, :]).astype(BF16)
    slot = jnp.where(member, dot(member.astype(BF16), earlier), -1.0)
    return jnp.stack([slot, gate], axis=1)


def flip(value, axis, bit):
    count = lax.axis_size(axis)
    return lax.ppermute(value, axis, [(i, i ^ bit) for i in range(count)])


def swap_order(value, side, pair, dim):
    shape = value.shape
    value = value.reshape(shape[:dim] + (2, 2, shape[dim] // 4) + shape[dim + 1 :])
    value = jnp.where(side == 1, jnp.flip(value, dim), value)
    return jnp.where(pair == 1, jnp.flip(value, dim + 1), value).reshape(shape)


def add(*terms):
    total = terms[0].astype(F32)
    for term in terms[1:]:
        total = total + term.astype(F32)
    return total.astype(BF16)


def quarters(value, count, at):
    return lax.dynamic_slice_in_dim(value, at * (count // 4), count // 4, 0)


def local_near(out_grad, routes, gate_values, layer_input, w_gate, w_up, w_down):
    experts, features, _ = w_gate.shape
    me = lax.axis_index("expert")
    position = lax.axis_index("dp")
    side, pair = position % 2, position // 2 % 2
    tokens = out_grad.shape[0]
    half, quarter = tokens // 2, tokens // 4
    corner = side * 2 + pair

    def fetched(block):
        return jnp.concatenate(
            [quarters(block, tokens, corner), quarters(block, tokens, 3 - corner)], axis=0
        )

    x_mine, g_mine = fetched(layer_input), fetched(out_grad)
    x_mine, g_mine, layer_input, out_grad, routes = lax.optimization_barrier(
        (x_mine, g_mine, layer_input, out_grad, routes)
    )
    table = route_table(routes, gate_values)
    tables = []
    for r in range(4):
        part = lax.dynamic_slice_in_dim(table, (me ^ r) * experts, experts, 0)
        tables.append(flip(part, "expert", r) if r > 0 else part)
    x_across, g_across = flip(x_mine, "expert", 2), flip(g_mine, "expert", 2)
    x_sibling, g_sibling = flip(layer_input, "expert", 1), flip(out_grad, "expert", 1)

    def onward(across):
        here = (across, flip(across[:quarter], "dp", 1), flip(across[:quarter], "dp", 2))
        return (*here, *(flip(v, "expert", 1) for v in here))

    weights = (w_gate, w_up, w_down)
    near = jnp.stack(tables[:2], axis=2)
    near_rows = ((layer_input, x_sibling), (out_grad, g_sibling), near, weights)
    made = slot_grads(*near_rows, None, 0, 1, 0, 2)
    x_across, tables[2], tables[3], *made = lax.optimization_barrier(
        (x_across, tables[2], tables[3], *made)
    )
    x_far = onward(x_across)
    made = slot_grads(*near_rows, made, 1, 2, 0, 2, (0, 2))
    g_across, *made = lax.optimization_barrier((g_across, *made))
    g_far = onward(g_across)
    made = slot_grads(*near_rows, made, 1, 2, 0, 2, (1, 2))
    far = jnp.stack(tables[2:], axis=2)
    slot_back = jnp.concatenate([near[:, 0], far[:, 0]], axis=1)
    back = back_matrix(swap_order(slot_back, side, pair, 2))
    far = swap_order(far, side, pair, 3).reshape(experts, 2, 2, 4, quarter)
    far = jnp.stack([far[:, :, :, q] for q in (0, 3, 2, 1)], axis=3)
    far = far.reshape(experts, 2, 2, tokens)
    rows, gate_grad, up_grad = slot_grads(x_far, g_far, far, weights, made, 0, experts, 1, 2)

    groups = ((0, 2), (1, 3))
    kept_a, sent_a = input_sums(back, gate_grad, up_grad, w_gate, w_up, groups, 0, 2)
    kept_b, sent_b = input_sums(back, gate_grad, up_grad, w_gate, w_up, groups, 1, 2)

    def piece(after, before, *which):
        held, rows_now = lax.optimization_barrier((after, rows))
        return held, weight_grads(rows_now, gate_grad, up_grad, before, *which)

    def corners(value):
        return [flip(v, "dp", step) for v, step in zip(value, (2, 1, 3))]

    def cut(value, count):
        return [value[i : i + quarter] for i in range(0, count * quarter, quarter)]

    chip_a = add(kept_a, flip(sent_a, "expert", 1))
    got = flip(sent_b, "expert", 1)
    chip_b = [add(a, b) for a, b in zip(cut(kept_b, 8), cut(got, 8))]
    far_a = chip_a[tokens:]
    away = [jnp.concatenate([chip_b[q], chip_b[4 + q]], axis=0) for q in (1, 2, 3)]
    (far_a, *away), grads = piece((far_a, *away), None, 0)
    got_a, got_b = flip(far_a, "expert", 2), corners(away)
    got_a, got_b, *grads = lax.optimization_barrier((got_a, got_b, *grads))
    own_a = [add(a, b) for a, b in zip(cut(chip_a, 4), cut(got_a, 4))]
    mine_b = add(chip_b[0], *(v[:quarter] for v in got_b))
    far_b = add(chip_b[4], *(v[quarter:] for v in got_b))
    got_a, got_b = corners(own_a[1:]), flip(far_b, "expert", 2)
    mine = jnp.concatenate([add(own_a[0], *got_a), add(mine_b, got_b)], axis=1)
    mine, grads = piece(mine, grads, 1, 0, 2)
    got = flip(mine, "dp", 4)
    got, *grads = lax.optimization_barrier((got, *grads))
    mine = add(mine, got)
    mine, grads = piece(mine, grads, 1, 1, 2)
    got = corners([mine] * 3)
    got, *grads = lax.optimization_barrier((got, *grads))
    total = swap_order(jnp.concatenate([mine, *got], axis=0), side, pair, 0)
    return (total, *grads)


def local_any(out_grad, routes, gate_values, layer_input, w_gate, w_up, w_down):
    experts = w_gate.shape[0]
    me = lax.axis_index("expert")
    rows_in = lax.all_gather(layer_input, "expert", tiled=True)
    grads_in = lax.all_gather(out_grad, "expert", tiled=True)
    table = lax.all_gather(route_table(routes, gate_values), "expert")
    table = lax.dynamic_slice_in_dim(table, me * experts, experts, 1).transpose(1, 2, 0, 3)
    rows, gate_grad, up_grad = slot_grads(
        [rows_in], [grads_in], table, (w_gate, w_up, w_down), None, 0, experts, 0, 1
    )
    slot = table[:, 0]
    groups = (tuple(range(slot.shape[1])),)
    (sums,) = input_sums(back_matrix(slot), gate_grad, up_grad, w_gate, w_up, groups, 0, 1)
    grads = None
    for l in range(experts):
        grads = weight_grads(rows, gate_grad, up_grad, grads, l)
    own = lax.psum_scatter(sums, "expert", scatter_dimension=0, tiled=True)
    return (lax.psum(own, "dp"), *grads)


def solution(mesh):
    near = mesh.shape["dp"] == 8 and mesh.shape["expert"] == 4
    placed = (
        P("expert", None),
        P("expert", None),
        P("expert", None),
        P("expert", None),
        P("expert", None, "dp"),
        P("expert", None, "dp"),
        P("expert", None, "dp"),
    )
    return jax.shard_map(
        local_near if near else local_any,
        mesh=mesh,
        in_specs=placed,
        out_specs=(P("expert", None), P("expert", None, "dp"), P("expert", None, "dp")),
        check_vma=False,
    )
```

```python
import functools

import jax
import jax.numpy as jnp
from jax import lax
from jax.experimental import pallas as pl
from jax.experimental.pallas import tpu as pltpu
from jax.sharding import PartitionSpec as P

EXPERTS = 8
MOST = 80
UNIT_TILE = 512
FEATURE_TILE = 512
VMEM_BYTES = 52 * 1024 * 1024
BF16 = jnp.bfloat16
F32 = jnp.float32
NN = (((1,), (0,)), ((), ()))
NT = (((1,), (1,)), ((), ()))
TN = (((0,), (0,)), ((), ()))


def dot(a, b, dims=NN):
    return lax.dot_general(a, b, dims, preferred_element_type=F32)


def params(count):
    return pltpu.CompilerParams(
        dimension_semantics=("arbitrary",) * count, vmem_limit_bytes=VMEM_BYTES
    )


def whole(shape):
    return pl.BlockSpec(
        shape, lambda *_: (0,) * len(shape), pipeline_mode=pl.Buffered(buffer_count=1)
    )


def one_hot(slot_row):
    slots = lax.broadcasted_iota(jnp.int32, (MOST, slot_row.shape[1]), 0)
    return slots == slot_row.astype(jnp.int32)


def lay_out(held, pieces, first):
    rows, at = held.shape[0], 0
    for piece in pieces:
        low, high = max(first, at), min(first + rows, at + piece.shape[0])
        if low < high:
            held[low - first : high - first] = piece[low - at : high - at]
        at += piece.shape[0]


def column_chunks(features):
    step = 768 if features % 768 == 0 else features
    return [slice(c, c + step) for c in range(0, features, step)]


def dispatch(pieces, slot, held, chosen, out, weight=None):
    experts, blocks, tokens = slot.shape
    group = held.shape[0] // tokens
    places = [(l, b) for l in range(experts) for b in range(group)]
    for start in range(0, blocks, group):
        chosen[...] = jnp.zeros_like(chosen)
        scales = []
        for i, (l, b) in enumerate(places):
            at = slice(start + b, start + b + 1)
            mask = one_hot(slot[l, at, :])
            chosen[i * MOST : (i + 1) * MOST, b * tokens : (b + 1) * tokens] = mask.astype(BF16)
            if weight is not None:
                scales.append(
                    jnp.sum(jnp.where(mask, weight[l, at, :], 0.0), axis=1, keepdims=True)
                )
        lay_out(held, pieces, start * tokens)
        for cols in column_chunks(held.shape[1]):
            taken = dot(chosen[...], held[:, cols])
            for i, (l, b) in enumerate(places):
                part = taken[i * MOST : (i + 1) * MOST]
                if scales:
                    part = part * scales[i]
                span = slice((start + b) * MOST, (start + b + 1) * MOST)
                out[l, span, cols] = part.astype(BF16)


def dispatch_scratch(experts, blocks, tokens, features):
    group = 2 if blocks % 2 == 0 else 1
    return [
        pltpu.VMEM((group * tokens, features), BF16),
        pltpu.VMEM((experts * group * MOST, group * tokens), BF16),
        pltpu.VMEM((experts, blocks * MOST, features), BF16),
    ]


def forward_kernel(count, *refs):
    pieces, (slot, w_gate, w_up, rows_out, act, slope) = refs[:count], refs[count : count + 6]
    held, chosen, rows, sent = refs[count + 6 :]
    expert, tile = pl.program_id(0), pl.program_id(1)
    copy = pltpu.make_async_copy(rows, rows_out, sent)

    @pl.when((expert == 0) & (tile == 0))
    def _():
        dispatch(pieces, slot, held, chosen, rows)
        copy.start()

    x = rows[expert]
    gate = dot(x, w_gate[0])
    up = dot(x, w_up[0])
    sig = jax.nn.sigmoid(gate)
    act[0] = gate * sig
    slope[0] = up * sig * (1.0 + gate * (1.0 - sig))

    @pl.when((expert == pl.num_programs(0) - 1) & (tile == pl.num_programs(1) - 1))
    def _():
        copy.wait()


def forward(pieces, slot, w_gate, w_up):
    experts, blocks, tokens = slot.shape
    _, features, units = w_gate.shape
    tile = min(UNIT_TILE, units)
    slots = blocks * MOST
    matrix = pl.BlockSpec((1, features, tile), lambda l, f: (l, 0, f))
    unit = pl.BlockSpec((1, slots, tile), lambda l, f: (l, 0, f))
    return pl.pallas_call(
        functools.partial(forward_kernel, len(pieces)),
        grid=(experts, units // tile),
        in_specs=[whole(p.shape) for p in pieces] + [whole(slot.shape), matrix, matrix],
        out_specs=[pl.BlockSpec(memory_space=pl.ANY), unit, unit],
        out_shape=[
            jax.ShapeDtypeStruct((experts, slots, features), BF16),
            jax.ShapeDtypeStruct((experts, slots, units), F32),
            jax.ShapeDtypeStruct((experts, slots, units), F32),
        ],
        scratch_shapes=dispatch_scratch(experts, blocks, tokens, features)
        + [pltpu.SemaphoreType.DMA],
        compiler_params=params(2),
        cost_estimate=pl.CostEstimate(
            flops=4 * experts * slots * features * units,
            bytes_accessed=4 * experts * features * units,
            transcendentals=experts * slots * units,
        ),
    )(*pieces, slot, w_gate, w_up)


def hidden_kernel(count, *refs):
    pieces, (slot, weight, act, slope, w_down) = refs[:count], refs[count : count + 5]
    gate_grad, up_grad, held, chosen, grads = refs[count + 5 :]
    expert = pl.program_id(0)

    @pl.when((expert == 0) & (pl.program_id(1) == 0))
    def _():
        dispatch(pieces, slot, held, chosen, grads, weight)

    hidden = dot(grads[expert], w_down[0])
    up_grad[0] = (hidden * act[0]).astype(BF16)
    gate_grad[0] = (hidden * slope[0]).astype(BF16)


def hidden_grads(pieces, slot, weight, act, slope, w_down):
    experts, blocks, tokens = slot.shape
    _, features, units = w_down.shape
    tile = min(UNIT_TILE, units)
    slots = blocks * MOST
    unit = pl.BlockSpec((1, slots, tile), lambda l, f: (l, 0, f))
    return pl.pallas_call(
        functools.partial(hidden_kernel, len(pieces)),
        grid=(experts, units // tile),
        in_specs=[whole(p.shape) for p in pieces]
        + [whole(slot.shape), whole(slot.shape), unit, unit]
        + [pl.BlockSpec((1, features, tile), lambda l, f: (l, 0, f))],
        out_specs=[unit, unit],
        out_shape=[jax.ShapeDtypeStruct((experts, slots, units), BF16)] * 2,
        scratch_shapes=dispatch_scratch(experts, blocks, tokens, features),
        compiler_params=params(2),
        cost_estimate=pl.CostEstimate(
            flops=2 * experts * slots * features * units,
            bytes_accessed=2 * experts * features * units,
            transcendentals=0,
        ),
    )(*pieces, slot, weight, act, slope, w_down)


def inputs_kernel(groups, back, gate_grad, up_grad, w_gate, w_up, *refs):
    sums, held = refs[:-1], refs[-1]
    blocks, tokens, _ = back.shape
    for l in range(gate_grad.shape[0]):
        partial = dot(gate_grad[l], w_gate[l], NT) + dot(up_grad[l], w_up[l], NT)
        for b in range(blocks):
            held[b, l * MOST : (l + 1) * MOST] = partial[b * MOST : (b + 1) * MOST].astype(BF16)
    for out, members in zip(sums, groups):
        for place, b in enumerate(members):
            out[place * tokens : (place + 1) * tokens] = dot(back[b], held[b]).astype(BF16)


def input_sums(back, gate_grad, up_grad, w_gate, w_up, groups, part, parts):
    blocks, tokens, _ = back.shape
    experts, features, units = w_gate.shape
    wide = FEATURE_TILE
    steps = features // parts // wide
    slots = blocks * MOST
    across = pl.BlockSpec((experts, wide, units), lambda i: (0, part * steps + i, 0))
    return pl.pallas_call(
        functools.partial(inputs_kernel, groups),
        grid=(steps,),
        in_specs=[whole(back.shape), whole(gate_grad.shape), whole(up_grad.shape), across, across],
        out_specs=[pl.BlockSpec((len(g) * tokens, wide), lambda i: (0, i)) for g in groups],
        out_shape=[
            jax.ShapeDtypeStruct((len(g) * tokens, features // parts), BF16) for g in groups
        ],
        scratch_shapes=[pltpu.VMEM((blocks, experts * MOST, wide), BF16)],
        compiler_params=params(1),
        cost_estimate=pl.CostEstimate(
            flops=4 * experts * slots * features * units // parts,
            bytes_accessed=4 * experts * features * units // parts,
            transcendentals=0,
        ),
    )(back, gate_grad, up_grad, w_gate, w_up)


def back_matrix(slot):
    places = jnp.arange(MOST, dtype=F32)
    chosen = slot.transpose(1, 2, 0)[..., None] == places
    return chosen.reshape(slot.shape[1], slot.shape[2], -1).astype(BF16)


def weights_kernel(rows, gate_grad, up_grad, *refs):
    grad_gate, grad_up = refs[-2:]
    grad_gate[0] = dot(rows[0], gate_grad[0], TN)
    grad_up[0] = dot(rows[0], up_grad[0], TN)


def weight_grads(rows, gate_grad, up_grad, before, expert, first=0, steps=None):
    experts, slots, features = rows.shape
    units = gate_grad.shape[2]
    wide = FEATURE_TILE
    steps = features // wide if steps is None else steps
    unit = pl.BlockSpec((1, slots, units), lambda d: (expert, 0, 0))
    out = pl.BlockSpec((1, wide, units), lambda d: (expert, first + d, 0))
    kept = [] if before is None else list(before)
    return pl.pallas_call(
        weights_kernel,
        grid=(steps,),
        in_specs=[
            pl.BlockSpec((1, slots, wide), lambda d: (expert, 0, first + d)), unit, unit
        ]
        + [pl.BlockSpec(memory_space=pl.ANY)] * len(kept),
        out_specs=[out, out],
        out_shape=[jax.ShapeDtypeStruct((experts, features, units), F32)] * 2,
        input_output_aliases={3 + i: i for i in range(len(kept))},
        compiler_params=params(1),
        cost_estimate=pl.CostEstimate(
            flops=4 * slots * steps * wide * units,
            bytes_accessed=8 * steps * wide * units,
            transcendentals=0,
        ),
    )(rows, gate_grad, up_grad, *kept)


def route_table(routes, gate_values):
    tokens = routes.shape[0]
    experts = jnp.arange(EXPERTS, dtype=jnp.int32)[:, None, None]
    match = routes.T[None] == experts
    member = jnp.any(match, axis=1)
    gate = jnp.sum(jnp.where(match, gate_values.T[None], 0.0), axis=1)
    place = jnp.arange(tokens, dtype=jnp.int32)
    earlier = (place[:, None] < place[None, :]).astype(BF16)
    slot = jnp.where(member, dot(member.astype(BF16), earlier), -1.0)
    return jnp.stack([slot, gate], axis=1)


def flip(value, axis, bit):
    count = lax.axis_size(axis)
    return lax.ppermute(value, axis, [(i, i ^ bit) for i in range(count)])


def swap_order(value, side, pair, dim):
    shape = value.shape
    value = value.reshape(shape[:dim] + (2, 2, shape[dim] // 4) + shape[dim + 1 :])
    value = jnp.where(side == 1, jnp.flip(value, dim), value)
    return jnp.where(pair == 1, jnp.flip(value, dim + 1), value).reshape(shape)


def add(*terms):
    total = terms[0].astype(F32)
    for term in terms[1:]:
        total = total + term.astype(F32)
    return total.astype(BF16)


def quarters(value, count, at):
    return lax.dynamic_slice_in_dim(value, at * (count // 4), count // 4, 0)


def local_near(out_grad, routes, gate_values, layer_input, w_gate, w_up, w_down):
    experts, features, _ = w_gate.shape
    me = lax.axis_index("expert")
    position = lax.axis_index("dp")
    side, pair = position % 2, position // 2 % 2
    tokens = out_grad.shape[0]
    half, quarter = tokens // 2, tokens // 4
    corner = side * 2 + pair

    def fetched(block):
        return jnp.concatenate(
            [quarters(block, tokens, corner), quarters(block, tokens, 3 - corner)], axis=0
        )

    def onward(across):
        return (flip(across[:quarter], "dp", 1), flip(across[:quarter], "dp", 2))

    def to_core(values):
        return tuple(flip(v, "expert", 1) for v in values)

    x_mine = fetched(layer_input)
    x_mine, layer_input, out_grad, routes = lax.optimization_barrier(
        (x_mine, layer_input, out_grad, routes)
    )
    x_across = flip(x_mine, "expert", 2)
    x_sibling, g_sibling = flip(layer_input, "expert", 1), flip(out_grad, "expert", 1)
    table = route_table(routes, gate_values)
    tables = []
    for r in range(4):
        part = lax.dynamic_slice_in_dim(table, (me ^ r) * experts, experts, 0)
        tables.append(flip(part, "expert", r) if r > 0 else part)
    tables[1], g_mine = lax.optimization_barrier((tables[1], fetched(out_grad)))
    g_across = flip(g_mine, "expert", 2)
    x_far = (x_across, *onward(x_across))
    x_far = (*x_far, *to_core(x_far))
    *x_far, g_across = lax.optimization_barrier((*x_far, g_across))
    g_beside = onward(g_across)
    g_passed = to_core((g_across,))
    table = jnp.stack(tables, axis=2)
    back = back_matrix(swap_order(table[:, 0], side, pair, 2))
    far = swap_order(table[:, :, 2:], side, pair, 3).reshape(experts, 2, 2, 4, quarter)
    far = jnp.stack([far[:, :, :, q] for q in (0, 3, 2, 1)], axis=3)
    table = jnp.concatenate([table[:, :, :2], far.reshape(experts, 2, 2, tokens)], axis=2)
    slot, weight = table[:, 0], table[:, 1]
    rows, act, slope = forward((layer_input, x_sibling, *x_far), slot, w_gate, w_up)
    act, *g_beside = lax.optimization_barrier((act, *g_beside))
    g_far = (g_across, *g_beside, *g_passed, *to_core(g_beside))
    gate_grad, up_grad = hidden_grads(
        (out_grad, g_sibling, *g_far), slot, weight, act, slope, w_down
    )

    groups = ((0, 2), (1, 3))
    kept_a, sent_a = input_sums(back, gate_grad, up_grad, w_gate, w_up, groups, 0, 2)
    kept_b, sent_b = input_sums(back, gate_grad, up_grad, w_gate, w_up, groups, 1, 2)

    def piece(after, before, *which):
        held, rows_now = lax.optimization_barrier((after, rows))
        return held, weight_grads(rows_now, gate_grad, up_grad, before, *which)

    def corners(value):
        return [flip(v, "dp", step) for v, step in zip(value, (2, 1, 3))]

    def cut(value, count):
        return [value[i : i + quarter] for i in range(0, count * quarter, quarter)]

    chip_a = add(kept_a, flip(sent_a, "expert", 1))
    got = flip(sent_b, "expert", 1)
    chip_b = [add(a, b) for a, b in zip(cut(kept_b, 8), cut(got, 8))]
    far_a = chip_a[tokens:]
    away = [jnp.concatenate([chip_b[q], chip_b[4 + q]], axis=0) for q in (1, 2, 3)]
    (far_a, *away), grads = piece((far_a, *away), None, 0, 0, 4)
    got_a, got_b = flip(far_a, "expert", 2), corners(away)
    got_a, got_b, *grads = lax.optimization_barrier((got_a, got_b, *grads))
    own_a = [add(a, b) for a, b in zip(cut(chip_a, 4), cut(got_a, 4))]
    mine_b = add(chip_b[0], *(v[:quarter] for v in got_b))
    far_b = add(chip_b[4], *(v[quarter:] for v in got_b))
    (far_b, *own_a), grads = piece((far_b, *own_a), grads, 0, 4, 2)
    got_a, got_b = corners(own_a[1:]), flip(far_b, "expert", 2)
    got_a, got_b, *grads = lax.optimization_barrier((got_a, got_b, *grads))
    mine = jnp.concatenate([add(own_a[0], *got_a), add(mine_b, got_b)], axis=1)
    mine, grads = piece(mine, grads, 1, 0, 3)
    got = flip(mine, "dp", 4)
    got, *grads = lax.optimization_barrier((got, *grads))
    mine = add(mine, got)
    mine, grads = piece(mine, grads, 1, 3, 3)
    got = corners([mine] * 3)
    got, *grads = lax.optimization_barrier((got, *grads))
    total = swap_order(jnp.concatenate([mine, *got], axis=0), side, pair, 0)
    return (total, *grads)


def local_any(out_grad, routes, gate_values, layer_input, w_gate, w_up, w_down):
    experts = w_gate.shape[0]
    me = lax.axis_index("expert")
    rows_in = lax.all_gather(layer_input, "expert", tiled=True)
    grads_in = lax.all_gather(out_grad, "expert", tiled=True)
    table = lax.all_gather(route_table(routes, gate_values), "expert")
    table = lax.dynamic_slice_in_dim(table, me * experts, experts, 1).transpose(1, 2, 0, 3)
    slot, weight = table[:, 0], table[:, 1]
    rows, act, slope = forward([rows_in], slot, w_gate, w_up)
    gate_grad, up_grad = hidden_grads([grads_in], slot, weight, act, slope, w_down)
    groups = (tuple(range(slot.shape[1])),)
    (sums,) = input_sums(back_matrix(slot), gate_grad, up_grad, w_gate, w_up, groups, 0, 1)
    grads = None
    for l in range(experts):
        grads = weight_grads(rows, gate_grad, up_grad, grads, l)
    own = lax.psum_scatter(sums, "expert", scatter_dimension=0, tiled=True)
    return (lax.psum(own, "dp"), *grads)


def solution(mesh):
    near = mesh.shape["dp"] == 8 and mesh.shape["expert"] == 4
    placed = (
        P("expert", None),
        P("expert", None),
        P("expert", None),
        P("expert", None),
        P("expert", None, "dp"),
        P("expert", None, "dp"),
        P("expert", None, "dp"),
    )
    return jax.shard_map(
        local_near if near else local_any,
        mesh=mesh,
        in_specs=placed,
        out_specs=(P("expert", None), P("expert", None, "dp"), P("expert", None, "dp")),
        check_vma=False,
    )
```

```python
import functools

import jax
import jax.numpy as jnp
from jax import lax
from jax.experimental import pallas as pl
from jax.experimental.pallas import tpu as pltpu
from jax.sharding import PartitionSpec as P

EXPERTS = 8
MOST = 80
UNIT_TILE = 512
FEATURE_TILE = 512
VMEM_BYTES = 40 * 1024 * 1024
BF16 = jnp.bfloat16
F32 = jnp.float32
NN = (((1,), (0,)), ((), ()))
NT = (((1,), (1,)), ((), ()))
TN = (((0,), (0,)), ((), ()))


def dot(a, b, dims=NN):
    return lax.dot_general(a, b, dims, preferred_element_type=F32)


def params(count):
    return pltpu.CompilerParams(
        dimension_semantics=("arbitrary",) * count, vmem_limit_bytes=VMEM_BYTES
    )


def whole(shape):
    return pl.BlockSpec(
        shape, lambda *_: (0,) * len(shape), pipeline_mode=pl.Buffered(buffer_count=1)
    )


def one_hot(slot_row):
    slots = lax.broadcasted_iota(jnp.int32, (MOST, slot_row.shape[1]), 0)
    return slots == slot_row.astype(jnp.int32)


def lay_out(held, pieces, first):
    rows, at = held.shape[0], 0
    for piece in pieces:
        low, high = max(first, at), min(first + rows, at + piece.shape[0])
        if low < high:
            held[low - first : high - first] = piece[low - at : high - at]
        at += piece.shape[0]


def column_chunks(features):
    step = 768 if features % 768 == 0 else features
    return [slice(c, c + step) for c in range(0, features, step)]


def dispatch(pieces, slot, held, chosen, out, weight=None):
    experts, blocks, tokens = slot.shape
    group = held.shape[0] // tokens
    places = [(l, b) for l in range(experts) for b in range(group)]
    for start in range(0, blocks, group):
        chosen[...] = jnp.zeros_like(chosen)
        scales = []
        for i, (l, b) in enumerate(places):
            at = slice(start + b, start + b + 1)
            mask = one_hot(slot[l, at, :])
            chosen[i * MOST : (i + 1) * MOST, b * tokens : (b + 1) * tokens] = mask.astype(BF16)
            if weight is not None:
                scales.append(
                    jnp.sum(jnp.where(mask, weight[l, at, :], 0.0), axis=1, keepdims=True)
                )
        lay_out(held, pieces, start * tokens)
        for cols in column_chunks(held.shape[1]):
            taken = dot(chosen[...], held[:, cols])
            for i, (l, b) in enumerate(places):
                part = taken[i * MOST : (i + 1) * MOST]
                if scales:
                    part = part * scales[i]
                span = slice((start + b) * MOST, (start + b + 1) * MOST)
                out[l, span, cols] = part.astype(BF16)


def dispatch_scratch(experts, blocks, tokens, features):
    group = 2 if blocks % 2 == 0 else 1
    return [
        pltpu.VMEM((group * tokens, features), BF16),
        pltpu.VMEM((experts * group * MOST, group * tokens), BF16),
        pltpu.VMEM((experts, blocks * MOST, features), BF16),
    ]


def forward_kernel(count, *refs):
    pieces, (slot, w_gate, w_up, rows_out, act, slope) = refs[:count], refs[count : count + 6]
    held, chosen, rows, sent = refs[count + 6 :]
    expert, tile = pl.program_id(0), pl.program_id(1)
    copy = pltpu.make_async_copy(rows, rows_out, sent)

    @pl.when((expert == 0) & (tile == 0))
    def _():
        dispatch(pieces, slot, held, chosen, rows)
        copy.start()

    x = rows[expert]
    gate = dot(x, w_gate[0])
    up = dot(x, w_up[0])
    sig = jax.nn.sigmoid(gate)
    act[0] = gate * sig
    slope[0] = up * sig * (1.0 + gate * (1.0 - sig))

    @pl.when((expert == pl.num_programs(0) - 1) & (tile == pl.num_programs(1) - 1))
    def _():
        copy.wait()


def forward(pieces, slot, w_gate, w_up):
    experts, blocks, tokens = slot.shape
    _, features, units = w_gate.shape
    tile = min(UNIT_TILE, units)
    slots = blocks * MOST
    matrix = pl.BlockSpec((1, features, tile), lambda l, f: (l, 0, f))
    unit = pl.BlockSpec((1, slots, tile), lambda l, f: (l, 0, f))
    return pl.pallas_call(
        functools.partial(forward_kernel, len(pieces)),
        grid=(experts, units // tile),
        in_specs=[whole(p.shape) for p in pieces] + [whole(slot.shape), matrix, matrix],
        out_specs=[pl.BlockSpec(memory_space=pl.ANY), unit, unit],
        out_shape=[
            jax.ShapeDtypeStruct((experts, slots, features), BF16),
            jax.ShapeDtypeStruct((experts, slots, units), F32),
            jax.ShapeDtypeStruct((experts, slots, units), F32),
        ],
        scratch_shapes=dispatch_scratch(experts, blocks, tokens, features)
        + [pltpu.SemaphoreType.DMA],
        compiler_params=params(2),
        cost_estimate=pl.CostEstimate(
            flops=4 * experts * slots * features * units,
            bytes_accessed=4 * experts * features * units,
            transcendentals=experts * slots * units,
        ),
    )(*pieces, slot, w_gate, w_up)


def hidden_kernel(count, *refs):
    pieces, (slot, weight, act, slope, w_down) = refs[:count], refs[count : count + 5]
    gate_grad, up_grad, held, chosen, grads = refs[count + 5 :]
    expert = pl.program_id(0)

    @pl.when((expert == 0) & (pl.program_id(1) == 0))
    def _():
        dispatch(pieces, slot, held, chosen, grads, weight)

    hidden = dot(grads[expert], w_down[0])
    up_grad[0] = (hidden * act[0]).astype(BF16)
    gate_grad[0] = (hidden * slope[0]).astype(BF16)


def hidden_grads(pieces, slot, weight, act, slope, w_down):
    experts, blocks, tokens = slot.shape
    _, features, units = w_down.shape
    tile = min(UNIT_TILE, units)
    slots = blocks * MOST
    unit = pl.BlockSpec((1, slots, tile), lambda l, f: (l, 0, f))
    return pl.pallas_call(
        functools.partial(hidden_kernel, len(pieces)),
        grid=(experts, units // tile),
        in_specs=[whole(p.shape) for p in pieces]
        + [whole(slot.shape), whole(slot.shape), unit, unit]
        + [pl.BlockSpec((1, features, tile), lambda l, f: (l, 0, f))],
        out_specs=[unit, unit],
        out_shape=[jax.ShapeDtypeStruct((experts, slots, units), BF16)] * 2,
        scratch_shapes=dispatch_scratch(experts, blocks, tokens, features),
        compiler_params=params(2),
        cost_estimate=pl.CostEstimate(
            flops=2 * experts * slots * features * units,
            bytes_accessed=2 * experts * features * units,
            transcendentals=0,
        ),
    )(*pieces, slot, weight, act, slope, w_down)


def inputs_kernel(groups, back, gate_grad, up_grad, w_gate, w_up, *refs):
    sums, held = refs[:-1], refs[-1]
    blocks, tokens, _ = back.shape
    for l in range(gate_grad.shape[0]):
        partial = dot(gate_grad[l], w_gate[l], NT) + dot(up_grad[l], w_up[l], NT)
        for b in range(blocks):
            held[b, l * MOST : (l + 1) * MOST] = partial[b * MOST : (b + 1) * MOST].astype(BF16)
    for out, members in zip(sums, groups):
        for place, b in enumerate(members):
            out[place * tokens : (place + 1) * tokens] = dot(back[b], held[b]).astype(BF16)


def input_sums(back, gate_grad, up_grad, w_gate, w_up, groups, part, parts):
    blocks, tokens, _ = back.shape
    experts, features, units = w_gate.shape
    wide = FEATURE_TILE
    steps = features // parts // wide
    slots = blocks * MOST
    across = pl.BlockSpec((experts, wide, units), lambda i: (0, part * steps + i, 0))
    return pl.pallas_call(
        functools.partial(inputs_kernel, groups),
        grid=(steps,),
        in_specs=[whole(back.shape), whole(gate_grad.shape), whole(up_grad.shape), across, across],
        out_specs=[pl.BlockSpec((len(g) * tokens, wide), lambda i: (0, i)) for g in groups],
        out_shape=[
            jax.ShapeDtypeStruct((len(g) * tokens, features // parts), BF16) for g in groups
        ],
        scratch_shapes=[pltpu.VMEM((blocks, experts * MOST, wide), BF16)],
        compiler_params=params(1),
        cost_estimate=pl.CostEstimate(
            flops=4 * experts * slots * features * units // parts,
            bytes_accessed=4 * experts * features * units // parts,
            transcendentals=0,
        ),
    )(back, gate_grad, up_grad, w_gate, w_up)


def back_matrix(slot):
    places = jnp.arange(MOST, dtype=F32)
    chosen = slot.transpose(1, 2, 0)[..., None] == places
    return chosen.reshape(slot.shape[1], slot.shape[2], -1).astype(BF16)


def weights_kernel(rows, gate_grad, up_grad, *refs):
    grad_gate, grad_up = refs[-2:]
    grad_gate[0] = dot(rows[0], gate_grad[0], TN)
    grad_up[0] = dot(rows[0], up_grad[0], TN)


def weight_grads(rows, gate_grad, up_grad, before, expert, first=0, steps=None):
    experts, slots, features = rows.shape
    units = gate_grad.shape[2]
    wide = FEATURE_TILE
    steps = features // wide if steps is None else steps
    unit = pl.BlockSpec((1, slots, units), lambda d: (expert, 0, 0))
    out = pl.BlockSpec((1, wide, units), lambda d: (expert, first + d, 0))
    kept = [] if before is None else list(before)
    return pl.pallas_call(
        weights_kernel,
        grid=(steps,),
        in_specs=[
            pl.BlockSpec((1, slots, wide), lambda d: (expert, 0, first + d)), unit, unit
        ]
        + [pl.BlockSpec(memory_space=pl.ANY)] * len(kept),
        out_specs=[out, out],
        out_shape=[jax.ShapeDtypeStruct((experts, features, units), F32)] * 2,
        input_output_aliases={3 + i: i for i in range(len(kept))},
        compiler_params=params(1),
        cost_estimate=pl.CostEstimate(
            flops=4 * slots * steps * wide * units,
            bytes_accessed=8 * steps * wide * units,
            transcendentals=0,
        ),
    )(rows, gate_grad, up_grad, *kept)


def route_table(routes, gate_values):
    tokens = routes.shape[0]
    experts = jnp.arange(EXPERTS, dtype=jnp.int32)[:, None, None]
    match = routes.T[None] == experts
    member = jnp.any(match, axis=1)
    gate = jnp.sum(jnp.where(match, gate_values.T[None], 0.0), axis=1)
    place = jnp.arange(tokens, dtype=jnp.int32)
    earlier = (place[:, None] < place[None, :]).astype(BF16)
    slot = jnp.where(member, dot(member.astype(BF16), earlier), -1.0)
    return jnp.stack([slot, gate], axis=1)


def flip(value, axis, bit):
    count = lax.axis_size(axis)
    return lax.ppermute(value, axis, [(i, i ^ bit) for i in range(count)])


def swap_order(value, side, pair, dim):
    shape = value.shape
    value = value.reshape(shape[:dim] + (2, 2, shape[dim] // 4) + shape[dim + 1 :])
    value = jnp.where(side == 1, jnp.flip(value, dim), value)
    return jnp.where(pair == 1, jnp.flip(value, dim + 1), value).reshape(shape)


def add(*terms):
    total = terms[0].astype(F32)
    for term in terms[1:]:
        total = total + term.astype(F32)
    return total.astype(BF16)


def quarters(value, count, at):
    return lax.dynamic_slice_in_dim(value, at * (count // 4), count // 4, 0)


def local_near(out_grad, routes, gate_values, layer_input, w_gate, w_up, w_down):
    experts, features, _ = w_gate.shape
    me = lax.axis_index("expert")
    position = lax.axis_index("dp")
    side, pair = position % 2, position // 2 % 2
    tokens = out_grad.shape[0]
    half, quarter = tokens // 2, tokens // 4
    corner = side * 2 + pair

    def to_core(values):
        return tuple(flip(v, "expert", 1) for v in values)

    x_mine = jnp.concatenate(
        [quarters(layer_input, tokens, q) for q in (corner, 3 - corner)], axis=0
    )
    x_mine, layer_input, out_grad, routes = lax.optimization_barrier(
        (x_mine, layer_input, out_grad, routes)
    )
    x_across = flip(x_mine, "expert", 2)
    x_sibling, g_sibling = to_core((layer_input, out_grad))
    table = route_table(routes, gate_values)
    tables = []
    for r in range(4):
        part = lax.dynamic_slice_in_dim(table, (me ^ r) * experts, experts, 0)
        tables.append(flip(part, "expert", r) if r > 0 else part)
    x_across, g_own = lax.optimization_barrier((x_across, out_grad))
    x_far = (x_across, flip(x_across[:quarter], "dp", 1), flip(x_across[:quarter], "dp", 2))
    g_across = flip(g_own, "expert", 2)
    x_far = (*x_far, *to_core(x_far))
    table = jnp.stack(tables, axis=2)
    slot, weight = table[:, 0], table[:, 1]
    back = back_matrix(swap_order(slot, side, pair, 2))
    far = swap_order(slot[:, 2:], side, pair, 2).reshape(experts, 2, 4, quarter)
    far = jnp.stack([far[:, :, q] for q in (0, 3, 2, 1)], axis=2).reshape(experts, 2, tokens)
    slot_x = jnp.concatenate([slot[:, :2], far], axis=1)
    rows, act, slope = forward((layer_input, x_sibling, *x_far), slot_x, w_gate, w_up)
    act, g_across = lax.optimization_barrier((act, g_across))
    gate_grad, up_grad = hidden_grads(
        (out_grad, g_sibling, g_across, *to_core((g_across,))), slot, weight, act, slope, w_down
    )

    groups = ((0, 2), (1, 3))
    kept_a, sent_a = input_sums(back, gate_grad, up_grad, w_gate, w_up, groups, 0, 2)
    kept_b, sent_b = input_sums(back, gate_grad, up_grad, w_gate, w_up, groups, 1, 2)

    def piece(after, before, *which):
        held, rows_now = lax.optimization_barrier((after, rows))
        return held, weight_grads(rows_now, gate_grad, up_grad, before, *which)

    def corners(value):
        return [flip(v, "dp", step) for v, step in zip(value, (2, 1, 3))]

    def cut(value, count):
        return [value[i : i + quarter] for i in range(0, count * quarter, quarter)]

    chip_a = add(kept_a, flip(sent_a, "expert", 1))
    got = flip(sent_b, "expert", 1)
    chip_b = [add(a, b) for a, b in zip(cut(kept_b, 8), cut(got, 8))]
    far_a = chip_a[tokens:]
    away = [jnp.concatenate([chip_b[q], chip_b[4 + q]], axis=0) for q in (1, 2, 3)]
    (far_a, *away), grads = piece((far_a, *away), None, 0, 0, 4)
    got_a, got_b = flip(far_a, "expert", 2), corners(away)
    got_a, got_b, *grads = lax.optimization_barrier((got_a, got_b, *grads))
    own_a = [add(a, b) for a, b in zip(cut(chip_a, 4), cut(got_a, 4))]
    mine_b = add(chip_b[0], *(v[:quarter] for v in got_b))
    far_b = add(chip_b[4], *(v[quarter:] for v in got_b))
    (far_b, *own_a), grads = piece((far_b, *own_a), grads, 0, 4, 2)
    got_a, got_b = corners(own_a[1:]), flip(far_b, "expert", 2)
    got_a, got_b, *grads = lax.optimization_barrier((got_a, got_b, *grads))
    mine = jnp.concatenate([add(own_a[0], *got_a), add(mine_b, got_b)], axis=1)
    mine, grads = piece(mine, grads, 1, 0, 3)
    got = flip(mine, "dp", 4)
    got, *grads = lax.optimization_barrier((got, *grads))
    mine = add(mine, got)
    mine, grads = piece(mine, grads, 1, 3, 3)
    got = corners([mine] * 3)
    got, *grads = lax.optimization_barrier((got, *grads))
    total = swap_order(jnp.concatenate([mine, *got], axis=0), side, pair, 0)
    return (total, *grads)


def local_any(out_grad, routes, gate_values, layer_input, w_gate, w_up, w_down):
    experts = w_gate.shape[0]
    me = lax.axis_index("expert")
    rows_in = lax.all_gather(layer_input, "expert", tiled=True)
    grads_in = lax.all_gather(out_grad, "expert", tiled=True)
    table = lax.all_gather(route_table(routes, gate_values), "expert")
    table = lax.dynamic_slice_in_dim(table, me * experts, experts, 1).transpose(1, 2, 0, 3)
    slot, weight = table[:, 0], table[:, 1]
    rows, act, slope = forward([rows_in], slot, w_gate, w_up)
    gate_grad, up_grad = hidden_grads([grads_in], slot, weight, act, slope, w_down)
    groups = (tuple(range(slot.shape[1])),)
    (sums,) = input_sums(back_matrix(slot), gate_grad, up_grad, w_gate, w_up, groups, 0, 1)
    grads = None
    for l in range(experts):
        grads = weight_grads(rows, gate_grad, up_grad, grads, l)
    own = lax.psum_scatter(sums, "expert", scatter_dimension=0, tiled=True)
    return (lax.psum(own, "dp"), *grads)


def solution(mesh):
    near = mesh.shape["dp"] == 8 and mesh.shape["expert"] == 4
    placed = (
        P("expert", None),
        P("expert", None),
        P("expert", None),
        P("expert", None),
        P("expert", None, "dp"),
        P("expert", None, "dp"),
        P("expert", None, "dp"),
    )
    return jax.shard_map(
        local_near if near else local_any,
        mesh=mesh,
        in_specs=placed,
        out_specs=(P("expert", None), P("expert", None, "dp"), P("expert", None, "dp")),
        check_vma=False,
    )
```

```python
import functools

import jax
import jax.numpy as jnp
from jax import lax
from jax.experimental import pallas as pl
from jax.experimental.pallas import tpu as pltpu
from jax.sharding import PartitionSpec as P

EXPERTS = 8
MOST = 80
UNIT_TILE = 512
FEATURE_TILE = 512
BF16 = jnp.bfloat16
F32 = jnp.float32
NN = (((1,), (0,)), ((), ()))
NT = (((1,), (1,)), ((), ()))
TN = (((0,), (0,)), ((), ()))


def dot(a, b, dims=NN):
    return lax.dot_general(a, b, dims, preferred_element_type=F32)


def params(count, mebibytes):
    return pltpu.CompilerParams(
        dimension_semantics=("arbitrary",) * count, vmem_limit_bytes=mebibytes * 1024 * 1024
    )


def whole(shape):
    return pl.BlockSpec(
        shape, lambda *_: (0,) * len(shape), pipeline_mode=pl.Buffered(buffer_count=1)
    )


def one_hot(slot_row):
    slots = lax.broadcasted_iota(jnp.int32, (MOST, slot_row.shape[1]), 0)
    return slots == slot_row.astype(jnp.int32)


def lay_out(held, pieces, first):
    rows, at = held.shape[0], 0
    for piece in pieces:
        low, high = max(first, at), min(first + rows, at + piece.shape[0])
        if low < high:
            held[low - first : high - first] = piece[low - at : high - at]
        at += piece.shape[0]


def column_chunks(features):
    step = 768 if features % 768 == 0 else features
    return [slice(c, c + step) for c in range(0, features, step)]


def dispatch(pieces, slot, held, chosen, out, weight=None):
    experts, blocks, tokens = slot.shape
    group = held.shape[0] // tokens
    places = [(l, b) for l in range(experts) for b in range(group)]
    for start in range(0, blocks, group):
        chosen[...] = jnp.zeros_like(chosen)
        scales = []
        for i, (l, b) in enumerate(places):
            at = slice(start + b, start + b + 1)
            mask = one_hot(slot[l, at, :])
            chosen[i * MOST : (i + 1) * MOST, b * tokens : (b + 1) * tokens] = mask.astype(BF16)
            if weight is not None:
                scales.append(
                    jnp.sum(jnp.where(mask, weight[l, at, :], 0.0), axis=1, keepdims=True)
                )
        lay_out(held, pieces, start * tokens)
        for cols in column_chunks(held.shape[1]):
            taken = dot(chosen[...], held[:, cols])
            for i, (l, b) in enumerate(places):
                part = taken[i * MOST : (i + 1) * MOST]
                if scales:
                    part = part * scales[i]
                span = slice((start + b) * MOST, (start + b + 1) * MOST)
                out[l, span, cols] = part.astype(BF16)


def dispatch_scratch(experts, blocks, tokens, features):
    group = 2 if blocks % 2 == 0 else 1
    return [
        pltpu.VMEM((group * tokens, features), BF16),
        pltpu.VMEM((experts * group * MOST, group * tokens), BF16),
        pltpu.VMEM((experts, blocks * MOST, features), BF16),
    ]


def forward_kernel(count, *refs):
    pieces, (slot, w_gate, w_up, rows_out, act, slope) = refs[:count], refs[count : count + 6]
    held, chosen, rows, sent = refs[count + 6 :]
    expert, tile = pl.program_id(0), pl.program_id(1)
    copy = pltpu.make_async_copy(rows, rows_out, sent)

    @pl.when((expert == 0) & (tile == 0))
    def _():
        dispatch(pieces, slot, held, chosen, rows)
        copy.start()

    x = rows[expert]
    gate = dot(x, w_gate[0])
    up = dot(x, w_up[0])
    sig = jax.nn.sigmoid(gate)
    act[0] = gate * sig
    slope[0] = up * sig * (1.0 + gate * (1.0 - sig))

    @pl.when((expert == pl.num_programs(0) - 1) & (tile == pl.num_programs(1) - 1))
    def _():
        copy.wait()


def forward(pieces, slot, w_gate, w_up):
    experts, blocks, tokens = slot.shape
    _, features, units = w_gate.shape
    tile = min(UNIT_TILE, units)
    slots = blocks * MOST
    matrix = pl.BlockSpec((1, features, tile), lambda l, f: (l, 0, f))
    unit = pl.BlockSpec((1, slots, tile), lambda l, f: (l, 0, f))
    return pl.pallas_call(
        functools.partial(forward_kernel, len(pieces)),
        grid=(experts, units // tile),
        in_specs=[whole(p.shape) for p in pieces] + [whole(slot.shape), matrix, matrix],
        out_specs=[pl.BlockSpec(memory_space=pltpu.HBM), unit, unit],
        out_shape=[
            jax.ShapeDtypeStruct((experts, slots, features), BF16),
            jax.ShapeDtypeStruct((experts, slots, units), F32),
            jax.ShapeDtypeStruct((experts, slots, units), F32),
        ],
        scratch_shapes=dispatch_scratch(experts, blocks, tokens, features)
        + [pltpu.SemaphoreType.DMA],
        compiler_params=params(2, 52),
        cost_estimate=pl.CostEstimate(
            flops=4 * experts * slots * features * units,
            bytes_accessed=4 * experts * features * units,
            transcendentals=experts * slots * units,
        ),
    )(*pieces, slot, w_gate, w_up)


def hidden_kernel(count, *refs):
    pieces, (slot, weight, act, slope, w_down) = refs[:count], refs[count : count + 5]
    gate_grad, up_grad, held, chosen, grads = refs[count + 5 :]
    expert = pl.program_id(0)

    @pl.when((expert == 0) & (pl.program_id(1) == 0))
    def _():
        dispatch(pieces, slot, held, chosen, grads, weight)

    hidden = dot(grads[expert], w_down[0])
    up_grad[0] = (hidden * act[0]).astype(BF16)
    gate_grad[0] = (hidden * slope[0]).astype(BF16)


def hidden_grads(pieces, slot, weight, act, slope, w_down):
    experts, blocks, tokens = slot.shape
    _, features, units = w_down.shape
    tile = min(UNIT_TILE, units)
    slots = blocks * MOST
    unit = pl.BlockSpec((1, slots, tile), lambda l, f: (l, 0, f))
    return pl.pallas_call(
        functools.partial(hidden_kernel, len(pieces)),
        grid=(experts, units // tile),
        in_specs=[whole(p.shape) for p in pieces]
        + [whole(slot.shape), whole(slot.shape), unit, unit]
        + [pl.BlockSpec((1, features, tile), lambda l, f: (l, 0, f))],
        out_specs=[unit, unit],
        out_shape=[jax.ShapeDtypeStruct((experts, slots, units), BF16)] * 2,
        scratch_shapes=dispatch_scratch(experts, blocks, tokens, features),
        compiler_params=params(2, 48),
        cost_estimate=pl.CostEstimate(
            flops=2 * experts * slots * features * units,
            bytes_accessed=2 * experts * features * units,
            transcendentals=0,
        ),
    )(*pieces, slot, weight, act, slope, w_down)


def inputs_kernel(groups, back, gate_grad, up_grad, w_gate, w_up, *refs):
    sums, held = refs[:-1], refs[-1]
    blocks, tokens, _ = back.shape
    for l in range(gate_grad.shape[0]):
        partial = dot(gate_grad[l], w_gate[l], NT) + dot(up_grad[l], w_up[l], NT)
        for b in range(blocks):
            held[b, l * MOST : (l + 1) * MOST] = partial[b * MOST : (b + 1) * MOST].astype(BF16)
    for out, members in zip(sums, groups):
        for place, b in enumerate(members):
            out[place * tokens : (place + 1) * tokens] = dot(back[b], held[b]).astype(BF16)


def input_sums(back, gate_grad, up_grad, w_gate, w_up, groups, part, parts):
    blocks, tokens, _ = back.shape
    experts, features, units = w_gate.shape
    wide = FEATURE_TILE
    steps = features // parts // wide
    slots = blocks * MOST
    across = pl.BlockSpec((experts, wide, units), lambda i: (0, part * steps + i, 0))
    return pl.pallas_call(
        functools.partial(inputs_kernel, groups),
        grid=(steps,),
        in_specs=[whole(back.shape), whole(gate_grad.shape), whole(up_grad.shape), across, across],
        out_specs=[pl.BlockSpec((len(g) * tokens, wide), lambda i: (0, i)) for g in groups],
        out_shape=[
            jax.ShapeDtypeStruct((len(g) * tokens, features // parts), BF16) for g in groups
        ],
        scratch_shapes=[pltpu.VMEM((blocks, experts * MOST, wide), BF16)],
        compiler_params=params(1, 40),
        cost_estimate=pl.CostEstimate(
            flops=4 * experts * slots * features * units // parts,
            bytes_accessed=4 * experts * features * units // parts,
            transcendentals=0,
        ),
    )(back, gate_grad, up_grad, w_gate, w_up)


def back_matrix(slot):
    places = jnp.arange(MOST, dtype=F32)
    slot = lax.optimization_barrier(slot.transpose(1, 2, 0))
    parts = [slot[..., l : l + 1] == places for l in range(slot.shape[2])]
    return jnp.concatenate([p.astype(BF16) for p in parts], axis=2)


def weights_kernel(rows, gate_grad, up_grad, *refs):
    grad_gate, grad_up = refs[-2:]
    grad_gate[0] = dot(rows[0], gate_grad[0], TN)
    grad_up[0] = dot(rows[0], up_grad[0], TN)


def weight_grads(rows, gate_grad, up_grad, before, expert, first=0, steps=None):
    experts, slots, features = rows.shape
    units = gate_grad.shape[2]
    wide = FEATURE_TILE
    steps = features // wide if steps is None else steps
    unit = pl.BlockSpec((1, slots, units), lambda d: (expert, 0, 0))
    out = pl.BlockSpec((1, wide, units), lambda d: (expert, first + d, 0))
    kept = [] if before is None else list(before)
    return pl.pallas_call(
        weights_kernel,
        grid=(steps,),
        in_specs=[
            pl.BlockSpec((1, slots, wide), lambda d: (expert, 0, first + d)), unit, unit
        ]
        + [pl.BlockSpec(memory_space=pl.ANY)] * len(kept),
        out_specs=[out, out],
        out_shape=[jax.ShapeDtypeStruct((experts, features, units), F32)] * 2,
        input_output_aliases={3 + i: i for i in range(len(kept))},
        compiler_params=params(1, 30),
        cost_estimate=pl.CostEstimate(
            flops=4 * slots * steps * wide * units,
            bytes_accessed=8 * steps * wide * units,
            transcendentals=0,
        ),
    )(rows, gate_grad, up_grad, *kept)


def route_table(routes, gate_values):
    tokens = routes.shape[0]
    experts = jnp.arange(EXPERTS, dtype=jnp.int32)[:, None, None]
    match = routes.T[None] == experts
    member = jnp.any(match, axis=1)
    gate = jnp.sum(jnp.where(match, gate_values.T[None], 0.0), axis=1)
    place = jnp.arange(tokens, dtype=jnp.int32)
    earlier = (place[:, None] < place[None, :]).astype(BF16)
    slot = jnp.where(member, dot(member.astype(BF16), earlier), -1.0)
    return jnp.stack([slot, gate], axis=1)


def flip(value, axis, bit):
    count = lax.axis_size(axis)
    return lax.ppermute(value, axis, [(i, i ^ bit) for i in range(count)])


def swap_order(value, side, pair, dim):
    shape = value.shape
    value = value.reshape(shape[:dim] + (2, 2, shape[dim] // 4) + shape[dim + 1 :])
    value = jnp.where(side == 1, jnp.flip(value, dim), value)
    return jnp.where(pair == 1, jnp.flip(value, dim + 1), value).reshape(shape)


def add(*terms):
    total = terms[0].astype(F32)
    for term in terms[1:]:
        total = total + term.astype(F32)
    return total.astype(BF16)


def quarters(value, count, at):
    return lax.dynamic_slice_in_dim(value, at * (count // 4), count // 4, 0)


def local_near(out_grad, routes, gate_values, layer_input, w_gate, w_up, w_down):
    experts, features, _ = w_gate.shape
    me = lax.axis_index("expert")
    position = lax.axis_index("dp")
    side, pair = position % 2, position // 2 % 2
    tokens = out_grad.shape[0]
    half, quarter = tokens // 2, tokens // 4
    corner = side * 2 + pair

    def to_core(values):
        return tuple(flip(v, "expert", 1) for v in values)

    x_mine = jnp.concatenate(
        [quarters(layer_input, tokens, q) for q in (corner, 3 - corner)], axis=0
    )
    x_mine, layer_input, out_grad, routes = lax.optimization_barrier(
        (x_mine, layer_input, out_grad, routes)
    )
    x_across = flip(x_mine, "expert", 2)
    x_sibling, g_sibling = to_core((layer_input, out_grad))
    x_sibling, routes = lax.optimization_barrier((x_sibling, routes))
    table = route_table(routes, gate_values)
    tables = []
    for r in range(4):
        part = lax.dynamic_slice_in_dim(table, (me ^ r) * experts, experts, 0)
        tables.append(flip(part, "expert", r) if r > 0 else part)
    x_across, g_own = lax.optimization_barrier((x_across, out_grad))
    x_far = (x_across, flip(x_across[:quarter], "dp", 1), flip(x_across[:quarter], "dp", 2))
    g_across = flip(g_own, "expert", 2)
    x_far = (*x_far, *to_core(x_far))
    table = jnp.stack(tables, axis=2)
    slot, weight = table[:, 0], table[:, 1]
    back = back_matrix(swap_order(slot, side, pair, 2))
    far = swap_order(slot[:, 2:], side, pair, 2).reshape(experts, 2, 4, quarter)
    far = jnp.stack([far[:, :, q] for q in (0, 3, 2, 1)], axis=2).reshape(experts, 2, tokens)
    slot_x = jnp.concatenate([slot[:, :2], far], axis=1)
    slot_x, back = lax.optimization_barrier((slot_x, back))
    rows, act, slope = forward((layer_input, x_sibling, *x_far), slot_x, w_gate, w_up)
    act, g_across = lax.optimization_barrier((act, g_across))
    gate_grad, up_grad = hidden_grads(
        (out_grad, g_sibling, g_across, *to_core((g_across,))), slot, weight, act, slope, w_down
    )

    groups = ((0, 2), (1, 3))
    kept_a, sent_a = input_sums(back, gate_grad, up_grad, w_gate, w_up, groups, 0, 2)
    kept_b, sent_b = input_sums(back, gate_grad, up_grad, w_gate, w_up, groups, 1, 2)

    def piece(after, before, *which):
        held, rows_now = lax.optimization_barrier((after, rows))
        return held, weight_grads(rows_now, gate_grad, up_grad, before, *which)

    def corners(value):
        return [flip(v, "dp", step) for v, step in zip(value, (2, 1, 3))]

    def cut(value, count):
        return [value[i : i + quarter] for i in range(0, count * quarter, quarter)]

    chip_a = add(kept_a, flip(sent_a, "expert", 1))
    got = flip(sent_b, "expert", 1)
    chip_b = [add(a, b) for a, b in zip(cut(kept_b, 8), cut(got, 8))]
    far_a = chip_a[tokens:]
    away = [jnp.concatenate([chip_b[q], chip_b[4 + q]], axis=0) for q in (1, 2, 3)]
    (far_a, *away), grads = piece((far_a, *away), None, 0, 0, 5)
    got_a, got_b = flip(far_a, "expert", 2), corners(away)
    got_a, got_b, *grads = lax.optimization_barrier((got_a, got_b, *grads))
    own_a = [add(a, b) for a, b in zip(cut(chip_a, 4), cut(got_a, 4))]
    mine_b = add(chip_b[0], *(v[:quarter] for v in got_b))
    far_b = add(chip_b[4], *(v[quarter:] for v in got_b))
    (far_b, *own_a), grads = piece((far_b, *own_a), grads, 0, 5, 1)
    got_a, got_b = corners(own_a[1:]), flip(far_b, "expert", 2)
    got_a, got_b, *grads = lax.optimization_barrier((got_a, got_b, *grads))
    mine = jnp.concatenate([add(own_a[0], *got_a), add(mine_b, got_b)], axis=1)
    mine, grads = piece(mine, grads, 1, 0, 3)
    got = flip(mine, "dp", 4)
    got, *grads = lax.optimization_barrier((got, *grads))
    mine = add(mine, got)
    mine, grads = piece(mine, grads, 1, 3, 3)
    got = corners([mine] * 3)
    got, *grads = lax.optimization_barrier((got, *grads))
    total = swap_order(jnp.concatenate([mine, *got], axis=0), side, pair, 0)
    return (total, *grads)


def local_any(out_grad, routes, gate_values, layer_input, w_gate, w_up, w_down):
    experts = w_gate.shape[0]
    me = lax.axis_index("expert")
    rows_in = lax.all_gather(layer_input, "expert", tiled=True)
    grads_in = lax.all_gather(out_grad, "expert", tiled=True)
    table = lax.all_gather(route_table(routes, gate_values), "expert")
    table = lax.dynamic_slice_in_dim(table, me * experts, experts, 1).transpose(1, 2, 0, 3)
    slot, weight = table[:, 0], table[:, 1]
    rows, act, slope = forward([rows_in], slot, w_gate, w_up)
    gate_grad, up_grad = hidden_grads([grads_in], slot, weight, act, slope, w_down)
    groups = (tuple(range(slot.shape[1])),)
    (sums,) = input_sums(back_matrix(slot), gate_grad, up_grad, w_gate, w_up, groups, 0, 1)
    grads = None
    for l in range(experts):
        grads = weight_grads(rows, gate_grad, up_grad, grads, l)
    own = lax.psum_scatter(sums, "expert", scatter_dimension=0, tiled=True)
    return (lax.psum(own, "dp"), *grads)


def solution(mesh):
    near = mesh.shape["dp"] == 8 and mesh.shape["expert"] == 4
    placed = (
        P("expert", None),
        P("expert", None),
        P("expert", None),
        P("expert", None),
        P("expert", None, "dp"),
        P("expert", None, "dp"),
        P("expert", None, "dp"),
    )
    return jax.shard_map(
        local_near if near else local_any,
        mesh=mesh,
        in_specs=placed,
        out_specs=(P("expert", None), P("expert", None, "dp"), P("expert", None, "dp")),
        check_vma=False,
    )
```

```python
import functools

import jax
import jax.numpy as jnp
from jax import lax
from jax.experimental import pallas as pl
from jax.experimental.pallas import tpu as pltpu
from jax.sharding import PartitionSpec as P

EXPERTS = 8
MOST = 80
UNIT_TILE = 512
FEATURE_TILE = 512
BF16 = jnp.bfloat16
F32 = jnp.float32
NN = (((1,), (0,)), ((), ()))
NT = (((1,), (1,)), ((), ()))
TN = (((0,), (0,)), ((), ()))


def dot(a, b, dims=NN):
    return lax.dot_general(a, b, dims, preferred_element_type=F32)


def params(count, mebibytes):
    return pltpu.CompilerParams(
        dimension_semantics=("arbitrary",) * count, vmem_limit_bytes=mebibytes * 1024 * 1024
    )


def whole(shape):
    return pl.BlockSpec(
        shape, lambda *_: (0,) * len(shape), pipeline_mode=pl.Buffered(buffer_count=1)
    )


def one_hot(slot_row):
    slots = lax.broadcasted_iota(jnp.int32, (MOST, slot_row.shape[1]), 0)
    return slots == slot_row.astype(jnp.int32)


def lay_out(held, pieces, first):
    rows, at = held.shape[0], 0
    for piece in pieces:
        low, high = max(first, at), min(first + rows, at + piece.shape[0])
        if low < high:
            held[low - first : high - first] = piece[low - at : high - at]
        at += piece.shape[0]


def column_chunks(features):
    step = 768 if features % 768 == 0 else features
    return [slice(c, c + step) for c in range(0, features, step)]


def dispatch(pieces, slot, held, chosen, out, weight=None):
    experts, blocks, tokens = slot.shape
    group = held.shape[0] // tokens
    places = [(l, b) for l in range(experts) for b in range(group)]
    for start in range(0, blocks, group):
        chosen[...] = jnp.zeros_like(chosen)
        scales = []
        for i, (l, b) in enumerate(places):
            at = slice(start + b, start + b + 1)
            mask = one_hot(slot[l, at, :])
            chosen[i * MOST : (i + 1) * MOST, b * tokens : (b + 1) * tokens] = mask.astype(BF16)
            if weight is not None:
                scales.append(
                    jnp.sum(jnp.where(mask, weight[l, at, :], 0.0), axis=1, keepdims=True)
                )
        lay_out(held, pieces, start * tokens)
        for cols in column_chunks(held.shape[1]):
            taken = dot(chosen[...], held[:, cols])
            for i, (l, b) in enumerate(places):
                part = taken[i * MOST : (i + 1) * MOST]
                if scales:
                    part = part * scales[i]
                span = slice((start + b) * MOST, (start + b + 1) * MOST)
                out[l, span, cols] = part.astype(BF16)


def dispatch_scratch(experts, blocks, tokens, features):
    group = 2 if blocks % 2 == 0 else 1
    return [
        pltpu.VMEM((group * tokens, features), BF16),
        pltpu.VMEM((experts * group * MOST, group * tokens), BF16),
        pltpu.VMEM((experts, blocks * MOST, features), BF16),
    ]


def forward_kernel(count, *refs):
    pieces, (slot, w_gate, w_up, rows_out, act, slope) = refs[:count], refs[count : count + 6]
    held, chosen, rows, sent = refs[count + 6 :]
    expert, tile = pl.program_id(0), pl.program_id(1)
    copy = pltpu.make_async_copy(rows, rows_out, sent)

    @pl.when((expert == 0) & (tile == 0))
    def _():
        dispatch(pieces, slot, held, chosen, rows)
        copy.start()

    x = rows[expert]
    gate = dot(x, w_gate[0])
    up = dot(x, w_up[0])
    sig = jax.nn.sigmoid(gate)
    act[0] = gate * sig
    slope[0] = up * sig * (1.0 + gate * (1.0 - sig))

    @pl.when((expert == pl.num_programs(0) - 1) & (tile == pl.num_programs(1) - 1))
    def _():
        copy.wait()


def forward(pieces, slot, w_gate, w_up):
    experts, blocks, tokens = slot.shape
    _, features, units = w_gate.shape
    tile = min(UNIT_TILE, units)
    slots = blocks * MOST
    matrix = pl.BlockSpec((1, features, tile), lambda l, f: (l, 0, f))
    unit = pl.BlockSpec((1, slots, tile), lambda l, f: (l, 0, f))
    return pl.pallas_call(
        functools.partial(forward_kernel, len(pieces)),
        grid=(experts, units // tile),
        in_specs=[whole(p.shape) for p in pieces] + [whole(slot.shape), matrix, matrix],
        out_specs=[pl.BlockSpec(memory_space=pltpu.HBM), unit, unit],
        out_shape=[
            jax.ShapeDtypeStruct((experts, slots, features), BF16),
            jax.ShapeDtypeStruct((experts, slots, units), F32),
            jax.ShapeDtypeStruct((experts, slots, units), F32),
        ],
        scratch_shapes=dispatch_scratch(experts, blocks, tokens, features)
        + [pltpu.SemaphoreType.DMA],
        compiler_params=params(2, 52),
        cost_estimate=pl.CostEstimate(
            flops=4 * experts * slots * features * units,
            bytes_accessed=4 * experts * features * units,
            transcendentals=experts * slots * units,
        ),
    )(*pieces, slot, w_gate, w_up)


def hidden_kernel(count, *refs):
    pieces, (slot, weight, act, slope, w_down) = refs[:count], refs[count : count + 5]
    gate_grad, up_grad, held, chosen, grads = refs[count + 5 :]
    expert = pl.program_id(0)

    @pl.when((expert == 0) & (pl.program_id(1) == 0))
    def _():
        dispatch(pieces, slot, held, chosen, grads, weight)

    hidden = dot(grads[expert], w_down[0])
    up_grad[0] = (hidden * act[0]).astype(BF16)
    gate_grad[0] = (hidden * slope[0]).astype(BF16)


def hidden_grads(pieces, slot, weight, act, slope, w_down):
    experts, blocks, tokens = slot.shape
    _, features, units = w_down.shape
    tile = min(UNIT_TILE, units)
    slots = blocks * MOST
    unit = pl.BlockSpec((1, slots, tile), lambda l, f: (l, 0, f))
    return pl.pallas_call(
        functools.partial(hidden_kernel, len(pieces)),
        grid=(experts, units // tile),
        in_specs=[whole(p.shape) for p in pieces]
        + [whole(slot.shape), whole(slot.shape), unit, unit]
        + [pl.BlockSpec((1, features, tile), lambda l, f: (l, 0, f))],
        out_specs=[unit, unit],
        out_shape=[jax.ShapeDtypeStruct((experts, slots, units), BF16)] * 2,
        scratch_shapes=dispatch_scratch(experts, blocks, tokens, features),
        compiler_params=params(2, 48),
        cost_estimate=pl.CostEstimate(
            flops=2 * experts * slots * features * units,
            bytes_accessed=2 * experts * features * units,
            transcendentals=0,
        ),
    )(*pieces, slot, weight, act, slope, w_down)


def inputs_kernel(groups, back, gate_grad, up_grad, w_gate, w_up, *refs):
    sums, held = refs[:-1], refs[-1]
    blocks, tokens, _ = back.shape
    for l in range(gate_grad.shape[0]):
        partial = dot(gate_grad[l], w_gate[l], NT) + dot(up_grad[l], w_up[l], NT)
        for b in range(blocks):
            held[b, l * MOST : (l + 1) * MOST] = partial[b * MOST : (b + 1) * MOST].astype(BF16)
    for out, members in zip(sums, groups):
        for place, b in enumerate(members):
            out[place * tokens : (place + 1) * tokens] = dot(back[b], held[b]).astype(BF16)


def input_sums(back, gate_grad, up_grad, w_gate, w_up, groups, part, parts):
    blocks, tokens, _ = back.shape
    experts, features, units = w_gate.shape
    wide = FEATURE_TILE
    steps = features // parts // wide
    slots = blocks * MOST
    across = pl.BlockSpec((experts, wide, units), lambda i: (0, part * steps + i, 0))
    return pl.pallas_call(
        functools.partial(inputs_kernel, groups),
        grid=(steps,),
        in_specs=[whole(back.shape), whole(gate_grad.shape), whole(up_grad.shape), across, across],
        out_specs=[pl.BlockSpec((len(g) * tokens, wide), lambda i: (0, i)) for g in groups],
        out_shape=[
            jax.ShapeDtypeStruct((len(g) * tokens, features // parts), BF16) for g in groups
        ],
        scratch_shapes=[pltpu.VMEM((blocks, experts * MOST, wide), BF16)],
        compiler_params=params(1, 40),
        cost_estimate=pl.CostEstimate(
            flops=4 * experts * slots * features * units // parts,
            bytes_accessed=4 * experts * features * units // parts,
            transcendentals=0,
        ),
    )(back, gate_grad, up_grad, w_gate, w_up)


def back_matrix(slot):
    places = jnp.arange(MOST, dtype=F32)
    slot = lax.optimization_barrier(slot.transpose(1, 2, 0))
    parts = [slot[..., l : l + 1] == places for l in range(slot.shape[2])]
    return jnp.concatenate([p.astype(BF16) for p in parts], axis=2)


def weights_kernel(rows, gate_grad, up_grad, *refs):
    grad_gate, grad_up = refs[-2:]
    grad_gate[0] = dot(rows[0], gate_grad[0], TN)
    grad_up[0] = dot(rows[0], up_grad[0], TN)


def weight_grads(rows, gate_grad, up_grad, before, first, steps):
    experts, slots, features = rows.shape
    units = gate_grad.shape[2]
    wide = FEATURE_TILE
    each = features // wide
    unit = pl.BlockSpec((1, slots, units), lambda i: ((first + i) // each, 0, 0))
    out = pl.BlockSpec((1, wide, units), lambda i: ((first + i) // each, (first + i) % each, 0))
    kept = [] if before is None else list(before)
    return pl.pallas_call(
        weights_kernel,
        grid=(steps,),
        in_specs=[
            pl.BlockSpec((1, slots, wide), lambda i: ((first + i) // each, 0, (first + i) % each)),
            unit,
            unit,
        ]
        + [pl.BlockSpec(memory_space=pl.ANY)] * len(kept),
        out_specs=[out, out],
        out_shape=[jax.ShapeDtypeStruct((experts, features, units), F32)] * 2,
        input_output_aliases={3 + i: i for i in range(len(kept))},
        compiler_params=params(1, 30),
        cost_estimate=pl.CostEstimate(
            flops=4 * slots * steps * wide * units,
            bytes_accessed=8 * steps * wide * units,
            transcendentals=0,
        ),
    )(rows, gate_grad, up_grad, *kept)


def route_table(routes, gate_values):
    tokens = routes.shape[0]
    experts = jnp.arange(EXPERTS, dtype=jnp.int32)[:, None, None]
    match = routes.T[None] == experts
    member = jnp.any(match, axis=1)
    gate = jnp.sum(jnp.where(match, gate_values.T[None], 0.0), axis=1)
    place = jnp.arange(tokens, dtype=jnp.int32)
    earlier = (place[:, None] < place[None, :]).astype(BF16)
    slot = jnp.where(member, dot(member.astype(BF16), earlier), -1.0)
    return jnp.stack([slot, gate], axis=1)


def flip(value, axis, bit):
    count = lax.axis_size(axis)
    return lax.ppermute(value, axis, [(i, i ^ bit) for i in range(count)])


def swap_order(value, side, pair, dim):
    shape = value.shape
    value = value.reshape(shape[:dim] + (2, 2, shape[dim] // 4) + shape[dim + 1 :])
    value = jnp.where(side == 1, jnp.flip(value, dim), value)
    return jnp.where(pair == 1, jnp.flip(value, dim + 1), value).reshape(shape)


def add(*terms):
    total = terms[0].astype(F32)
    for term in terms[1:]:
        total = total + term.astype(F32)
    return total.astype(BF16)


def quarters(value, count, at):
    return lax.dynamic_slice_in_dim(value, at * (count // 4), count // 4, 0)


def local_near(out_grad, routes, gate_values, layer_input, w_gate, w_up, w_down):
    experts, features, _ = w_gate.shape
    me = lax.axis_index("expert")
    position = lax.axis_index("dp")
    side, pair = position % 2, position // 2 % 2
    tokens = out_grad.shape[0]
    half, quarter = tokens // 2, tokens // 4
    corner = side * 2 + pair

    def to_core(values):
        return tuple(flip(v, "expert", 1) for v in values)

    x_mine = [quarters(layer_input, tokens, q) for q in (corner, 3 - corner)]
    *x_mine, layer_input, out_grad, routes = lax.optimization_barrier(
        (*x_mine, layer_input, out_grad, routes)
    )
    x_across, x_corner = [flip(v, "expert", 2) for v in x_mine]
    x_sibling, g_sibling = to_core((layer_input, out_grad))
    x_sibling, routes = lax.optimization_barrier((x_sibling, routes))
    table = route_table(routes, gate_values)
    tables = []
    for r in range(4):
        part = lax.dynamic_slice_in_dim(table, (me ^ r) * experts, experts, 0)
        tables.append(flip(part, "expert", r) if r > 0 else part)
    x_corner, g_own = lax.optimization_barrier((x_corner, out_grad))
    x_far = (x_across, x_corner, flip(x_across, "dp", 1), flip(x_across, "dp", 2))
    g_across = flip(g_own, "expert", 2)
    x_far = (*x_far, *to_core(x_far))
    table = jnp.stack(tables, axis=2)
    slot, weight = table[:, 0], table[:, 1]
    back = back_matrix(swap_order(slot, side, pair, 2))
    far = swap_order(slot[:, 2:], side, pair, 2).reshape(experts, 2, 4, quarter)
    far = jnp.stack([far[:, :, q] for q in (0, 3, 2, 1)], axis=2).reshape(experts, 2, tokens)
    slot_x = jnp.concatenate([slot[:, :2], far], axis=1)
    slot_x, back = lax.optimization_barrier((slot_x, back))
    rows, act, slope = forward((layer_input, x_sibling, *x_far), slot_x, w_gate, w_up)
    act, g_across = lax.optimization_barrier((act, g_across))
    gate_grad, up_grad = hidden_grads(
        (out_grad, g_sibling, g_across, *to_core((g_across,))), slot, weight, act, slope, w_down
    )

    groups = ((0, 2), (1, 3))
    kept_a, sent_a = input_sums(back, gate_grad, up_grad, w_gate, w_up, groups, 0, 2)
    kept_b, sent_b = input_sums(back, gate_grad, up_grad, w_gate, w_up, groups, 1, 2)

    def piece(after, before, *which):
        held, rows_now = lax.optimization_barrier((after, rows))
        return held, weight_grads(rows_now, gate_grad, up_grad, before, *which)

    def corners(value):
        return [flip(v, "dp", step) for v, step in zip(value, (2, 1, 3))]

    def cut(value, count):
        return [value[i : i + quarter] for i in range(0, count * quarter, quarter)]

    chip_a = add(kept_a, flip(sent_a, "expert", 1))
    got = flip(sent_b, "expert", 1)
    chip_b = [add(a, b) for a, b in zip(cut(kept_b, 8), cut(got, 8))]
    far_a = chip_a[tokens:]
    away = [jnp.concatenate([chip_b[q], chip_b[4 + q]], axis=0) for q in (1, 2, 3)]
    (far_a, *away), grads = piece((far_a, *away), None, 0, 3)
    got_a, got_b = flip(far_a, "expert", 2), corners(away)
    got_a, got_b, *grads = lax.optimization_barrier((got_a, got_b, *grads))
    own_a = [add(a, b) for a, b in zip(cut(chip_a, 4), cut(got_a, 4))]
    mine_b = add(chip_b[0], *(v[:quarter] for v in got_b))
    far_b = add(chip_b[4], *(v[quarter:] for v in got_b))
    (far_b, *own_a), grads = piece((far_b, *own_a), grads, 3, 2)
    got_a, got_b = corners(own_a[1:]), flip(far_b, "expert", 2)
    got_a, got_b, *grads = lax.optimization_barrier((got_a, got_b, *grads))
    mine = jnp.concatenate([add(own_a[0], *got_a), add(mine_b, got_b)], axis=1)
    mine, grads = piece(mine, grads, 5, 4)
    got = flip(mine, "dp", 4)
    got, *grads = lax.optimization_barrier((got, *grads))
    mine = add(mine, got)
    mine, grads = piece(mine, grads, 9, 3)
    got = corners([mine] * 3)
    got, *grads = lax.optimization_barrier((got, *grads))
    total = swap_order(jnp.concatenate([mine, *got], axis=0), side, pair, 0)
    return (total, *grads)


def local_any(out_grad, routes, gate_values, layer_input, w_gate, w_up, w_down):
    experts = w_gate.shape[0]
    me = lax.axis_index("expert")
    rows_in = lax.all_gather(layer_input, "expert", tiled=True)
    grads_in = lax.all_gather(out_grad, "expert", tiled=True)
    table = lax.all_gather(route_table(routes, gate_values), "expert")
    table = lax.dynamic_slice_in_dim(table, me * experts, experts, 1).transpose(1, 2, 0, 3)
    slot, weight = table[:, 0], table[:, 1]
    rows, act, slope = forward([rows_in], slot, w_gate, w_up)
    gate_grad, up_grad = hidden_grads([grads_in], slot, weight, act, slope, w_down)
    groups = (tuple(range(slot.shape[1])),)
    (sums,) = input_sums(back_matrix(slot), gate_grad, up_grad, w_gate, w_up, groups, 0, 1)
    blocks = experts * layer_input.shape[1] // FEATURE_TILE
    grads = weight_grads(rows, gate_grad, up_grad, None, 0, blocks)
    own = lax.psum_scatter(sums, "expert", scatter_dimension=0, tiled=True)
    return (lax.psum(own, "dp"), *grads)


def solution(mesh):
    near = mesh.shape["dp"] == 8 and mesh.shape["expert"] == 4
    placed = (
        P("expert", None),
        P("expert", None),
        P("expert", None),
        P("expert", None),
        P("expert", None, "dp"),
        P("expert", None, "dp"),
        P("expert", None, "dp"),
    )
    return jax.shard_map(
        local_near if near else local_any,
        mesh=mesh,
        in_specs=placed,
        out_specs=(P("expert", None), P("expert", None, "dp"), P("expert", None, "dp")),
        check_vma=False,
    )
```

```python
import functools

import jax
import jax.numpy as jnp
from jax import lax
from jax.experimental import pallas as pl
from jax.experimental.pallas import tpu as pltpu
from jax.sharding import PartitionSpec as P

EXPERTS = 8
MOST = 80
UNIT_TILE = 512
FEATURE_TILE = 512
BF16 = jnp.bfloat16
F32 = jnp.float32
NN = (((1,), (0,)), ((), ()))
NT = (((1,), (1,)), ((), ()))
TN = (((0,), (0,)), ((), ()))


def dot(a, b, dims=NN):
    return lax.dot_general(a, b, dims, preferred_element_type=F32)


def params(count, mebibytes):
    return pltpu.CompilerParams(
        dimension_semantics=("arbitrary",) * count, vmem_limit_bytes=mebibytes * 1024 * 1024
    )


def whole(shape):
    return pl.BlockSpec(
        shape, lambda *_: (0,) * len(shape), pipeline_mode=pl.Buffered(buffer_count=1)
    )


def one_hot(slot_row):
    slots = lax.broadcasted_iota(jnp.int32, (MOST, slot_row.shape[1]), 0)
    return slots == slot_row.astype(jnp.int32)


def lay_out(held, pieces, first):
    rows, at = held.shape[0], 0
    for piece in pieces:
        low, high = max(first, at), min(first + rows, at + piece.shape[0])
        if low < high:
            held[low - first : high - first] = piece[low - at : high - at]
        at += piece.shape[0]


def column_chunks(features):
    step = 768 if features % 768 == 0 else features
    return [slice(c, c + step) for c in range(0, features, step)]


def dispatch(pieces, slot, held, chosen, out, weight=None):
    experts, blocks, tokens = slot.shape
    group = held.shape[0] // tokens
    places = [(l, b) for l in range(experts) for b in range(group)]
    for start in range(0, blocks, group):
        chosen[...] = jnp.zeros_like(chosen)
        scales = []
        for i, (l, b) in enumerate(places):
            at = slice(start + b, start + b + 1)
            mask = one_hot(slot[l, at, :])
            chosen[i * MOST : (i + 1) * MOST, b * tokens : (b + 1) * tokens] = mask.astype(BF16)
            if weight is not None:
                scales.append(
                    jnp.sum(jnp.where(mask, weight[l, at, :], 0.0), axis=1, keepdims=True)
                )
        lay_out(held, pieces, start * tokens)
        for cols in column_chunks(held.shape[1]):
            taken = dot(chosen[...], held[:, cols])
            for i, (l, b) in enumerate(places):
                part = taken[i * MOST : (i + 1) * MOST]
                if scales:
                    part = part * scales[i]
                span = slice((start + b) * MOST, (start + b + 1) * MOST)
                out[l, span, cols] = part.astype(BF16)


def dispatch_scratch(experts, blocks, tokens, features):
    group = 2 if blocks % 2 == 0 else 1
    return [
        pltpu.VMEM((group * tokens, features), BF16),
        pltpu.VMEM((experts * group * MOST, group * tokens), BF16),
        pltpu.VMEM((experts, blocks * MOST, features), BF16),
    ]


def weight_tiles(step, matrices, buffers, ready):
    _, features, tile = buffers[0].shape
    tiles = matrices[0].shape[2] // tile
    cols = pl.ds(pl.multiple_of(step % tiles * tile, tile), tile)
    return [
        pltpu.make_async_copy(
            matrix.at[step // tiles, :, cols], buffer.at[step % 2], ready.at[step % 2, i]
        )
        for i, (matrix, buffer) in enumerate(zip(matrices, buffers))
    ]


def next_tiles(step, matrices, buffers, ready):
    @pl.when(step + 1 < pl.num_programs(0))
    def _():
        for copy in weight_tiles(step + 1, matrices, buffers, ready):
            copy.start()

    for copy in weight_tiles(step, matrices, buffers, ready):
        copy.wait()


def forward_kernel(count, *refs):
    pieces, (slot, w_gate, w_up, rows_out, act, slope) = refs[:count], refs[count : count + 6]
    held, chosen, rows, gates, ups, ready, sent = refs[count + 6 :]
    step = pl.program_id(0)
    tiles = pl.num_programs(0) // rows.shape[0]
    fetching = ((w_gate, w_up), (gates, ups), ready)
    copy = pltpu.make_async_copy(rows, rows_out, sent)

    @pl.when(step == 0)
    def _():
        for first in weight_tiles(step, *fetching):
            first.start()
        dispatch(pieces, slot, held, chosen, rows)
        copy.start()

    next_tiles(step, *fetching)
    x = rows[step // tiles]
    gate = dot(x, gates[step % 2])
    up = dot(x, ups[step % 2])
    sig = jax.nn.sigmoid(gate)
    act[0] = gate * sig
    slope[0] = up * sig * (1.0 + gate * (1.0 - sig))

    @pl.when(step == pl.num_programs(0) - 1)
    def _():
        copy.wait()


def forward(pieces, slot, w_gate, w_up):
    experts, blocks, tokens = slot.shape
    _, features, units = w_gate.shape
    tile = min(UNIT_TILE, units)
    tiles = units // tile
    slots = blocks * MOST
    unit = pl.BlockSpec((1, slots, tile), lambda i: (i // tiles, 0, i % tiles))
    return pl.pallas_call(
        functools.partial(forward_kernel, len(pieces)),
        grid=(experts * tiles,),
        in_specs=[whole(p.shape) for p in pieces]
        + [whole(slot.shape)]
        + [pl.BlockSpec(memory_space=pl.ANY)] * 2,
        out_specs=[pl.BlockSpec(memory_space=pltpu.HBM), unit, unit],
        out_shape=[
            jax.ShapeDtypeStruct((experts, slots, features), BF16),
            jax.ShapeDtypeStruct((experts, slots, units), F32),
            jax.ShapeDtypeStruct((experts, slots, units), F32),
        ],
        scratch_shapes=dispatch_scratch(experts, blocks, tokens, features)
        + [pltpu.VMEM((2, features, tile), BF16)] * 2
        + [pltpu.SemaphoreType.DMA((2, 2)), pltpu.SemaphoreType.DMA],
        compiler_params=params(1, 52),
        cost_estimate=pl.CostEstimate(
            flops=4 * experts * slots * features * units,
            bytes_accessed=4 * experts * features * units,
            transcendentals=experts * slots * units,
        ),
    )(*pieces, slot, w_gate, w_up)


def hidden_kernel(count, *refs):
    pieces, (slot, weight, act, slope, w_down) = refs[:count], refs[count : count + 5]
    gate_grad, up_grad, held, chosen, grads, downs, ready = refs[count + 5 :]
    step = pl.program_id(0)
    tiles = pl.num_programs(0) // grads.shape[0]
    fetching = ((w_down,), (downs,), ready)

    @pl.when(step == 0)
    def _():
        for first in weight_tiles(step, *fetching):
            first.start()
        dispatch(pieces, slot, held, chosen, grads, weight)

    next_tiles(step, *fetching)
    hidden = dot(grads[step // tiles], downs[step % 2])
    up_grad[0] = (hidden * act[0]).astype(BF16)
    gate_grad[0] = (hidden * slope[0]).astype(BF16)


def hidden_grads(pieces, slot, weight, act, slope, w_down):
    experts, blocks, tokens = slot.shape
    _, features, units = w_down.shape
    tile = min(UNIT_TILE, units)
    tiles = units // tile
    slots = blocks * MOST
    unit = pl.BlockSpec((1, slots, tile), lambda i: (i // tiles, 0, i % tiles))
    return pl.pallas_call(
        functools.partial(hidden_kernel, len(pieces)),
        grid=(experts * tiles,),
        in_specs=[whole(p.shape) for p in pieces]
        + [whole(slot.shape), whole(slot.shape), unit, unit, pl.BlockSpec(memory_space=pl.ANY)],
        out_specs=[unit, unit],
        out_shape=[jax.ShapeDtypeStruct((experts, slots, units), BF16)] * 2,
        scratch_shapes=dispatch_scratch(experts, blocks, tokens, features)
        + [pltpu.VMEM((2, features, tile), BF16), pltpu.SemaphoreType.DMA((2, 1))],
        compiler_params=params(1, 48),
        cost_estimate=pl.CostEstimate(
            flops=2 * experts * slots * features * units,
            bytes_accessed=2 * experts * features * units,
            transcendentals=0,
        ),
    )(*pieces, slot, weight, act, slope, w_down)


def inputs_kernel(groups, back, gate_grad, up_grad, w_gate, w_up, *refs):
    sums, held = refs[:-1], refs[-1]
    blocks, tokens, _ = back.shape
    for l in range(gate_grad.shape[0]):
        partial = dot(gate_grad[l], w_gate[l], NT) + dot(up_grad[l], w_up[l], NT)
        for b in range(blocks):
            held[b, l * MOST : (l + 1) * MOST] = partial[b * MOST : (b + 1) * MOST].astype(BF16)
    for out, members in zip(sums, groups):
        for place, b in enumerate(members):
            out[place * tokens : (place + 1) * tokens] = dot(back[b], held[b]).astype(BF16)


def input_sums(back, gate_grad, up_grad, w_gate, w_up, groups, part, parts):
    blocks, tokens, _ = back.shape
    experts, features, units = w_gate.shape
    wide = FEATURE_TILE
    steps = features // parts // wide
    slots = blocks * MOST
    across = pl.BlockSpec((experts, wide, units), lambda i: (0, part * steps + i, 0))
    return pl.pallas_call(
        functools.partial(inputs_kernel, groups),
        grid=(steps,),
        in_specs=[whole(back.shape), whole(gate_grad.shape), whole(up_grad.shape), across, across],
        out_specs=[pl.BlockSpec((len(g) * tokens, wide), lambda i: (0, i)) for g in groups],
        out_shape=[
            jax.ShapeDtypeStruct((len(g) * tokens, features // parts), BF16) for g in groups
        ],
        scratch_shapes=[pltpu.VMEM((blocks, experts * MOST, wide), BF16)],
        compiler_params=params(1, 40),
        cost_estimate=pl.CostEstimate(
            flops=4 * experts * slots * features * units // parts,
            bytes_accessed=4 * experts * features * units // parts,
            transcendentals=0,
        ),
    )(back, gate_grad, up_grad, w_gate, w_up)


def back_matrix(slot):
    places = jnp.arange(MOST, dtype=F32)
    slot = lax.optimization_barrier(slot.transpose(1, 2, 0))
    parts = [slot[..., l : l + 1] == places for l in range(slot.shape[2])]
    return jnp.concatenate([p.astype(BF16) for p in parts], axis=2)


def weights_kernel(rows, gate_grad, up_grad, *refs):
    grad_gate, grad_up = refs[-2:]
    grad_gate[0] = dot(rows[0], gate_grad[0], TN)
    grad_up[0] = dot(rows[0], up_grad[0], TN)


def weight_grads(rows, gate_grad, up_grad, before, first, steps):
    experts, slots, features = rows.shape
    units = gate_grad.shape[2]
    wide = FEATURE_TILE
    each = features // wide
    unit = pl.BlockSpec((1, slots, units), lambda i: ((first + i) // each, 0, 0))
    out = pl.BlockSpec((1, wide, units), lambda i: ((first + i) // each, (first + i) % each, 0))
    kept = [] if before is None else list(before)
    return pl.pallas_call(
        weights_kernel,
        grid=(steps,),
        in_specs=[
            pl.BlockSpec((1, slots, wide), lambda i: ((first + i) // each, 0, (first + i) % each)),
            unit,
            unit,
        ]
        + [pl.BlockSpec(memory_space=pl.ANY)] * len(kept),
        out_specs=[out, out],
        out_shape=[jax.ShapeDtypeStruct((experts, features, units), F32)] * 2,
        input_output_aliases={3 + i: i for i in range(len(kept))},
        compiler_params=params(1, 30),
        cost_estimate=pl.CostEstimate(
            flops=4 * slots * steps * wide * units,
            bytes_accessed=8 * steps * wide * units,
            transcendentals=0,
        ),
    )(rows, gate_grad, up_grad, *kept)


def route_table(routes, gate_values):
    tokens = routes.shape[0]
    experts = jnp.arange(EXPERTS, dtype=jnp.int32)[:, None, None]
    match = routes.T[None] == experts
    member = jnp.any(match, axis=1)
    gate = jnp.sum(jnp.where(match, gate_values.T[None], 0.0), axis=1)
    place = jnp.arange(tokens, dtype=jnp.int32)
    earlier = (place[:, None] < place[None, :]).astype(BF16)
    slot = jnp.where(member, dot(member.astype(BF16), earlier), -1.0)
    return jnp.stack([slot, gate], axis=1)


def flip(value, axis, bit):
    count = lax.axis_size(axis)
    return lax.ppermute(value, axis, [(i, i ^ bit) for i in range(count)])


def swap_order(value, side, pair, dim):
    shape = value.shape
    value = value.reshape(shape[:dim] + (2, 2, shape[dim] // 4) + shape[dim + 1 :])
    value = jnp.where(side == 1, jnp.flip(value, dim), value)
    return jnp.where(pair == 1, jnp.flip(value, dim + 1), value).reshape(shape)


def add(*terms):
    total = terms[0].astype(F32)
    for term in terms[1:]:
        total = total + term.astype(F32)
    return total.astype(BF16)


def quarters(value, count, at):
    return lax.dynamic_slice_in_dim(value, at * (count // 4), count // 4, 0)


def local_near(out_grad, routes, gate_values, layer_input, w_gate, w_up, w_down):
    experts, features, _ = w_gate.shape
    me = lax.axis_index("expert")
    position = lax.axis_index("dp")
    side, pair = position % 2, position // 2 % 2
    tokens = out_grad.shape[0]
    half, quarter = tokens // 2, tokens // 4
    corner = side * 2 + pair

    def to_core(values):
        return tuple(flip(v, "expert", 1) for v in values)

    x_mine = [quarters(layer_input, tokens, q) for q in (corner, 3 - corner)]
    *x_mine, layer_input, out_grad, routes = lax.optimization_barrier(
        (*x_mine, layer_input, out_grad, routes)
    )
    x_across, x_corner = [flip(v, "expert", 2) for v in x_mine]
    x_sibling, g_sibling = to_core((layer_input, out_grad))
    x_sibling, routes = lax.optimization_barrier((x_sibling, routes))
    table = route_table(routes, gate_values)
    tables = []
    for r in range(4):
        part = lax.dynamic_slice_in_dim(table, (me ^ r) * experts, experts, 0)
        tables.append(flip(part, "expert", r) if r > 0 else part)
    x_corner, g_own = lax.optimization_barrier((x_corner, out_grad))
    x_far = (x_across, x_corner, flip(x_across, "dp", 1), flip(x_across, "dp", 2))
    g_across = flip(g_own, "expert", 2)
    x_far = (*x_far, *to_core(x_far))
    table = jnp.stack(tables, axis=2)
    slot, weight = table[:, 0], table[:, 1]
    back = back_matrix(swap_order(slot, side, pair, 2))
    far = swap_order(slot[:, 2:], side, pair, 2).reshape(experts, 2, 4, quarter)
    far = jnp.stack([far[:, :, q] for q in (0, 3, 2, 1)], axis=2).reshape(experts, 2, tokens)
    slot_x = jnp.concatenate([slot[:, :2], far], axis=1)
    slot_x, back = lax.optimization_barrier((slot_x, back))
    rows, act, slope = forward((layer_input, x_sibling, *x_far), slot_x, w_gate, w_up)
    act, g_across = lax.optimization_barrier((act, g_across))
    gate_grad, up_grad = hidden_grads(
        (out_grad, g_sibling, g_across, *to_core((g_across,))), slot, weight, act, slope, w_down
    )

    groups = ((0, 2), (1, 3))
    kept_a, sent_a = input_sums(back, gate_grad, up_grad, w_gate, w_up, groups, 0, 2)
    kept_b, sent_b = input_sums(back, gate_grad, up_grad, w_gate, w_up, groups, 1, 2)

    def piece(after, before, *which):
        held, rows_now = lax.optimization_barrier((after, rows))
        return held, weight_grads(rows_now, gate_grad, up_grad, before, *which)

    def corners(value):
        z, x, diagonal = value
        x, diagonal = flip(x, "dp", 1), flip(diagonal, "dp", 3)
        return [flip(z, "dp", 2), x, diagonal]

    def cut(value, count):
        return [value[i : i + quarter] for i in range(0, count * quarter, quarter)]

    chip_a = add(kept_a, flip(sent_a, "expert", 1))
    got = flip(sent_b, "expert", 1)
    chip_b = [add(a, b) for a, b in zip(cut(kept_b, 8), cut(got, 8))]
    far_a = chip_a[tokens:]
    away = [jnp.concatenate([chip_b[q], chip_b[4 + q]], axis=0) for q in (1, 2, 3)]
    (far_a, *away), grads = piece((far_a, *away), None, 0, 3)
    got_x = flip(away[1], "dp", 1)
    got_a = flip(far_a, "expert", 2)
    got_b = [flip(away[2], "dp", 3), flip(away[0], "dp", 2), got_x]
    got_a, got_b, *grads = lax.optimization_barrier((got_a, got_b, *grads))
    own_a = [add(a, b) for a, b in zip(cut(chip_a, 4), cut(got_a, 4))]
    mine_b = add(chip_b[0], *(v[:quarter] for v in got_b))
    far_b = add(chip_b[4], *(v[quarter:] for v in got_b))
    (far_b, *own_a), grads = piece((far_b, *own_a), grads, 3, 2)
    got_a, got_b = corners(own_a[1:]), flip(far_b, "expert", 2)
    got_a, got_b, *grads = lax.optimization_barrier((got_a, got_b, *grads))
    mine = jnp.concatenate([add(own_a[0], *got_a), add(mine_b, got_b)], axis=1)
    mine, grads = piece(mine, grads, 5, 4)
    got = flip(mine, "dp", 4)
    got, *grads = lax.optimization_barrier((got, *grads))
    mine = add(mine, got)
    mine, grads = piece(mine, grads, 9, 3)
    got = corners([mine] * 3)
    got, *grads = lax.optimization_barrier((got, *grads))
    total = swap_order(jnp.concatenate([mine, *got], axis=0), side, pair, 0)
    return (total, *grads)


def local_any(out_grad, routes, gate_values, layer_input, w_gate, w_up, w_down):
    experts = w_gate.shape[0]
    me = lax.axis_index("expert")
    rows_in = lax.all_gather(layer_input, "expert", tiled=True)
    grads_in = lax.all_gather(out_grad, "expert", tiled=True)
    table = lax.all_gather(route_table(routes, gate_values), "expert")
    table = lax.dynamic_slice_in_dim(table, me * experts, experts, 1).transpose(1, 2, 0, 3)
    slot, weight = table[:, 0], table[:, 1]
    rows, act, slope = forward([rows_in], slot, w_gate, w_up)
    gate_grad, up_grad = hidden_grads([grads_in], slot, weight, act, slope, w_down)
    groups = (tuple(range(slot.shape[1])),)
    (sums,) = input_sums(back_matrix(slot), gate_grad, up_grad, w_gate, w_up, groups, 0, 1)
    blocks = experts * layer_input.shape[1] // FEATURE_TILE
    grads = weight_grads(rows, gate_grad, up_grad, None, 0, blocks)
    own = lax.psum_scatter(sums, "expert", scatter_dimension=0, tiled=True)
    return (lax.psum(own, "dp"), *grads)


def solution(mesh):
    near = mesh.shape["dp"] == 8 and mesh.shape["expert"] == 4
    placed = (
        P("expert", None),
        P("expert", None),
        P("expert", None),
        P("expert", None),
        P("expert", None, "dp"),
        P("expert", None, "dp"),
        P("expert", None, "dp"),
    )
    return jax.shard_map(
        local_near if near else local_any,
        mesh=mesh,
        in_specs=placed,
        out_specs=(P("expert", None), P("expert", None, "dp"), P("expert", None, "dp")),
        check_vma=False,
    )
```

```python
import functools

import jax
import jax.numpy as jnp
from jax import lax
from jax.experimental import pallas as pl
from jax.experimental.pallas import tpu as pltpu
from jax.sharding import PartitionSpec as P

EXPERTS = 8
MOST = 80
UNIT_TILE = 512
FEATURE_TILE = 512
BF16 = jnp.bfloat16
F32 = jnp.float32
NN = (((1,), (0,)), ((), ()))
NT = (((1,), (1,)), ((), ()))
TN = (((0,), (0,)), ((), ()))


def dot(a, b, dims=NN):
    return lax.dot_general(a, b, dims, preferred_element_type=F32)


def params(count, mebibytes):
    return pltpu.CompilerParams(
        dimension_semantics=("arbitrary",) * count, vmem_limit_bytes=mebibytes * 1024 * 1024
    )


def whole(shape):
    return pl.BlockSpec(
        shape, lambda *_: (0,) * len(shape), pipeline_mode=pl.Buffered(buffer_count=1)
    )


def one_hot(slot_row):
    slots = lax.broadcasted_iota(jnp.int32, (MOST, slot_row.shape[1]), 0)
    return slots == slot_row.astype(jnp.int32)


def lay_out(held, pieces, first):
    rows, at = held.shape[0], 0
    for piece in pieces:
        low, high = max(first, at), min(first + rows, at + piece.shape[0])
        if low < high:
            held[low - first : high - first] = piece[low - at : high - at]
        at += piece.shape[0]


def column_chunks(features):
    step = 768 if features % 768 == 0 else features
    return [slice(c, c + step) for c in range(0, features, step)]


def dispatch(pieces, slot, held, chosen, out, weight=None):
    experts, blocks, tokens = slot.shape
    group = held.shape[0] // tokens
    places = [(l, b) for l in range(experts) for b in range(group)]
    for start in range(0, blocks, group):
        chosen[...] = jnp.zeros_like(chosen)
        scales = []
        for i, (l, b) in enumerate(places):
            at = slice(start + b, start + b + 1)
            mask = one_hot(slot[l, at, :])
            chosen[i * MOST : (i + 1) * MOST, b * tokens : (b + 1) * tokens] = mask.astype(BF16)
            if weight is not None:
                scales.append(
                    jnp.sum(jnp.where(mask, weight[l, at, :], 0.0), axis=1, keepdims=True)
                )
        lay_out(held, pieces, start * tokens)
        for cols in column_chunks(held.shape[1]):
            taken = dot(chosen[...], held[:, cols])
            for i, (l, b) in enumerate(places):
                part = taken[i * MOST : (i + 1) * MOST]
                if scales:
                    part = part * scales[i]
                span = slice((start + b) * MOST, (start + b + 1) * MOST)
                out[l, span, cols] = part.astype(BF16)


def dispatch_scratch(experts, blocks, tokens, features):
    group = 2 if blocks % 2 == 0 else 1
    return [
        pltpu.VMEM((group * tokens, features), BF16),
        pltpu.VMEM((experts * group * MOST, group * tokens), BF16),
        pltpu.VMEM((experts, blocks * MOST, features), BF16),
    ]


def weight_tiles(step, matrices, buffers, ready):
    _, features, tile = buffers[0].shape
    tiles = matrices[0].shape[2] // tile
    cols = pl.ds(pl.multiple_of(step % tiles * tile, tile), tile)
    return [
        pltpu.make_async_copy(
            matrix.at[step // tiles, :, cols], buffer.at[step % 2], ready.at[step % 2, i]
        )
        for i, (matrix, buffer) in enumerate(zip(matrices, buffers))
    ]


def next_tiles(step, matrices, buffers, ready):
    @pl.when(step + 1 < pl.num_programs(0))
    def _():
        for copy in weight_tiles(step + 1, matrices, buffers, ready):
            copy.start()

    for copy in weight_tiles(step, matrices, buffers, ready):
        copy.wait()


def forward_kernel(count, *refs):
    pieces, (slot, w_gate, w_up, rows_out, act, slope) = refs[:count], refs[count : count + 6]
    held, chosen, rows, sent = refs[count + 6 :]
    expert, tile = pl.program_id(0), pl.program_id(1)
    copy = pltpu.make_async_copy(rows, rows_out, sent)

    @pl.when((expert == 0) & (tile == 0))
    def _():
        dispatch(pieces, slot, held, chosen, rows)
        copy.start()

    x = rows[expert]
    gate = dot(x, w_gate[0])
    up = dot(x, w_up[0])
    sig = jax.nn.sigmoid(gate)
    act[0] = gate * sig
    slope[0] = up * sig * (1.0 + gate * (1.0 - sig))

    @pl.when((expert == pl.num_programs(0) - 1) & (tile == pl.num_programs(1) - 1))
    def _():
        copy.wait()


def forward(pieces, slot, w_gate, w_up):
    experts, blocks, tokens = slot.shape
    _, features, units = w_gate.shape
    tile = min(UNIT_TILE, units)
    slots = blocks * MOST
    matrix = pl.BlockSpec((1, features, tile), lambda l, f: (l, 0, f))
    unit = pl.BlockSpec((1, slots, tile), lambda l, f: (l, 0, f))
    return pl.pallas_call(
        functools.partial(forward_kernel, len(pieces)),
        grid=(experts, units // tile),
        in_specs=[whole(p.shape) for p in pieces] + [whole(slot.shape), matrix, matrix],
        out_specs=[pl.BlockSpec(memory_space=pltpu.HBM), unit, unit],
        out_shape=[
            jax.ShapeDtypeStruct((experts, slots, features), BF16),
            jax.ShapeDtypeStruct((experts, slots, units), F32),
            jax.ShapeDtypeStruct((experts, slots, units), F32),
        ],
        scratch_shapes=dispatch_scratch(experts, blocks, tokens, features)
        + [pltpu.SemaphoreType.DMA],
        compiler_params=params(2, 52),
        cost_estimate=pl.CostEstimate(
            flops=4 * experts * slots * features * units,
            bytes_accessed=4 * experts * features * units,
            transcendentals=experts * slots * units,
        ),
    )(*pieces, slot, w_gate, w_up)


def hidden_kernel(count, *refs):
    pieces, (slot, weight, act, slope, w_down) = refs[:count], refs[count : count + 5]
    gate_grad, up_grad, held, chosen, grads, downs, ready = refs[count + 5 :]
    step = pl.program_id(0)
    tiles = pl.num_programs(0) // grads.shape[0]
    fetching = ((w_down,), (downs,), ready)

    @pl.when(step == 0)
    def _():
        for first in weight_tiles(step, *fetching):
            first.start()
        dispatch(pieces, slot, held, chosen, grads, weight)

    next_tiles(step, *fetching)
    hidden = dot(grads[step // tiles], downs[step % 2])
    up_grad[0] = (hidden * act[0]).astype(BF16)
    gate_grad[0] = (hidden * slope[0]).astype(BF16)


def hidden_grads(pieces, slot, weight, act, slope, w_down):
    experts, blocks, tokens = slot.shape
    _, features, units = w_down.shape
    tile = min(UNIT_TILE, units)
    tiles = units // tile
    slots = blocks * MOST
    unit = pl.BlockSpec((1, slots, tile), lambda i: (i // tiles, 0, i % tiles))
    return pl.pallas_call(
        functools.partial(hidden_kernel, len(pieces)),
        grid=(experts * tiles,),
        in_specs=[whole(p.shape) for p in pieces]
        + [whole(slot.shape), whole(slot.shape), unit, unit, pl.BlockSpec(memory_space=pl.ANY)],
        out_specs=[unit, unit],
        out_shape=[jax.ShapeDtypeStruct((experts, slots, units), BF16)] * 2,
        scratch_shapes=dispatch_scratch(experts, blocks, tokens, features)
        + [pltpu.VMEM((2, features, tile), BF16), pltpu.SemaphoreType.DMA((2, 1))],
        compiler_params=params(1, 48),
        cost_estimate=pl.CostEstimate(
            flops=2 * experts * slots * features * units,
            bytes_accessed=2 * experts * features * units,
            transcendentals=0,
        ),
    )(*pieces, slot, weight, act, slope, w_down)


def inputs_kernel(groups, back, gate_grad, up_grad, w_gate, w_up, *refs):
    sums, held = refs[:-1], refs[-1]
    blocks, tokens, _ = back.shape
    for l in range(gate_grad.shape[0]):
        partial = dot(gate_grad[l], w_gate[l], NT) + dot(up_grad[l], w_up[l], NT)
        for b in range(blocks):
            held[b, l * MOST : (l + 1) * MOST] = partial[b * MOST : (b + 1) * MOST].astype(BF16)
    for out, members in zip(sums, groups):
        for place, b in enumerate(members):
            out[place * tokens : (place + 1) * tokens] = dot(back[b], held[b]).astype(BF16)


def input_sums(back, gate_grad, up_grad, w_gate, w_up, groups, part, parts):
    blocks, tokens, _ = back.shape
    experts, features, units = w_gate.shape
    wide = FEATURE_TILE
    steps = features // parts // wide
    slots = blocks * MOST
    across = pl.BlockSpec((experts, wide, units), lambda i: (0, part * steps + i, 0))
    return pl.pallas_call(
        functools.partial(inputs_kernel, groups),
        grid=(steps,),
        in_specs=[whole(back.shape), whole(gate_grad.shape), whole(up_grad.shape), across, across],
        out_specs=[pl.BlockSpec((len(g) * tokens, wide), lambda i: (0, i)) for g in groups],
        out_shape=[
            jax.ShapeDtypeStruct((len(g) * tokens, features // parts), BF16) for g in groups
        ],
        scratch_shapes=[pltpu.VMEM((blocks, experts * MOST, wide), BF16)],
        compiler_params=params(1, 40),
        cost_estimate=pl.CostEstimate(
            flops=4 * experts * slots * features * units // parts,
            bytes_accessed=4 * experts * features * units // parts,
            transcendentals=0,
        ),
    )(back, gate_grad, up_grad, w_gate, w_up)


def back_matrix(slot):
    places = jnp.arange(MOST, dtype=F32)
    slot = lax.optimization_barrier(slot.transpose(1, 2, 0))
    parts = [slot[..., l : l + 1] == places for l in range(slot.shape[2])]
    return jnp.concatenate([p.astype(BF16) for p in parts], axis=2)


def weights_kernel(rows, gate_grad, up_grad, *refs):
    grad_gate, grad_up = refs[-2:]
    grad_gate[0] = dot(rows[0], gate_grad[0], TN)
    grad_up[0] = dot(rows[0], up_grad[0], TN)


def weight_grads(rows, gate_grad, up_grad, before, first, steps):
    experts, slots, features = rows.shape
    units = gate_grad.shape[2]
    wide = FEATURE_TILE
    each = features // wide
    unit = pl.BlockSpec((1, slots, units), lambda i: ((first + i) // each, 0, 0))
    out = pl.BlockSpec((1, wide, units), lambda i: ((first + i) // each, (first + i) % each, 0))
    kept = [] if before is None else list(before)
    return pl.pallas_call(
        weights_kernel,
        grid=(steps,),
        in_specs=[
            pl.BlockSpec((1, slots, wide), lambda i: ((first + i) // each, 0, (first + i) % each)),
            unit,
            unit,
        ]
        + [pl.BlockSpec(memory_space=pl.ANY)] * len(kept),
        out_specs=[out, out],
        out_shape=[jax.ShapeDtypeStruct((experts, features, units), F32)] * 2,
        input_output_aliases={3 + i: i for i in range(len(kept))},
        compiler_params=params(1, 30),
        cost_estimate=pl.CostEstimate(
            flops=4 * slots * steps * wide * units,
            bytes_accessed=8 * steps * wide * units,
            transcendentals=0,
        ),
    )(rows, gate_grad, up_grad, *kept)


def route_table(routes, gate_values):
    tokens = routes.shape[0]
    experts = jnp.arange(EXPERTS, dtype=jnp.int32)[:, None, None]
    match = routes.T[None] == experts
    member = jnp.any(match, axis=1)
    gate = jnp.sum(jnp.where(match, gate_values.T[None], 0.0), axis=1)
    place = jnp.arange(tokens, dtype=jnp.int32)
    earlier = (place[:, None] < place[None, :]).astype(BF16)
    slot = jnp.where(member, dot(member.astype(BF16), earlier), -1.0)
    return jnp.stack([slot, gate], axis=1)


def flip(value, axis, bit):
    count = lax.axis_size(axis)
    return lax.ppermute(value, axis, [(i, i ^ bit) for i in range(count)])


def swap_order(value, side, pair, dim):
    shape = value.shape
    value = value.reshape(shape[:dim] + (2, 2, shape[dim] // 4) + shape[dim + 1 :])
    value = jnp.where(side == 1, jnp.flip(value, dim), value)
    return jnp.where(pair == 1, jnp.flip(value, dim + 1), value).reshape(shape)


def add(*terms):
    total = terms[0].astype(F32)
    for term in terms[1:]:
        total = total + term.astype(F32)
    return total.astype(BF16)


def quarters(value, count, at):
    return lax.dynamic_slice_in_dim(value, at * (count // 4), count // 4, 0)


def local_near(out_grad, routes, gate_values, layer_input, w_gate, w_up, w_down):
    experts, features, _ = w_gate.shape
    me = lax.axis_index("expert")
    position = lax.axis_index("dp")
    side, pair = position % 2, position // 2 % 2
    tokens = out_grad.shape[0]
    half, quarter = tokens // 2, tokens // 4
    corner = side * 2 + pair

    def to_core(values):
        return tuple(flip(v, "expert", 1) for v in values)

    x_mine = [quarters(layer_input, tokens, q) for q in (corner, 3 - corner)]
    *x_mine, layer_input, out_grad, routes = lax.optimization_barrier(
        (*x_mine, layer_input, out_grad, routes)
    )
    x_across, x_corner = [flip(v, "expert", 2) for v in x_mine]
    x_sibling, g_sibling = to_core((layer_input, out_grad))
    x_sibling, routes = lax.optimization_barrier((x_sibling, routes))
    table = route_table(routes, gate_values)
    tables = []
    for r in range(4):
        part = lax.dynamic_slice_in_dim(table, (me ^ r) * experts, experts, 0)
        tables.append(flip(part, "expert", r) if r > 0 else part)
    x_corner, g_own = lax.optimization_barrier((x_corner, out_grad))
    x_far = (x_across, x_corner, flip(x_across, "dp", 1), flip(x_across, "dp", 2))
    g_across = flip(g_own, "expert", 2)
    x_far = (*x_far, *to_core(x_far))
    table = jnp.stack(tables, axis=2)
    slot, weight = table[:, 0], table[:, 1]
    back = back_matrix(swap_order(slot, side, pair, 2))
    far = swap_order(slot[:, 2:], side, pair, 2).reshape(experts, 2, 4, quarter)
    far = jnp.stack([far[:, :, q] for q in (0, 3, 2, 1)], axis=2).reshape(experts, 2, tokens)
    slot_x = jnp.concatenate([slot[:, :2], far], axis=1)
    rows, act, slope = forward((layer_input, x_sibling, *x_far), slot_x, w_gate, w_up)
    act, g_across = lax.optimization_barrier((act, g_across))
    gate_grad, up_grad = hidden_grads(
        (out_grad, g_sibling, g_across, *to_core((g_across,))), slot, weight, act, slope, w_down
    )

    groups = ((0, 2), (1, 3))
    kept_a, sent_a = input_sums(back, gate_grad, up_grad, w_gate, w_up, groups, 0, 2)
    kept_b, sent_b = input_sums(back, gate_grad, up_grad, w_gate, w_up, groups, 1, 2)

    def piece(after, before, *which):
        held, rows_now = lax.optimization_barrier((after, rows))
        return held, weight_grads(rows_now, gate_grad, up_grad, before, *which)

    def corners(value):
        z, x, diagonal = value
        x, diagonal = flip(x, "dp", 1), flip(diagonal, "dp", 3)
        return [flip(z, "dp", 2), x, diagonal]

    def cut(value, count):
        return [value[i : i + quarter] for i in range(0, count * quarter, quarter)]

    chip_a = add(kept_a, flip(sent_a, "expert", 1))
    got = flip(sent_b, "expert", 1)
    chip_b = [add(a, b) for a, b in zip(cut(kept_b, 8), cut(got, 8))]
    far_a = chip_a[tokens:]
    away = [jnp.concatenate([chip_b[q], chip_b[4 + q]], axis=0) for q in (1, 2, 3)]
    (far_a, *away), grads = piece((far_a, *away), None, 0, 4)
    got_x = flip(away[1], "dp", 1)
    got_a = flip(far_a, "expert", 2)
    got_b = [flip(away[2], "dp", 3), flip(away[0], "dp", 2), got_x]
    got_a, got_b, *grads = lax.optimization_barrier((got_a, got_b, *grads))
    own_a = [add(a, b) for a, b in zip(cut(chip_a, 4), cut(got_a, 4))]
    mine_b = add(chip_b[0], *(v[:quarter] for v in got_b))
    far_b = add(chip_b[4], *(v[quarter:] for v in got_b))
    (far_b, *own_a), grads = piece((far_b, *own_a), grads, 4, 1)
    got_a, got_b = corners(own_a[1:]), flip(far_b, "expert", 2)
    got_a, got_b, *grads = lax.optimization_barrier((got_a, got_b, *grads))
    mine = jnp.concatenate([add(own_a[0], *got_a), add(mine_b, got_b)], axis=1)
    mine, grads = piece(mine, grads, 5, 4)
    got = flip(mine, "dp", 4)
    got, *grads = lax.optimization_barrier((got, *grads))
    mine = add(mine, got)
    mine, grads = piece(mine, grads, 9, 3)
    got = corners([mine] * 3)
    got, *grads = lax.optimization_barrier((got, *grads))
    total = swap_order(jnp.concatenate([mine, *got], axis=0), side, pair, 0)
    return (total, *grads)


def local_any(out_grad, routes, gate_values, layer_input, w_gate, w_up, w_down):
    experts = w_gate.shape[0]
    me = lax.axis_index("expert")
    rows_in = lax.all_gather(layer_input, "expert", tiled=True)
    grads_in = lax.all_gather(out_grad, "expert", tiled=True)
    table = lax.all_gather(route_table(routes, gate_values), "expert")
    table = lax.dynamic_slice_in_dim(table, me * experts, experts, 1).transpose(1, 2, 0, 3)
    slot, weight = table[:, 0], table[:, 1]
    rows, act, slope = forward([rows_in], slot, w_gate, w_up)
    gate_grad, up_grad = hidden_grads([grads_in], slot, weight, act, slope, w_down)
    groups = (tuple(range(slot.shape[1])),)
    (sums,) = input_sums(back_matrix(slot), gate_grad, up_grad, w_gate, w_up, groups, 0, 1)
    blocks = experts * layer_input.shape[1] // FEATURE_TILE
    grads = weight_grads(rows, gate_grad, up_grad, None, 0, blocks)
    own = lax.psum_scatter(sums, "expert", scatter_dimension=0, tiled=True)
    return (lax.psum(own, "dp"), *grads)


def solution(mesh):
    near = mesh.shape["dp"] == 8 and mesh.shape["expert"] == 4
    placed = (
        P("expert", None),
        P("expert", None),
        P("expert", None),
        P("expert", None),
        P("expert", None, "dp"),
        P("expert", None, "dp"),
        P("expert", None, "dp"),
    )
    return jax.shard_map(
        local_near if near else local_any,
        mesh=mesh,
        in_specs=placed,
        out_specs=(P("expert", None), P("expert", None, "dp"), P("expert", None, "dp")),
        check_vma=False,
    )
```

```python
import functools

import jax
import jax.numpy as jnp
from jax import lax
from jax.experimental import pallas as pl
from jax.experimental.pallas import tpu as pltpu
from jax.sharding import PartitionSpec as P

EXPERTS = 8
MOST = 80
UNIT_TILE = 512
FEATURE_TILE = 512
BF16 = jnp.bfloat16
F32 = jnp.float32
NN = (((1,), (0,)), ((), ()))
NT = (((1,), (1,)), ((), ()))
TN = (((0,), (0,)), ((), ()))


def dot(a, b, dims=NN):
    return lax.dot_general(a, b, dims, preferred_element_type=F32)


def params(count, mebibytes):
    return pltpu.CompilerParams(
        dimension_semantics=("arbitrary",) * count, vmem_limit_bytes=mebibytes * 1024 * 1024
    )


def whole(shape):
    return pl.BlockSpec(
        shape, lambda *_: (0,) * len(shape), pipeline_mode=pl.Buffered(buffer_count=1)
    )


def one_hot(slot_row):
    slots = lax.broadcasted_iota(jnp.int32, (MOST, slot_row.shape[1]), 0)
    return slots == slot_row.astype(jnp.int32)


def lay_out(held, pieces, first):
    rows, at = held.shape[0], 0
    for piece in pieces:
        low, high = max(first, at), min(first + rows, at + piece.shape[0])
        if low < high:
            held[low - first : high - first] = piece[low - at : high - at]
        at += piece.shape[0]


def column_chunks(features):
    step = 768 if features % 768 == 0 else features
    return [slice(c, c + step) for c in range(0, features, step)]


def dispatch(pieces, slot, held, chosen, out, weight=None):
    experts, blocks, tokens = slot.shape
    group = held.shape[0] // tokens
    places = [(l, b) for l in range(experts) for b in range(group)]
    for start in range(0, blocks, group):
        chosen[...] = jnp.zeros_like(chosen)
        scales = []
        for i, (l, b) in enumerate(places):
            at = slice(start + b, start + b + 1)
            mask = one_hot(slot[l, at, :])
            chosen[i * MOST : (i + 1) * MOST, b * tokens : (b + 1) * tokens] = mask.astype(BF16)
            if weight is not None:
                scales.append(
                    jnp.sum(jnp.where(mask, weight[l, at, :], 0.0), axis=1, keepdims=True)
                )
        lay_out(held, pieces, start * tokens)
        for cols in column_chunks(held.shape[1]):
            taken = dot(chosen[...], held[:, cols])
            for i, (l, b) in enumerate(places):
                part = taken[i * MOST : (i + 1) * MOST]
                if scales:
                    part = part * scales[i]
                span = slice((start + b) * MOST, (start + b + 1) * MOST)
                out[l, span, cols] = part.astype(BF16)


def dispatch_scratch(experts, blocks, tokens, features):
    group = 2 if blocks % 2 == 0 else 1
    return [
        pltpu.VMEM((group * tokens, features), BF16),
        pltpu.VMEM((experts * group * MOST, group * tokens), BF16),
        pltpu.VMEM((experts, blocks * MOST, features), BF16),
    ]


def weight_tiles(step, matrices, buffers, ready):
    _, features, tile = buffers[0].shape
    tiles = matrices[0].shape[2] // tile
    cols = pl.ds(pl.multiple_of(step % tiles * tile, tile), tile)
    return [
        pltpu.make_async_copy(
            matrix.at[step // tiles, :, cols], buffer.at[step % 2], ready.at[step % 2, i]
        )
        for i, (matrix, buffer) in enumerate(zip(matrices, buffers))
    ]


def next_tiles(step, matrices, buffers, ready):
    @pl.when(step + 1 < pl.num_programs(0))
    def _():
        for copy in weight_tiles(step + 1, matrices, buffers, ready):
            copy.start()

    for copy in weight_tiles(step, matrices, buffers, ready):
        copy.wait()


def forward_kernel(count, *refs):
    pieces, (slot, w_gate, w_up, rows_out, act, slope) = refs[:count], refs[count : count + 6]
    held, chosen, rows, sent = refs[count + 6 :]
    expert, tile = pl.program_id(0), pl.program_id(1)
    copy = pltpu.make_async_copy(rows, rows_out, sent)

    @pl.when((expert == 0) & (tile == 0))
    def _():
        dispatch(pieces, slot, held, chosen, rows)
        copy.start()

    x = rows[expert]
    gate = dot(x, w_gate[0])
    up = dot(x, w_up[0])
    sig = jax.nn.sigmoid(gate)
    act[0] = gate * sig
    slope[0] = up * sig * (1.0 + gate * (1.0 - sig))

    @pl.when((expert == pl.num_programs(0) - 1) & (tile == pl.num_programs(1) - 1))
    def _():
        copy.wait()


def forward(pieces, slot, w_gate, w_up):
    experts, blocks, tokens = slot.shape
    _, features, units = w_gate.shape
    tile = min(UNIT_TILE, units)
    slots = blocks * MOST
    matrix = pl.BlockSpec((1, features, tile), lambda l, f: (l, 0, f))
    unit = pl.BlockSpec((1, slots, tile), lambda l, f: (l, 0, f))
    return pl.pallas_call(
        functools.partial(forward_kernel, len(pieces)),
        grid=(experts, units // tile),
        in_specs=[whole(p.shape) for p in pieces] + [whole(slot.shape), matrix, matrix],
        out_specs=[pl.BlockSpec(memory_space=pltpu.HBM), unit, unit],
        out_shape=[
            jax.ShapeDtypeStruct((experts, slots, features), BF16),
            jax.ShapeDtypeStruct((experts, slots, units), F32),
            jax.ShapeDtypeStruct((experts, slots, units), F32),
        ],
        scratch_shapes=dispatch_scratch(experts, blocks, tokens, features)
        + [pltpu.SemaphoreType.DMA],
        compiler_params=params(2, 52),
        cost_estimate=pl.CostEstimate(
            flops=4 * experts * slots * features * units,
            bytes_accessed=4 * experts * features * units,
            transcendentals=experts * slots * units,
        ),
    )(*pieces, slot, w_gate, w_up)


def hidden_kernel(count, *refs):
    pieces, (slot, weight, act, slope, w_down) = refs[:count], refs[count : count + 5]
    gate_grad, up_grad, held, chosen, grads, downs, ready = refs[count + 5 :]
    step = pl.program_id(0)
    tiles = pl.num_programs(0) // grads.shape[0]
    fetching = ((w_down,), (downs,), ready)

    @pl.when(step == 0)
    def _():
        for first in weight_tiles(step, *fetching):
            first.start()
        dispatch(pieces, slot, held, chosen, grads, weight)

    next_tiles(step, *fetching)
    hidden = dot(grads[step // tiles], downs[step % 2])
    up_grad[0] = (hidden * act[0]).astype(BF16)
    gate_grad[0] = (hidden * slope[0]).astype(BF16)


def hidden_grads(pieces, slot, weight, act, slope, w_down):
    experts, blocks, tokens = slot.shape
    _, features, units = w_down.shape
    tile = min(UNIT_TILE, units)
    tiles = units // tile
    slots = blocks * MOST
    unit = pl.BlockSpec((1, slots, tile), lambda i: (i // tiles, 0, i % tiles))
    return pl.pallas_call(
        functools.partial(hidden_kernel, len(pieces)),
        grid=(experts * tiles,),
        in_specs=[whole(p.shape) for p in pieces]
        + [whole(slot.shape), whole(slot.shape), unit, unit, pl.BlockSpec(memory_space=pl.ANY)],
        out_specs=[unit, unit],
        out_shape=[jax.ShapeDtypeStruct((experts, slots, units), BF16)] * 2,
        scratch_shapes=dispatch_scratch(experts, blocks, tokens, features)
        + [pltpu.VMEM((2, features, tile), BF16), pltpu.SemaphoreType.DMA((2, 1))],
        compiler_params=params(1, 48),
        cost_estimate=pl.CostEstimate(
            flops=2 * experts * slots * features * units,
            bytes_accessed=2 * experts * features * units,
            transcendentals=0,
        ),
    )(*pieces, slot, weight, act, slope, w_down)


def inputs_kernel(groups, back, gate_grad, up_grad, w_gate, w_up, *refs):
    sums, held = refs[:-1], refs[-1]
    blocks, tokens, _ = back.shape
    for l in range(gate_grad.shape[0]):
        partial = dot(gate_grad[l], w_gate[l], NT) + dot(up_grad[l], w_up[l], NT)
        for b in range(blocks):
            held[b, l * MOST : (l + 1) * MOST] = partial[b * MOST : (b + 1) * MOST].astype(BF16)
    for out, members in zip(sums, groups):
        for place, b in enumerate(members):
            out[place * tokens : (place + 1) * tokens] = dot(back[b], held[b]).astype(BF16)


def input_sums(back, gate_grad, up_grad, w_gate, w_up, groups, part, parts):
    blocks, tokens, _ = back.shape
    experts, features, units = w_gate.shape
    wide = FEATURE_TILE
    steps = features // parts // wide
    slots = blocks * MOST
    across = pl.BlockSpec((experts, wide, units), lambda i: (0, part * steps + i, 0))
    return pl.pallas_call(
        functools.partial(inputs_kernel, groups),
        grid=(steps,),
        in_specs=[whole(back.shape), whole(gate_grad.shape), whole(up_grad.shape), across, across],
        out_specs=[pl.BlockSpec((len(g) * tokens, wide), lambda i: (0, i)) for g in groups],
        out_shape=[
            jax.ShapeDtypeStruct((len(g) * tokens, features // parts), BF16) for g in groups
        ],
        scratch_shapes=[pltpu.VMEM((blocks, experts * MOST, wide), BF16)],
        compiler_params=params(1, 40),
        cost_estimate=pl.CostEstimate(
            flops=4 * experts * slots * features * units // parts,
            bytes_accessed=4 * experts * features * units // parts,
            transcendentals=0,
        ),
    )(back, gate_grad, up_grad, w_gate, w_up)


def back_matrix(slot):
    places = jnp.arange(MOST, dtype=F32)
    slot = lax.optimization_barrier(slot.transpose(1, 2, 0))
    parts = [slot[..., l : l + 1] == places for l in range(slot.shape[2])]
    return jnp.concatenate([p.astype(BF16) for p in parts], axis=2)


def weights_kernel(rows, gate_grad, up_grad, *refs):
    grad_gate, grad_up = refs[-2:]
    grad_gate[0] = dot(rows[0], gate_grad[0], TN)
    grad_up[0] = dot(rows[0], up_grad[0], TN)


def weight_grads(rows, gate_grad, up_grad, before, first, steps):
    experts, slots, features = rows.shape
    units = gate_grad.shape[2]
    wide = FEATURE_TILE
    each = features // wide
    unit = pl.BlockSpec((1, slots, units), lambda i: ((first + i) // each, 0, 0))
    out = pl.BlockSpec((1, wide, units), lambda i: ((first + i) // each, (first + i) % each, 0))
    kept = [] if before is None else list(before)
    return pl.pallas_call(
        weights_kernel,
        grid=(steps,),
        in_specs=[
            pl.BlockSpec((1, slots, wide), lambda i: ((first + i) // each, 0, (first + i) % each)),
            unit,
            unit,
        ]
        + [pl.BlockSpec(memory_space=pl.ANY)] * len(kept),
        out_specs=[out, out],
        out_shape=[jax.ShapeDtypeStruct((experts, features, units), F32)] * 2,
        input_output_aliases={3 + i: i for i in range(len(kept))},
        compiler_params=params(1, 30),
        cost_estimate=pl.CostEstimate(
            flops=4 * slots * steps * wide * units,
            bytes_accessed=8 * steps * wide * units,
            transcendentals=0,
        ),
    )(rows, gate_grad, up_grad, *kept)


def route_table(routes, gate_values):
    tokens = routes.shape[0]
    experts = jnp.arange(EXPERTS, dtype=jnp.int32)[:, None, None]
    match = routes.T[None] == experts
    member = jnp.any(match, axis=1)
    gate = jnp.sum(jnp.where(match, gate_values.T[None], 0.0), axis=1)
    place = jnp.arange(tokens, dtype=jnp.int32)
    earlier = (place[:, None] < place[None, :]).astype(BF16)
    slot = jnp.where(member, dot(member.astype(BF16), earlier), -1.0)
    return jnp.stack([slot, gate], axis=1)


def flip(value, axis, bit):
    count = lax.axis_size(axis)
    return lax.ppermute(value, axis, [(i, i ^ bit) for i in range(count)])


def swap_order(value, side, pair, dim):
    shape = value.shape
    value = value.reshape(shape[:dim] + (2, 2, shape[dim] // 4) + shape[dim + 1 :])
    value = jnp.where(side == 1, jnp.flip(value, dim), value)
    return jnp.where(pair == 1, jnp.flip(value, dim + 1), value).reshape(shape)


def add(*terms):
    total = terms[0].astype(F32)
    for term in terms[1:]:
        total = total + term.astype(F32)
    return total.astype(BF16)


def quarters(value, count, at):
    return lax.dynamic_slice_in_dim(value, at * (count // 4), count // 4, 0)


def local_near(out_grad, routes, gate_values, layer_input, w_gate, w_up, w_down):
    experts, features, _ = w_gate.shape
    me = lax.axis_index("expert")
    position = lax.axis_index("dp")
    side, pair = position % 2, position // 2 % 2
    tokens = out_grad.shape[0]
    half, quarter = tokens // 2, tokens // 4
    corner = side * 2 + pair

    def to_core(values):
        return tuple(flip(v, "expert", 1) for v in values)

    x_mine = [quarters(layer_input, tokens, q) for q in (corner, 3 - corner)]
    *x_mine, layer_input, out_grad, routes = lax.optimization_barrier(
        (*x_mine, layer_input, out_grad, routes)
    )
    x_across, x_corner = [flip(v, "expert", 2) for v in x_mine]
    x_sibling, g_sibling = to_core((layer_input, out_grad))
    x_sibling, routes = lax.optimization_barrier((x_sibling, routes))
    table = route_table(routes, gate_values)
    tables = []
    for r in range(4):
        part = lax.dynamic_slice_in_dim(table, (me ^ r) * experts, experts, 0)
        tables.append(flip(part, "expert", r) if r > 0 else part)
    x_far = (x_across, x_corner, flip(x_across, "dp", 1), flip(x_across, "dp", 2))
    g_across = flip(out_grad, "expert", 2)
    x_far = (*x_far, *to_core(x_far))
    table = jnp.stack(tables, axis=2)
    slot, weight = table[:, 0], table[:, 1]
    back = back_matrix(swap_order(slot, side, pair, 2))
    far = swap_order(slot[:, 2:], side, pair, 2).reshape(experts, 2, 4, quarter)
    far = jnp.stack([far[:, :, q] for q in (0, 3, 2, 1)], axis=2).reshape(experts, 2, tokens)
    slot_x = jnp.concatenate([slot[:, :2], far], axis=1)
    slot_x, back = lax.optimization_barrier((slot_x, back))
    rows, act, slope = forward((layer_input, x_sibling, *x_far), slot_x, w_gate, w_up)
    act, g_across = lax.optimization_barrier((act, g_across))
    gate_grad, up_grad = hidden_grads(
        (out_grad, g_sibling, g_across, *to_core((g_across,))), slot, weight, act, slope, w_down
    )

    groups = ((0, 2), (1, 3))
    kept_a, sent_a = input_sums(back, gate_grad, up_grad, w_gate, w_up, groups, 0, 2)
    kept_b, sent_b = input_sums(back, gate_grad, up_grad, w_gate, w_up, groups, 1, 2)

    def piece(after, before, *which):
        held, rows_now = lax.optimization_barrier((after, rows))
        return held, weight_grads(rows_now, gate_grad, up_grad, before, *which)

    def corners(value):
        z, x, diagonal = value
        x, diagonal = flip(x, "dp", 1), flip(diagonal, "dp", 3)
        return [flip(z, "dp", 2), x, diagonal]

    def cut(value, count):
        return [value[i : i + quarter] for i in range(0, count * quarter, quarter)]

    chip_a = add(kept_a, flip(sent_a, "expert", 1))
    got = flip(sent_b, "expert", 1)
    chip_b = [add(a, b) for a, b in zip(cut(kept_b, 8), cut(got, 8))]
    far_a = chip_a[tokens:]
    away = [jnp.concatenate([chip_b[q], chip_b[4 + q]], axis=0) for q in (1, 2, 3)]
    (far_a, *away), grads = piece((far_a, *away), None, 0, 4)
    got_x = flip(away[1], "dp", 1)
    got_a = flip(far_a, "expert", 2)
    got_b = [flip(away[2], "dp", 3), flip(away[0], "dp", 2), got_x]
    got_a, got_b, *grads = lax.optimization_barrier((got_a, got_b, *grads))
    own_a = [add(a, b) for a, b in zip(cut(chip_a, 4), cut(got_a, 4))]
    mine_b = add(chip_b[0], *(v[:quarter] for v in got_b))
    far_b = add(chip_b[4], *(v[quarter:] for v in got_b))
    (far_b, *own_a), grads = piece((far_b, *own_a), grads, 4, 1)
    got_a, got_b = corners(own_a[1:]), flip(far_b, "expert", 2)
    got_a, got_b, *grads = lax.optimization_barrier((got_a, got_b, *grads))
    mine = jnp.concatenate([add(own_a[0], *got_a), add(mine_b, got_b)], axis=1)
    mine, grads = piece(mine, grads, 5, 4)
    got = flip(mine, "dp", 4)
    got, *grads = lax.optimization_barrier((got, *grads))
    mine = add(mine, got)
    mine, grads = piece(mine, grads, 9, 3)
    got = corners([mine] * 3)
    got, *grads = lax.optimization_barrier((got, *grads))
    total = swap_order(jnp.concatenate([mine, *got], axis=0), side, pair, 0)
    return (total, *grads)


def local_any(out_grad, routes, gate_values, layer_input, w_gate, w_up, w_down):
    experts = w_gate.shape[0]
    me = lax.axis_index("expert")
    rows_in = lax.all_gather(layer_input, "expert", tiled=True)
    grads_in = lax.all_gather(out_grad, "expert", tiled=True)
    table = lax.all_gather(route_table(routes, gate_values), "expert")
    table = lax.dynamic_slice_in_dim(table, me * experts, experts, 1).transpose(1, 2, 0, 3)
    slot, weight = table[:, 0], table[:, 1]
    rows, act, slope = forward([rows_in], slot, w_gate, w_up)
    gate_grad, up_grad = hidden_grads([grads_in], slot, weight, act, slope, w_down)
    groups = (tuple(range(slot.shape[1])),)
    (sums,) = input_sums(back_matrix(slot), gate_grad, up_grad, w_gate, w_up, groups, 0, 1)
    blocks = experts * layer_input.shape[1] // FEATURE_TILE
    grads = weight_grads(rows, gate_grad, up_grad, None, 0, blocks)
    own = lax.psum_scatter(sums, "expert", scatter_dimension=0, tiled=True)
    return (lax.psum(own, "dp"), *grads)


def solution(mesh):
    near = mesh.shape["dp"] == 8 and mesh.shape["expert"] == 4
    placed = (
        P("expert", None),
        P("expert", None),
        P("expert", None),
        P("expert", None),
        P("expert", None, "dp"),
        P("expert", None, "dp"),
        P("expert", None, "dp"),
    )
    return jax.shard_map(
        local_near if near else local_any,
        mesh=mesh,
        in_specs=placed,
        out_specs=(P("expert", None), P("expert", None, "dp"), P("expert", None, "dp")),
        check_vma=False,
    )
```

```python
import functools

import jax
import jax.numpy as jnp
from jax import lax
from jax.experimental import pallas as pl
from jax.experimental.pallas import tpu as pltpu
from jax.sharding import PartitionSpec as P

EXPERTS = 8
MOST = 80
UNIT_TILE = 512
FEATURE_TILE = 512
BF16 = jnp.bfloat16
F32 = jnp.float32
NN = (((1,), (0,)), ((), ()))
NT = (((1,), (1,)), ((), ()))
TN = (((0,), (0,)), ((), ()))


def dot(a, b, dims=NN):
    return lax.dot_general(a, b, dims, preferred_element_type=F32)


def params(count, mebibytes):
    return pltpu.CompilerParams(
        dimension_semantics=("arbitrary",) * count, vmem_limit_bytes=mebibytes * 1024 * 1024
    )


def whole(shape):
    return pl.BlockSpec(
        shape, lambda *_: (0,) * len(shape), pipeline_mode=pl.Buffered(buffer_count=1)
    )


def one_hot(slot_row):
    slots = lax.broadcasted_iota(jnp.int32, (MOST, slot_row.shape[1]), 0)
    return slots == slot_row.astype(jnp.int32)


def lay_out(held, pieces, first):
    rows, at = held.shape[0], 0
    for piece in pieces:
        low, high = max(first, at), min(first + rows, at + piece.shape[0])
        if low < high:
            held[low - first : high - first] = piece[low - at : high - at]
        at += piece.shape[0]


def column_chunks(features):
    step = 768 if features % 768 == 0 else features
    return [slice(c, c + step) for c in range(0, features, step)]


def dispatch(pieces, slot, held, chosen, out, weight=None):
    experts, blocks, tokens = slot.shape
    group = held.shape[0] // tokens
    places = [(l, b) for l in range(experts) for b in range(group)]
    for start in range(0, blocks, group):
        chosen[...] = jnp.zeros_like(chosen)
        scales = []
        for i, (l, b) in enumerate(places):
            at = slice(start + b, start + b + 1)
            mask = one_hot(slot[l, at, :])
            chosen[i * MOST : (i + 1) * MOST, b * tokens : (b + 1) * tokens] = mask.astype(BF16)
            if weight is not None:
                scales.append(
                    jnp.sum(jnp.where(mask, weight[l, at, :], 0.0), axis=1, keepdims=True)
                )
        lay_out(held, pieces, start * tokens)
        for cols in column_chunks(held.shape[1]):
            taken = dot(chosen[...], held[:, cols])
            for i, (l, b) in enumerate(places):
                part = taken[i * MOST : (i + 1) * MOST]
                if scales:
                    part = part * scales[i]
                span = slice((start + b) * MOST, (start + b + 1) * MOST)
                out[l, span, cols] = part.astype(BF16)


def dispatch_scratch(experts, blocks, tokens, features):
    group = 2 if blocks % 2 == 0 else 1
    return [
        pltpu.VMEM((group * tokens, features), BF16),
        pltpu.VMEM((experts * group * MOST, group * tokens), BF16),
        pltpu.VMEM((experts, blocks * MOST, features), BF16),
    ]


def weight_tiles(step, matrices, buffers, ready):
    _, features, tile = buffers[0].shape
    tiles = matrices[0].shape[2] // tile
    cols = pl.ds(pl.multiple_of(step % tiles * tile, tile), tile)
    return [
        pltpu.make_async_copy(
            matrix.at[step // tiles, :, cols], buffer.at[step % 2], ready.at[step % 2, i]
        )
        for i, (matrix, buffer) in enumerate(zip(matrices, buffers))
    ]


def next_tiles(step, matrices, buffers, ready):
    @pl.when(step + 1 < pl.num_programs(0))
    def _():
        for copy in weight_tiles(step + 1, matrices, buffers, ready):
            copy.start()

    for copy in weight_tiles(step, matrices, buffers, ready):
        copy.wait()


def forward_kernel(count, *refs):
    pieces, (slot, w_gate, w_up, rows_out, act, slope) = refs[:count], refs[count : count + 6]
    held, chosen, rows, sent = refs[count + 6 :]
    expert, tile = pl.program_id(0), pl.program_id(1)
    copy = pltpu.make_async_copy(rows, rows_out, sent)

    @pl.when((expert == 0) & (tile == 0))
    def _():
        dispatch(pieces, slot, held, chosen, rows)
        copy.start()

    x = rows[expert]
    gate = dot(x, w_gate[0])
    up = dot(x, w_up[0])
    sig = jax.nn.sigmoid(gate)
    act[0] = gate * sig
    slope[0] = up * sig * (1.0 + gate * (1.0 - sig))

    @pl.when((expert == pl.num_programs(0) - 1) & (tile == pl.num_programs(1) - 1))
    def _():
        copy.wait()


def forward(pieces, slot, w_gate, w_up):
    experts, blocks, tokens = slot.shape
    _, features, units = w_gate.shape
    tile = min(UNIT_TILE, units)
    slots = blocks * MOST
    matrix = pl.BlockSpec((1, features, tile), lambda l, f: (l, 0, f))
    unit = pl.BlockSpec((1, slots, tile), lambda l, f: (l, 0, f))
    return pl.pallas_call(
        functools.partial(forward_kernel, len(pieces)),
        grid=(experts, units // tile),
        in_specs=[whole(p.shape) for p in pieces] + [whole(slot.shape), matrix, matrix],
        out_specs=[pl.BlockSpec(memory_space=pltpu.HBM), unit, unit],
        out_shape=[
            jax.ShapeDtypeStruct((experts, slots, features), BF16),
            jax.ShapeDtypeStruct((experts, slots, units), F32),
            jax.ShapeDtypeStruct((experts, slots, units), F32),
        ],
        scratch_shapes=dispatch_scratch(experts, blocks, tokens, features)
        + [pltpu.SemaphoreType.DMA],
        compiler_params=params(2, 52),
        cost_estimate=pl.CostEstimate(
            flops=4 * experts * slots * features * units,
            bytes_accessed=4 * experts * features * units,
            transcendentals=experts * slots * units,
        ),
    )(*pieces, slot, w_gate, w_up)


def hidden_kernel(count, *refs):
    pieces, (slot, weight, act, slope, w_down) = refs[:count], refs[count : count + 5]
    gate_grad, up_grad, held, chosen, grads, downs, ready = refs[count + 5 :]
    step = pl.program_id(0)
    tiles = pl.num_programs(0) // grads.shape[0]
    fetching = ((w_down,), (downs,), ready)

    @pl.when(step == 0)
    def _():
        for first in weight_tiles(step, *fetching):
            first.start()
        dispatch(pieces, slot, held, chosen, grads, weight)

    next_tiles(step, *fetching)
    hidden = dot(grads[step // tiles], downs[step % 2])
    up_grad[0] = (hidden * act[0]).astype(BF16)
    gate_grad[0] = (hidden * slope[0]).astype(BF16)


def hidden_grads(pieces, slot, weight, act, slope, w_down):
    experts, blocks, tokens = slot.shape
    _, features, units = w_down.shape
    tile = min(UNIT_TILE, units)
    tiles = units // tile
    slots = blocks * MOST
    unit = pl.BlockSpec((1, slots, tile), lambda i: (i // tiles, 0, i % tiles))
    return pl.pallas_call(
        functools.partial(hidden_kernel, len(pieces)),
        grid=(experts * tiles,),
        in_specs=[whole(p.shape) for p in pieces]
        + [whole(slot.shape), whole(slot.shape), unit, unit, pl.BlockSpec(memory_space=pl.ANY)],
        out_specs=[unit, unit],
        out_shape=[jax.ShapeDtypeStruct((experts, slots, units), BF16)] * 2,
        scratch_shapes=dispatch_scratch(experts, blocks, tokens, features)
        + [pltpu.VMEM((2, features, tile), BF16), pltpu.SemaphoreType.DMA((2, 1))],
        compiler_params=params(1, 48),
        cost_estimate=pl.CostEstimate(
            flops=2 * experts * slots * features * units,
            bytes_accessed=2 * experts * features * units,
            transcendentals=0,
        ),
    )(*pieces, slot, weight, act, slope, w_down)


def inputs_kernel(groups, back, gate_grad, up_grad, w_gate, w_up, *refs):
    sums, held = refs[:-1], refs[-1]
    blocks, tokens, _ = back.shape
    for l in range(gate_grad.shape[0]):
        partial = dot(gate_grad[l], w_gate[l], NT) + dot(up_grad[l], w_up[l], NT)
        for b in range(blocks):
            held[b, l * MOST : (l + 1) * MOST] = partial[b * MOST : (b + 1) * MOST].astype(BF16)
    for out, members in zip(sums, groups):
        for place, b in enumerate(members):
            out[place * tokens : (place + 1) * tokens] = dot(back[b], held[b]).astype(BF16)


def input_sums(back, gate_grad, up_grad, w_gate, w_up, groups, part, parts):
    blocks, tokens, _ = back.shape
    experts, features, units = w_gate.shape
    wide = FEATURE_TILE
    steps = features // parts // wide
    slots = blocks * MOST
    across = pl.BlockSpec((experts, wide, units), lambda i: (0, part * steps + i, 0))
    return pl.pallas_call(
        functools.partial(inputs_kernel, groups),
        grid=(steps,),
        in_specs=[whole(back.shape), whole(gate_grad.shape), whole(up_grad.shape), across, across],
        out_specs=[pl.BlockSpec((len(g) * tokens, wide), lambda i: (0, i)) for g in groups],
        out_shape=[
            jax.ShapeDtypeStruct((len(g) * tokens, features // parts), BF16) for g in groups
        ],
        scratch_shapes=[pltpu.VMEM((blocks, experts * MOST, wide), BF16)],
        compiler_params=params(1, 40),
        cost_estimate=pl.CostEstimate(
            flops=4 * experts * slots * features * units // parts,
            bytes_accessed=4 * experts * features * units // parts,
            transcendentals=0,
        ),
    )(back, gate_grad, up_grad, w_gate, w_up)


def back_matrix(slot):
    places = jnp.arange(MOST, dtype=F32)
    slot = lax.optimization_barrier(slot.transpose(1, 2, 0))
    parts = [slot[..., l : l + 1] == places for l in range(slot.shape[2])]
    return jnp.concatenate([p.astype(BF16) for p in parts], axis=2)


def weights_kernel(rows, gate_grad, up_grad, *refs):
    grad_gate, grad_up = refs[-2:]
    grad_gate[0] = dot(rows[0], gate_grad[0], TN)
    grad_up[0] = dot(rows[0], up_grad[0], TN)


def weight_grads(rows, gate_grad, up_grad, before, first, steps):
    experts, slots, features = rows.shape
    units = gate_grad.shape[2]
    wide = FEATURE_TILE
    each = features // wide
    unit = pl.BlockSpec((1, slots, units), lambda i: ((first + i) // each, 0, 0))
    out = pl.BlockSpec((1, wide, units), lambda i: ((first + i) // each, (first + i) % each, 0))
    kept = [] if before is None else list(before)
    return pl.pallas_call(
        weights_kernel,
        grid=(steps,),
        in_specs=[
            pl.BlockSpec((1, slots, wide), lambda i: ((first + i) // each, 0, (first + i) % each)),
            unit,
            unit,
        ]
        + [pl.BlockSpec(memory_space=pl.ANY)] * len(kept),
        out_specs=[out, out],
        out_shape=[jax.ShapeDtypeStruct((experts, features, units), F32)] * 2,
        input_output_aliases={3 + i: i for i in range(len(kept))},
        compiler_params=params(1, 30),
        cost_estimate=pl.CostEstimate(
            flops=4 * slots * steps * wide * units,
            bytes_accessed=8 * steps * wide * units,
            transcendentals=0,
        ),
    )(rows, gate_grad, up_grad, *kept)


def route_table(routes, gate_values):
    tokens = routes.shape[0]
    experts = jnp.arange(EXPERTS, dtype=jnp.int32)[:, None, None]
    match = routes.T[None] == experts
    member = jnp.any(match, axis=1)
    gate = jnp.sum(jnp.where(match, gate_values.T[None], 0.0), axis=1)
    place = jnp.arange(tokens, dtype=jnp.int32)
    earlier = (place[:, None] < place[None, :]).astype(BF16)
    slot = jnp.where(member, dot(member.astype(BF16), earlier), -1.0)
    return jnp.stack([slot, gate], axis=1)


def flip(value, axis, bit):
    count = lax.axis_size(axis)
    return lax.ppermute(value, axis, [(i, i ^ bit) for i in range(count)])


def swap_order(value, side, pair, dim):
    shape = value.shape
    value = value.reshape(shape[:dim] + (2, 2, shape[dim] // 4) + shape[dim + 1 :])
    value = jnp.where(side == 1, jnp.flip(value, dim), value)
    return jnp.where(pair == 1, jnp.flip(value, dim + 1), value).reshape(shape)


def add(*terms):
    total = terms[0].astype(F32)
    for term in terms[1:]:
        total = total + term.astype(F32)
    return total.astype(BF16)


def quarters(value, count, at):
    return lax.dynamic_slice_in_dim(value, at * (count // 4), count // 4, 0)


def local_near(out_grad, routes, gate_values, layer_input, w_gate, w_up, w_down):
    experts, features, _ = w_gate.shape
    me = lax.axis_index("expert")
    position = lax.axis_index("dp")
    side, pair = position % 2, position // 2 % 2
    tokens = out_grad.shape[0]
    half, quarter = tokens // 2, tokens // 4
    corner = side * 2 + pair

    def to_core(values):
        return tuple(flip(v, "expert", 1) for v in values)

    x_mine = [quarters(layer_input, tokens, q) for q in (corner, 3 - corner)]
    *x_mine, layer_input, out_grad, routes = lax.optimization_barrier(
        (*x_mine, layer_input, out_grad, routes)
    )
    x_across, x_corner = [flip(v, "expert", 2) for v in x_mine]
    x_sibling, g_sibling = to_core((layer_input, out_grad))
    x_sibling, routes = lax.optimization_barrier((x_sibling, routes))
    table = route_table(routes, gate_values)
    tables = []
    for r in range(4):
        part = lax.dynamic_slice_in_dim(table, (me ^ r) * experts, experts, 0)
        tables.append(flip(part, "expert", r) if r > 0 else part)
    x_far = (x_across, x_corner, flip(x_across, "dp", 1), flip(x_across, "dp", 2))
    g_across = flip(out_grad, "expert", 2)
    x_far = (*x_far, *to_core(x_far))
    table = jnp.stack(tables, axis=2)
    slot, weight = table[:, 0], table[:, 1]
    back = back_matrix(swap_order(slot, side, pair, 2))
    far = swap_order(slot[:, 2:], side, pair, 2).reshape(experts, 2, 4, quarter)
    far = jnp.stack([far[:, :, q] for q in (0, 3, 2, 1)], axis=2).reshape(experts, 2, tokens)
    slot_x = jnp.concatenate([slot[:, :2], far], axis=1)
    slot_x, back = lax.optimization_barrier((slot_x, back))
    rows, act, slope = forward((layer_input, x_sibling, *x_far), slot_x, w_gate, w_up)
    act, g_across = lax.optimization_barrier((act, g_across))
    gate_grad, up_grad = hidden_grads(
        (out_grad, g_sibling, g_across, *to_core((g_across,))), slot, weight, act, slope, w_down
    )

    groups = ((0, 2), (1, 3))
    kept_a, sent_a = input_sums(back, gate_grad, up_grad, w_gate, w_up, groups, 0, 2)
    kept_b, sent_b = input_sums(back, gate_grad, up_grad, w_gate, w_up, groups, 1, 2)

    def piece(after, before, *which):
        held, rows_now = lax.optimization_barrier((after, rows))
        return held, weight_grads(rows_now, gate_grad, up_grad, before, *which)

    def corners(value):
        z, x, diagonal = value
        x, diagonal = flip(x, "dp", 1), flip(diagonal, "dp", 3)
        return [flip(z, "dp", 2), x, diagonal]

    def cut(value, count):
        return [value[i : i + quarter] for i in range(0, count * quarter, quarter)]

    chip_a = add(kept_a, flip(sent_a, "expert", 1))
    got = flip(sent_b, "expert", 1)
    chip_b = [add(a, b) for a, b in zip(cut(kept_b, 8), cut(got, 8))]
    got_a = flip(chip_a[tokens:], "expert", 2)
    away = [jnp.concatenate([chip_b[q], chip_b[4 + q]], axis=0) for q in (1, 2, 3)]
    away, grads = piece(away, None, 0, 4)
    got_x = flip(away[1], "dp", 1)
    got_b = [flip(away[2], "dp", 3), flip(away[0], "dp", 2), got_x]
    got_a, got_b, *grads = lax.optimization_barrier((got_a, got_b, *grads))
    own_a = [add(a, b) for a, b in zip(cut(chip_a, 4), cut(got_a, 4))]
    mine_b = add(chip_b[0], *(v[:quarter] for v in got_b))
    far_b = add(chip_b[4], *(v[quarter:] for v in got_b))
    (far_b, *own_a), grads = piece((far_b, *own_a), grads, 4, 1)
    got_a, got_b = corners(own_a[1:]), flip(far_b, "expert", 2)
    got_a, got_b, *grads = lax.optimization_barrier((got_a, got_b, *grads))
    mine = jnp.concatenate([add(own_a[0], *got_a), add(mine_b, got_b)], axis=1)
    mine, grads = piece(mine, grads, 5, 4)
    got = flip(mine, "dp", 4)
    got, *grads = lax.optimization_barrier((got, *grads))
    mine = add(mine, got)
    mine, grads = piece(mine, grads, 9, 3)
    got = corners([mine] * 3)
    got, *grads = lax.optimization_barrier((got, *grads))
    total = swap_order(jnp.concatenate([mine, *got], axis=0), side, pair, 0)
    return (total, *grads)


def local_any(out_grad, routes, gate_values, layer_input, w_gate, w_up, w_down):
    experts = w_gate.shape[0]
    me = lax.axis_index("expert")
    rows_in = lax.all_gather(layer_input, "expert", tiled=True)
    grads_in = lax.all_gather(out_grad, "expert", tiled=True)
    table = lax.all_gather(route_table(routes, gate_values), "expert")
    table = lax.dynamic_slice_in_dim(table, me * experts, experts, 1).transpose(1, 2, 0, 3)
    slot, weight = table[:, 0], table[:, 1]
    rows, act, slope = forward([rows_in], slot, w_gate, w_up)
    gate_grad, up_grad = hidden_grads([grads_in], slot, weight, act, slope, w_down)
    groups = (tuple(range(slot.shape[1])),)
    (sums,) = input_sums(back_matrix(slot), gate_grad, up_grad, w_gate, w_up, groups, 0, 1)
    blocks = experts * layer_input.shape[1] // FEATURE_TILE
    grads = weight_grads(rows, gate_grad, up_grad, None, 0, blocks)
    own = lax.psum_scatter(sums, "expert", scatter_dimension=0, tiled=True)
    return (lax.psum(own, "dp"), *grads)


def solution(mesh):
    near = mesh.shape["dp"] == 8 and mesh.shape["expert"] == 4
    placed = (
        P("expert", None),
        P("expert", None),
        P("expert", None),
        P("expert", None),
        P("expert", None, "dp"),
        P("expert", None, "dp"),
        P("expert", None, "dp"),
    )
    return jax.shard_map(
        local_near if near else local_any,
        mesh=mesh,
        in_specs=placed,
        out_specs=(P("expert", None), P("expert", None, "dp"), P("expert", None, "dp")),
        check_vma=False,
    )
```

```python
import functools

import jax
import jax.numpy as jnp
from jax import lax
from jax.experimental import pallas as pl
from jax.experimental.pallas import tpu as pltpu
from jax.sharding import PartitionSpec as P

EXPERTS = 8
MOST = 80
UNIT_TILE = 512
FEATURE_TILE = 512
BF16 = jnp.bfloat16
F32 = jnp.float32
NN = (((1,), (0,)), ((), ()))
NT = (((1,), (1,)), ((), ()))
TN = (((0,), (0,)), ((), ()))


def dot(a, b, dims=NN):
    return lax.dot_general(a, b, dims, preferred_element_type=F32)


def params(count, mebibytes):
    return pltpu.CompilerParams(
        dimension_semantics=("arbitrary",) * count, vmem_limit_bytes=mebibytes * 1024 * 1024
    )


def whole(shape):
    return pl.BlockSpec(
        shape, lambda *_: (0,) * len(shape), pipeline_mode=pl.Buffered(buffer_count=1)
    )


def one_hot(slot_row):
    slots = lax.broadcasted_iota(jnp.int32, (MOST, slot_row.shape[1]), 0)
    return slots == slot_row.astype(jnp.int32)


def lay_out(held, pieces, first):
    rows, at = held.shape[0], 0
    for piece in pieces:
        low, high = max(first, at), min(first + rows, at + piece.shape[0])
        if low < high:
            held[low - first : high - first] = piece[low - at : high - at]
        at += piece.shape[0]


def column_chunks(features):
    step = 768 if features % 768 == 0 else features
    return [slice(c, c + step) for c in range(0, features, step)]


def dispatch(pieces, slot, held, chosen, out, weight=None):
    experts, blocks, tokens = slot.shape
    group = held.shape[0] // tokens
    places = [(l, b) for l in range(experts) for b in range(group)]
    for start in range(0, blocks, group):
        chosen[...] = jnp.zeros_like(chosen)
        scales = []
        for i, (l, b) in enumerate(places):
            at = slice(start + b, start + b + 1)
            mask = one_hot(slot[l, at, :])
            chosen[i * MOST : (i + 1) * MOST, b * tokens : (b + 1) * tokens] = mask.astype(BF16)
            if weight is not None:
                scales.append(
                    jnp.sum(jnp.where(mask, weight[l, at, :], 0.0), axis=1, keepdims=True)
                )
        lay_out(held, pieces, start * tokens)
        for cols in column_chunks(held.shape[1]):
            taken = dot(chosen[...], held[:, cols])
            for i, (l, b) in enumerate(places):
                part = taken[i * MOST : (i + 1) * MOST]
                if scales:
                    part = part * scales[i]
                span = slice((start + b) * MOST, (start + b + 1) * MOST)
                out[l, span, cols] = part.astype(BF16)


def dispatch_scratch(experts, blocks, tokens, features):
    group = 2 if blocks % 2 == 0 else 1
    return [
        pltpu.VMEM((group * tokens, features), BF16),
        pltpu.VMEM((experts * group * MOST, group * tokens), BF16),
        pltpu.VMEM((experts, blocks * MOST, features), BF16),
    ]


def weight_tiles(step, matrices, buffers, ready):
    _, features, tile = buffers[0].shape
    tiles = matrices[0].shape[2] // tile
    cols = pl.ds(pl.multiple_of(step % tiles * tile, tile), tile)
    return [
        pltpu.make_async_copy(
            matrix.at[step // tiles, :, cols], buffer.at[step % 2], ready.at[step % 2, i]
        )
        for i, (matrix, buffer) in enumerate(zip(matrices, buffers))
    ]


def next_tiles(step, matrices, buffers, ready):
    @pl.when(step + 1 < pl.num_programs(0))
    def _():
        for copy in weight_tiles(step + 1, matrices, buffers, ready):
            copy.start()

    for copy in weight_tiles(step, matrices, buffers, ready):
        copy.wait()


def forward_kernel(count, *refs):
    pieces, (slot, w_gate, w_up, rows_out, act, slope) = refs[:count], refs[count : count + 6]
    held, chosen, rows, sent = refs[count + 6 :]
    expert, tile = pl.program_id(0), pl.program_id(1)
    copy = pltpu.make_async_copy(rows, rows_out, sent)

    @pl.when((expert == 0) & (tile == 0))
    def _():
        dispatch(pieces, slot, held, chosen, rows)
        copy.start()

    x = rows[expert]
    gate = dot(x, w_gate[0])
    up = dot(x, w_up[0])
    sig = jax.nn.sigmoid(gate)
    act[0] = gate * sig
    slope[0] = up * sig * (1.0 + gate * (1.0 - sig))

    @pl.when((expert == pl.num_programs(0) - 1) & (tile == pl.num_programs(1) - 1))
    def _():
        copy.wait()


def forward(pieces, slot, w_gate, w_up):
    experts, blocks, tokens = slot.shape
    _, features, units = w_gate.shape
    tile = min(UNIT_TILE, units)
    slots = blocks * MOST
    matrix = pl.BlockSpec((1, features, tile), lambda l, f: (l, 0, f))
    unit = pl.BlockSpec((1, slots, tile), lambda l, f: (l, 0, f))
    return pl.pallas_call(
        functools.partial(forward_kernel, len(pieces)),
        grid=(experts, units // tile),
        in_specs=[whole(p.shape) for p in pieces] + [whole(slot.shape), matrix, matrix],
        out_specs=[pl.BlockSpec(memory_space=pltpu.HBM), unit, unit],
        out_shape=[
            jax.ShapeDtypeStruct((experts, slots, features), BF16),
            jax.ShapeDtypeStruct((experts, slots, units), F32),
            jax.ShapeDtypeStruct((experts, slots, units), F32),
        ],
        scratch_shapes=dispatch_scratch(experts, blocks, tokens, features)
        + [pltpu.SemaphoreType.DMA],
        compiler_params=params(2, 52),
        cost_estimate=pl.CostEstimate(
            flops=4 * experts * slots * features * units,
            bytes_accessed=4 * experts * features * units,
            transcendentals=experts * slots * units,
        ),
    )(*pieces, slot, w_gate, w_up)


def hidden_kernel(count, *refs):
    pieces, (slot, weight, act, slope, w_down) = refs[:count], refs[count : count + 5]
    gate_grad, up_grad, held, chosen, grads, downs, ready = refs[count + 5 :]
    step = pl.program_id(0)
    tiles = pl.num_programs(0) // grads.shape[0]
    fetching = ((w_down,), (downs,), ready)

    @pl.when(step == 0)
    def _():
        for first in weight_tiles(step, *fetching):
            first.start()
        dispatch(pieces, slot, held, chosen, grads, weight)

    next_tiles(step, *fetching)
    hidden = dot(grads[step // tiles], downs[step % 2])
    up_grad[0] = (hidden * act[0]).astype(BF16)
    gate_grad[0] = (hidden * slope[0]).astype(BF16)


def hidden_grads(pieces, slot, weight, act, slope, w_down):
    experts, blocks, tokens = slot.shape
    _, features, units = w_down.shape
    tile = min(UNIT_TILE, units)
    tiles = units // tile
    slots = blocks * MOST
    unit = pl.BlockSpec((1, slots, tile), lambda i: (i // tiles, 0, i % tiles))
    return pl.pallas_call(
        functools.partial(hidden_kernel, len(pieces)),
        grid=(experts * tiles,),
        in_specs=[whole(p.shape) for p in pieces]
        + [whole(slot.shape), whole(slot.shape), unit, unit, pl.BlockSpec(memory_space=pl.ANY)],
        out_specs=[unit, unit],
        out_shape=[jax.ShapeDtypeStruct((experts, slots, units), BF16)] * 2,
        scratch_shapes=dispatch_scratch(experts, blocks, tokens, features)
        + [pltpu.VMEM((2, features, tile), BF16), pltpu.SemaphoreType.DMA((2, 1))],
        compiler_params=params(1, 48),
        cost_estimate=pl.CostEstimate(
            flops=2 * experts * slots * features * units,
            bytes_accessed=2 * experts * features * units,
            transcendentals=0,
        ),
    )(*pieces, slot, weight, act, slope, w_down)


def inputs_kernel(groups, back, gate_grad, up_grad, w_gate, w_up, *refs):
    sums, held = refs[:-1], refs[-1]
    blocks, tokens, _ = back.shape
    for l in range(gate_grad.shape[0]):
        partial = dot(gate_grad[l], w_gate[l], NT) + dot(up_grad[l], w_up[l], NT)
        for b in range(blocks):
            held[b, l * MOST : (l + 1) * MOST] = partial[b * MOST : (b + 1) * MOST].astype(BF16)
    for out, members in zip(sums, groups):
        for place, b in enumerate(members):
            out[place * tokens : (place + 1) * tokens] = dot(back[b], held[b]).astype(BF16)


def input_sums(back, gate_grad, up_grad, w_gate, w_up, groups, part, parts):
    blocks, tokens, _ = back.shape
    experts, features, units = w_gate.shape
    wide = FEATURE_TILE
    steps = features // parts // wide
    slots = blocks * MOST
    across = pl.BlockSpec((experts, wide, units), lambda i: (0, part * steps + i, 0))
    return pl.pallas_call(
        functools.partial(inputs_kernel, groups),
        grid=(steps,),
        in_specs=[whole(back.shape), whole(gate_grad.shape), whole(up_grad.shape), across, across],
        out_specs=[pl.BlockSpec((len(g) * tokens, wide), lambda i: (0, i)) for g in groups],
        out_shape=[
            jax.ShapeDtypeStruct((len(g) * tokens, features // parts), BF16) for g in groups
        ],
        scratch_shapes=[pltpu.VMEM((blocks, experts * MOST, wide), BF16)],
        compiler_params=params(1, 40),
        cost_estimate=pl.CostEstimate(
            flops=4 * experts * slots * features * units // parts,
            bytes_accessed=4 * experts * features * units // parts,
            transcendentals=0,
        ),
    )(back, gate_grad, up_grad, w_gate, w_up)


def back_matrix(slot):
    places = jnp.arange(MOST, dtype=F32)
    slot = lax.optimization_barrier(slot.transpose(1, 2, 0))
    parts = [slot[..., l : l + 1] == places for l in range(slot.shape[2])]
    return jnp.concatenate([p.astype(BF16) for p in parts], axis=2)


def weights_kernel(rows, gate_grad, up_grad, *refs):
    grad_gate, grad_up = refs[-2:]
    grad_gate[0] = dot(rows[0], gate_grad[0], TN)
    grad_up[0] = dot(rows[0], up_grad[0], TN)


def weight_grads(rows, gate_grad, up_grad, before, first, steps):
    experts, slots, features = rows.shape
    units = gate_grad.shape[2]
    wide = FEATURE_TILE
    each = features // wide
    unit = pl.BlockSpec((1, slots, units), lambda i: ((first + i) // each, 0, 0))
    out = pl.BlockSpec((1, wide, units), lambda i: ((first + i) // each, (first + i) % each, 0))
    kept = [] if before is None else list(before)
    return pl.pallas_call(
        weights_kernel,
        grid=(steps,),
        in_specs=[
            pl.BlockSpec((1, slots, wide), lambda i: ((first + i) // each, 0, (first + i) % each)),
            unit,
            unit,
        ]
        + [pl.BlockSpec(memory_space=pl.ANY)] * len(kept),
        out_specs=[out, out],
        out_shape=[jax.ShapeDtypeStruct((experts, features, units), F32)] * 2,
        input_output_aliases={3 + i: i for i in range(len(kept))},
        compiler_params=params(1, 30),
        cost_estimate=pl.CostEstimate(
            flops=4 * slots * steps * wide * units,
            bytes_accessed=8 * steps * wide * units,
            transcendentals=0,
        ),
    )(rows, gate_grad, up_grad, *kept)


def route_table(routes, gate_values):
    tokens = routes.shape[0]
    experts = jnp.arange(EXPERTS, dtype=jnp.int32)[:, None, None]
    match = routes.T[None] == experts
    member = jnp.any(match, axis=1)
    gate = jnp.sum(jnp.where(match, gate_values.T[None], 0.0), axis=1)
    place = jnp.arange(tokens, dtype=jnp.int32)
    earlier = (place[:, None] < place[None, :]).astype(BF16)
    slot = jnp.where(member, dot(member.astype(BF16), earlier), -1.0)
    return jnp.stack([slot, gate], axis=1)


def flip(value, axis, bit):
    count = lax.axis_size(axis)
    return lax.ppermute(value, axis, [(i, i ^ bit) for i in range(count)])


def swap_order(value, side, pair, dim):
    shape = value.shape
    value = value.reshape(shape[:dim] + (2, 2, shape[dim] // 4) + shape[dim + 1 :])
    value = jnp.where(side == 1, jnp.flip(value, dim), value)
    return jnp.where(pair == 1, jnp.flip(value, dim + 1), value).reshape(shape)


def add(*terms):
    total = terms[0].astype(F32)
    for term in terms[1:]:
        total = total + term.astype(F32)
    return total.astype(BF16)


def quarters(value, count, at):
    return lax.dynamic_slice_in_dim(value, at * (count // 4), count // 4, 0)


def local_near(out_grad, routes, gate_values, layer_input, w_gate, w_up, w_down):
    experts, features, _ = w_gate.shape
    me = lax.axis_index("expert")
    position = lax.axis_index("dp")
    side, pair = position % 2, position // 2 % 2
    tokens = out_grad.shape[0]
    half, quarter = tokens // 2, tokens // 4
    corner = side * 2 + pair

    def to_core(values):
        return tuple(flip(v, "expert", 1) for v in values)

    x_mine = [quarters(layer_input, tokens, q) for q in (corner, 3 - corner)]
    *x_mine, layer_input, out_grad, routes = lax.optimization_barrier(
        (*x_mine, layer_input, out_grad, routes)
    )
    x_across, x_corner = [flip(v, "expert", 2) for v in x_mine]
    x_sibling, g_sibling = to_core((layer_input, out_grad))
    x_sibling, routes = lax.optimization_barrier((x_sibling, routes))
    table = route_table(routes, gate_values)
    tables = []
    for r in range(4):
        part = lax.dynamic_slice_in_dim(table, (me ^ r) * experts, experts, 0)
        tables.append(flip(part, "expert", r) if r > 0 else part)
    x_across, tables[1] = lax.optimization_barrier((x_across, tables[1]))
    x_far = (x_across, x_corner, flip(x_across, "dp", 1), flip(x_across, "dp", 2))
    x_far = lax.optimization_barrier(x_far)
    g_across = flip(out_grad, "expert", 2)
    x_far = (*x_far, *to_core(x_far))
    table = jnp.stack(tables, axis=2)
    slot, weight = table[:, 0], table[:, 1]
    back = back_matrix(swap_order(slot, side, pair, 2))
    far = swap_order(slot[:, 2:], side, pair, 2).reshape(experts, 2, 4, quarter)
    far = jnp.stack([far[:, :, q] for q in (0, 3, 2, 1)], axis=2).reshape(experts, 2, tokens)
    slot_x = jnp.concatenate([slot[:, :2], far], axis=1)
    slot_x, back = lax.optimization_barrier((slot_x, back))
    rows, act, slope = forward((layer_input, x_sibling, *x_far), slot_x, w_gate, w_up)
    act, g_across = lax.optimization_barrier((act, g_across))
    gate_grad, up_grad = hidden_grads(
        (out_grad, g_sibling, g_across, *to_core((g_across,))), slot, weight, act, slope, w_down
    )

    groups = ((0, 2), (1, 3))
    kept_a, sent_a = input_sums(back, gate_grad, up_grad, w_gate, w_up, groups, 0, 2)
    kept_b, sent_b = input_sums(back, gate_grad, up_grad, w_gate, w_up, groups, 1, 2)

    def piece(after, before, *which):
        held, rows_now = lax.optimization_barrier((after, rows))
        return held, weight_grads(rows_now, gate_grad, up_grad, before, *which)

    def corners(value):
        z, x, diagonal = value
        x, diagonal = flip(x, "dp", 1), flip(diagonal, "dp", 3)
        return [flip(z, "dp", 2), x, diagonal]

    def cut(value, count):
        return [value[i : i + quarter] for i in range(0, count * quarter, quarter)]

    chip_a = add(kept_a, flip(sent_a, "expert", 1))
    got = flip(sent_b, "expert", 1)
    chip_b = [add(a, b) for a, b in zip(cut(kept_b, 8), cut(got, 8))]
    got_a = flip(chip_a[tokens:], "expert", 2)
    away = [jnp.concatenate([chip_b[q], chip_b[4 + q]], axis=0) for q in (1, 2, 3)]
    away, grads = piece(away, None, 0, 4)
    got_x = flip(away[1], "dp", 1)
    got_b = [flip(away[2], "dp", 3), flip(away[0], "dp", 2), got_x]
    got_a, got_b, *grads = lax.optimization_barrier((got_a, got_b, *grads))
    own_a = [add(a, b) for a, b in zip(cut(chip_a, 4), cut(got_a, 4))]
    mine_b = add(chip_b[0], *(v[:quarter] for v in got_b))
    far_b = add(chip_b[4], *(v[quarter:] for v in got_b))
    (far_b, *own_a), grads = piece((far_b, *own_a), grads, 4, 1)
    got_a, got_b = corners(own_a[1:]), flip(far_b, "expert", 2)
    got_a, got_b, *grads = lax.optimization_barrier((got_a, got_b, *grads))
    mine = jnp.concatenate([add(own_a[0], *got_a), add(mine_b, got_b)], axis=1)
    mine, grads = piece(mine, grads, 5, 4)
    got = flip(mine, "dp", 4)
    got, *grads = lax.optimization_barrier((got, *grads))
    mine = add(mine, got)
    mine, grads = piece(mine, grads, 9, 3)
    got = corners([mine] * 3)
    got, *grads = lax.optimization_barrier((got, *grads))
    total = swap_order(jnp.concatenate([mine, *got], axis=0), side, pair, 0)
    return (total, *grads)


def local_any(out_grad, routes, gate_values, layer_input, w_gate, w_up, w_down):
    experts = w_gate.shape[0]
    me = lax.axis_index("expert")
    rows_in = lax.all_gather(layer_input, "expert", tiled=True)
    grads_in = lax.all_gather(out_grad, "expert", tiled=True)
    table = lax.all_gather(route_table(routes, gate_values), "expert")
    table = lax.dynamic_slice_in_dim(table, me * experts, experts, 1).transpose(1, 2, 0, 3)
    slot, weight = table[:, 0], table[:, 1]
    rows, act, slope = forward([rows_in], slot, w_gate, w_up)
    gate_grad, up_grad = hidden_grads([grads_in], slot, weight, act, slope, w_down)
    groups = (tuple(range(slot.shape[1])),)
    (sums,) = input_sums(back_matrix(slot), gate_grad, up_grad, w_gate, w_up, groups, 0, 1)
    blocks = experts * layer_input.shape[1] // FEATURE_TILE
    grads = weight_grads(rows, gate_grad, up_grad, None, 0, blocks)
    own = lax.psum_scatter(sums, "expert", scatter_dimension=0, tiled=True)
    return (lax.psum(own, "dp"), *grads)


def solution(mesh):
    near = mesh.shape["dp"] == 8 and mesh.shape["expert"] == 4
    placed = (
        P("expert", None),
        P("expert", None),
        P("expert", None),
        P("expert", None),
        P("expert", None, "dp"),
        P("expert", None, "dp"),
        P("expert", None, "dp"),
    )
    return jax.shard_map(
        local_near if near else local_any,
        mesh=mesh,
        in_specs=placed,
        out_specs=(P("expert", None), P("expert", None, "dp"), P("expert", None, "dp")),
        check_vma=False,
    )
```

```python
import functools

import jax
import jax.numpy as jnp
from jax import lax
from jax.experimental import pallas as pl
from jax.experimental.pallas import tpu as pltpu
from jax.sharding import PartitionSpec as P

EXPERTS = 8
MOST = 80
UNIT_TILE = 512
HIDDEN_TILE = 1024
FEATURE_TILE = 512
BF16 = jnp.bfloat16
F32 = jnp.float32
NN = (((1,), (0,)), ((), ()))
NT = (((1,), (1,)), ((), ()))
TN = (((0,), (0,)), ((), ()))


def dot(a, b, dims=NN):
    return lax.dot_general(a, b, dims, preferred_element_type=F32)


def params(count, mebibytes):
    return pltpu.CompilerParams(
        dimension_semantics=("arbitrary",) * count, vmem_limit_bytes=mebibytes * 1024 * 1024
    )


def whole(shape):
    return pl.BlockSpec(
        shape, lambda *_: (0,) * len(shape), pipeline_mode=pl.Buffered(buffer_count=1)
    )


def one_hot(slot_row):
    slots = lax.broadcasted_iota(jnp.int32, (MOST, slot_row.shape[1]), 0)
    return slots == slot_row.astype(jnp.int32)


def lay_out(held, pieces, first):
    rows, at = held.shape[0], 0
    for piece in pieces:
        low, high = max(first, at), min(first + rows, at + piece.shape[0])
        if low < high:
            held[low - first : high - first] = piece[low - at : high - at]
        at += piece.shape[0]


def column_chunks(features):
    step = 768 if features % 768 == 0 else features
    return [slice(c, c + step) for c in range(0, features, step)]


def dispatch(pieces, slot, held, chosen, out, weight=None):
    experts, blocks, tokens = slot.shape
    group = held.shape[0] // tokens
    places = [(l, b) for l in range(experts) for b in range(group)]
    for start in range(0, blocks, group):
        chosen[...] = jnp.zeros_like(chosen)
        scales = []
        for i, (l, b) in enumerate(places):
            at = slice(start + b, start + b + 1)
            mask = one_hot(slot[l, at, :])
            chosen[i * MOST : (i + 1) * MOST, b * tokens : (b + 1) * tokens] = mask.astype(BF16)
            if weight is not None:
                scales.append(
                    jnp.sum(jnp.where(mask, weight[l, at, :], 0.0), axis=1, keepdims=True)
                )
        lay_out(held, pieces, start * tokens)
        for cols in column_chunks(held.shape[1]):
            taken = dot(chosen[...], held[:, cols])
            for i, (l, b) in enumerate(places):
                part = taken[i * MOST : (i + 1) * MOST]
                if scales:
                    part = part * scales[i]
                span = slice((start + b) * MOST, (start + b + 1) * MOST)
                out[l, span, cols] = part.astype(BF16)


def dispatch_scratch(experts, blocks, tokens, features):
    group = 2 if blocks % 2 == 0 else 1
    return [
        pltpu.VMEM((group * tokens, features), BF16),
        pltpu.VMEM((experts * group * MOST, group * tokens), BF16),
        pltpu.VMEM((experts, blocks * MOST, features), BF16),
    ]


def weight_tiles(step, matrices, buffers, ready):
    _, features, tile = buffers[0].shape
    tiles = matrices[0].shape[2] // tile
    cols = pl.ds(pl.multiple_of(step % tiles * tile, tile), tile)
    return [
        pltpu.make_async_copy(
            matrix.at[step // tiles, :, cols], buffer.at[step % 2], ready.at[step % 2, i]
        )
        for i, (matrix, buffer) in enumerate(zip(matrices, buffers))
    ]


def next_tiles(step, matrices, buffers, ready):
    @pl.when(step + 1 < pl.num_programs(0))
    def _():
        for copy in weight_tiles(step + 1, matrices, buffers, ready):
            copy.start()

    for copy in weight_tiles(step, matrices, buffers, ready):
        copy.wait()


def forward_kernel(count, *refs):
    pieces, (slot, w_gate, w_up, rows_out, act, slope) = refs[:count], refs[count : count + 6]
    held, chosen, rows, sent = refs[count + 6 :]
    expert, tile = pl.program_id(0), pl.program_id(1)
    copy = pltpu.make_async_copy(rows, rows_out, sent)

    @pl.when((expert == 0) & (tile == 0))
    def _():
        dispatch(pieces, slot, held, chosen, rows)
        copy.start()

    x = rows[expert]
    gate = dot(x, w_gate[0])
    up = dot(x, w_up[0])
    sig = jax.nn.sigmoid(gate)
    act[0] = gate * sig
    slope[0] = up * sig * (1.0 + gate * (1.0 - sig))

    @pl.when((expert == pl.num_programs(0) - 1) & (tile == pl.num_programs(1) - 1))
    def _():
        copy.wait()


def forward(pieces, slot, w_gate, w_up):
    experts, blocks, tokens = slot.shape
    _, features, units = w_gate.shape
    tile = min(UNIT_TILE, units)
    slots = blocks * MOST
    matrix = pl.BlockSpec((1, features, tile), lambda l, f: (l, 0, f))
    unit = pl.BlockSpec((1, slots, tile), lambda l, f: (l, 0, f))
    return pl.pallas_call(
        functools.partial(forward_kernel, len(pieces)),
        grid=(experts, units // tile),
        in_specs=[whole(p.shape) for p in pieces] + [whole(slot.shape), matrix, matrix],
        out_specs=[pl.BlockSpec(memory_space=pltpu.HBM), unit, unit],
        out_shape=[
            jax.ShapeDtypeStruct((experts, slots, features), BF16),
            jax.ShapeDtypeStruct((experts, slots, units), F32),
            jax.ShapeDtypeStruct((experts, slots, units), F32),
        ],
        scratch_shapes=dispatch_scratch(experts, blocks, tokens, features)
        + [pltpu.SemaphoreType.DMA],
        compiler_params=params(2, 52),
        cost_estimate=pl.CostEstimate(
            flops=4 * experts * slots * features * units,
            bytes_accessed=4 * experts * features * units,
            transcendentals=experts * slots * units,
        ),
    )(*pieces, slot, w_gate, w_up)


def hidden_kernel(count, *refs):
    pieces, (slot, weight, act, slope, w_down) = refs[:count], refs[count : count + 5]
    gate_grad, up_grad, held, chosen, grads, downs, ready = refs[count + 5 :]
    step = pl.program_id(0)
    tiles = pl.num_programs(0) // grads.shape[0]
    fetching = ((w_down,), (downs,), ready)

    @pl.when(step == 0)
    def _():
        for first in weight_tiles(step, *fetching):
            first.start()
        dispatch(pieces, slot, held, chosen, grads, weight)

    next_tiles(step, *fetching)
    hidden = dot(grads[step // tiles], downs[step % 2])
    up_grad[0] = (hidden * act[0]).astype(BF16)
    gate_grad[0] = (hidden * slope[0]).astype(BF16)


def hidden_grads(pieces, slot, weight, act, slope, w_down):
    experts, blocks, tokens = slot.shape
    _, features, units = w_down.shape
    tile = min(HIDDEN_TILE, units)
    tiles = units // tile
    slots = blocks * MOST
    unit = pl.BlockSpec((1, slots, tile), lambda i: (i // tiles, 0, i % tiles))
    return pl.pallas_call(
        functools.partial(hidden_kernel, len(pieces)),
        grid=(experts * tiles,),
        in_specs=[whole(p.shape) for p in pieces]
        + [whole(slot.shape), whole(slot.shape), unit, unit, pl.BlockSpec(memory_space=pl.ANY)],
        out_specs=[unit, unit],
        out_shape=[jax.ShapeDtypeStruct((experts, slots, units), BF16)] * 2,
        scratch_shapes=dispatch_scratch(experts, blocks, tokens, features)
        + [pltpu.VMEM((2, features, tile), BF16), pltpu.SemaphoreType.DMA((2, 1))],
        compiler_params=params(1, 48),
        cost_estimate=pl.CostEstimate(
            flops=2 * experts * slots * features * units,
            bytes_accessed=2 * experts * features * units,
            transcendentals=0,
        ),
    )(*pieces, slot, weight, act, slope, w_down)


def inputs_kernel(groups, back, gate_grad, up_grad, w_gate, w_up, *refs):
    sums, held = refs[:-1], refs[-1]
    blocks, tokens, _ = back.shape
    for l in range(gate_grad.shape[0]):
        partial = dot(gate_grad[l], w_gate[l], NT) + dot(up_grad[l], w_up[l], NT)
        for b in range(blocks):
            held[b, l * MOST : (l + 1) * MOST] = partial[b * MOST : (b + 1) * MOST].astype(BF16)
    for out, members in zip(sums, groups):
        for place, b in enumerate(members):
            out[place * tokens : (place + 1) * tokens] = dot(back[b], held[b]).astype(BF16)


def input_sums(back, gate_grad, up_grad, w_gate, w_up, groups, part, parts):
    blocks, tokens, _ = back.shape
    experts, features, units = w_gate.shape
    wide = FEATURE_TILE
    steps = features // parts // wide
    slots = blocks * MOST
    across = pl.BlockSpec((experts, wide, units), lambda i: (0, part * steps + i, 0))
    return pl.pallas_call(
        functools.partial(inputs_kernel, groups),
        grid=(steps,),
        in_specs=[whole(back.shape), whole(gate_grad.shape), whole(up_grad.shape), across, across],
        out_specs=[pl.BlockSpec((len(g) * tokens, wide), lambda i: (0, i)) for g in groups],
        out_shape=[
            jax.ShapeDtypeStruct((len(g) * tokens, features // parts), BF16) for g in groups
        ],
        scratch_shapes=[pltpu.VMEM((blocks, experts * MOST, wide), BF16)],
        compiler_params=params(1, 40),
        cost_estimate=pl.CostEstimate(
            flops=4 * experts * slots * features * units // parts,
            bytes_accessed=4 * experts * features * units // parts,
            transcendentals=0,
        ),
    )(back, gate_grad, up_grad, w_gate, w_up)


def back_matrix(slot):
    places = jnp.arange(MOST, dtype=F32)
    slot = lax.optimization_barrier(slot.transpose(1, 2, 0))
    parts = [slot[..., l : l + 1] == places for l in range(slot.shape[2])]
    return jnp.concatenate([p.astype(BF16) for p in parts], axis=2)


def weights_kernel(rows, gate_grad, up_grad, *refs):
    grad_gate, grad_up = refs[-2:]
    grad_gate[0] = dot(rows[0], gate_grad[0], TN)
    grad_up[0] = dot(rows[0], up_grad[0], TN)


def weight_grads(rows, gate_grad, up_grad, before, first, steps):
    experts, slots, features = rows.shape
    units = gate_grad.shape[2]
    wide = FEATURE_TILE
    each = features // wide
    unit = pl.BlockSpec((1, slots, units), lambda i: ((first + i) // each, 0, 0))
    out = pl.BlockSpec((1, wide, units), lambda i: ((first + i) // each, (first + i) % each, 0))
    kept = [] if before is None else list(before)
    return pl.pallas_call(
        weights_kernel,
        grid=(steps,),
        in_specs=[
            pl.BlockSpec((1, slots, wide), lambda i: ((first + i) // each, 0, (first + i) % each)),
            unit,
            unit,
        ]
        + [pl.BlockSpec(memory_space=pl.ANY)] * len(kept),
        out_specs=[out, out],
        out_shape=[jax.ShapeDtypeStruct((experts, features, units), F32)] * 2,
        input_output_aliases={3 + i: i for i in range(len(kept))},
        compiler_params=params(1, 30),
        cost_estimate=pl.CostEstimate(
            flops=4 * slots * steps * wide * units,
            bytes_accessed=8 * steps * wide * units,
            transcendentals=0,
        ),
    )(rows, gate_grad, up_grad, *kept)


def route_table(routes, gate_values):
    tokens = routes.shape[0]
    experts = jnp.arange(EXPERTS, dtype=jnp.int32)[:, None, None]
    match = routes.T[None] == experts
    member = jnp.any(match, axis=1)
    gate = jnp.sum(jnp.where(match, gate_values.T[None], 0.0), axis=1)
    place = jnp.arange(tokens, dtype=jnp.int32)
    earlier = (place[:, None] < place[None, :]).astype(BF16)
    slot = jnp.where(member, dot(member.astype(BF16), earlier), -1.0)
    return jnp.stack([slot, gate], axis=1)


def flip(value, axis, bit):
    count = lax.axis_size(axis)
    return lax.ppermute(value, axis, [(i, i ^ bit) for i in range(count)])


def swap_order(value, side, pair, dim):
    shape = value.shape
    value = value.reshape(shape[:dim] + (2, 2, shape[dim] // 4) + shape[dim + 1 :])
    value = jnp.where(side == 1, jnp.flip(value, dim), value)
    return jnp.where(pair == 1, jnp.flip(value, dim + 1), value).reshape(shape)


def add(*terms):
    total = terms[0].astype(F32)
    for term in terms[1:]:
        total = total + term.astype(F32)
    return total.astype(BF16)


def quarters(value, count, at):
    return lax.dynamic_slice_in_dim(value, at * (count // 4), count // 4, 0)


def local_near(out_grad, routes, gate_values, layer_input, w_gate, w_up, w_down):
    experts, features, _ = w_gate.shape
    me = lax.axis_index("expert")
    position = lax.axis_index("dp")
    side, pair = position % 2, position // 2 % 2
    tokens = out_grad.shape[0]
    half, quarter = tokens // 2, tokens // 4
    corner = side * 2 + pair

    def to_core(values):
        return tuple(flip(v, "expert", 1) for v in values)

    x_mine = [quarters(layer_input, tokens, q) for q in (corner, 3 - corner)]
    *x_mine, layer_input, out_grad, routes = lax.optimization_barrier(
        (*x_mine, layer_input, out_grad, routes)
    )
    x_across, x_corner = [flip(v, "expert", 2) for v in x_mine]
    x_sibling, g_sibling = to_core((layer_input, out_grad))
    x_sibling, routes = lax.optimization_barrier((x_sibling, routes))
    table = route_table(routes, gate_values)
    tables = []
    for r in range(4):
        part = lax.dynamic_slice_in_dim(table, (me ^ r) * experts, experts, 0)
        tables.append(flip(part, "expert", r) if r > 0 else part)
    x_far = (x_across, x_corner, flip(x_across, "dp", 1), flip(x_across, "dp", 2))
    g_across = flip(out_grad, "expert", 2)
    x_far = (*x_far, *to_core(x_far))
    table = jnp.stack(tables, axis=2)
    slot, weight = table[:, 0], table[:, 1]
    back = back_matrix(swap_order(slot, side, pair, 2))
    far = swap_order(slot[:, 2:], side, pair, 2).reshape(experts, 2, 4, quarter)
    far = jnp.stack([far[:, :, q] for q in (0, 3, 2, 1)], axis=2).reshape(experts, 2, tokens)
    slot_x = jnp.concatenate([slot[:, :2], far], axis=1)
    slot_x, back = lax.optimization_barrier((slot_x, back))
    rows, act, slope = forward((layer_input, x_sibling, *x_far), slot_x, w_gate, w_up)
    act, g_across = lax.optimization_barrier((act, g_across))
    gate_grad, up_grad = hidden_grads(
        (out_grad, g_sibling, g_across, *to_core((g_across,))), slot, weight, act, slope, w_down
    )

    groups = ((0, 2), (1, 3))
    kept_a, sent_a = input_sums(back, gate_grad, up_grad, w_gate, w_up, groups, 0, 2)
    kept_b, sent_b = input_sums(back, gate_grad, up_grad, w_gate, w_up, groups, 1, 2)

    def piece(after, before, *which):
        held, rows_now = lax.optimization_barrier((after, rows))
        return held, weight_grads(rows_now, gate_grad, up_grad, before, *which)

    def corners(value):
        z, x, diagonal = value
        x, diagonal = flip(x, "dp", 1), flip(diagonal, "dp", 3)
        return [flip(z, "dp", 2), x, diagonal]

    def cut(value, count):
        return [value[i : i + quarter] for i in range(0, count * quarter, quarter)]

    chip_a = add(kept_a, flip(sent_a, "expert", 1))
    got = flip(sent_b, "expert", 1)
    chip_b = [add(a, b) for a, b in zip(cut(kept_b, 8), cut(got, 8))]
    got_a = flip(chip_a[tokens:], "expert", 2)
    away = [jnp.concatenate([chip_b[q], chip_b[4 + q]], axis=0) for q in (1, 2, 3)]
    away, grads = piece(away, None, 0, 4)
    got_x = flip(away[1], "dp", 1)
    got_b = [flip(away[2], "dp", 3), flip(away[0], "dp", 2), got_x]
    got_a, got_b, *grads = lax.optimization_barrier((got_a, got_b, *grads))
    own_a = [add(a, b) for a, b in zip(cut(chip_a, 4), cut(got_a, 4))]
    mine_b = add(chip_b[0], *(v[:quarter] for v in got_b))
    far_b = add(chip_b[4], *(v[quarter:] for v in got_b))
    (far_b, *own_a), grads = piece((far_b, *own_a), grads, 4, 1)
    got_a, got_b = corners(own_a[1:]), flip(far_b, "expert", 2)
    got_a, got_b, *grads = lax.optimization_barrier((got_a, got_b, *grads))
    mine = jnp.concatenate([add(own_a[0], *got_a), add(mine_b, got_b)], axis=1)
    mine, grads = piece(mine, grads, 5, 4)
    got = flip(mine, "dp", 4)
    got, *grads = lax.optimization_barrier((got, *grads))
    mine = add(mine, got)
    mine, grads = piece(mine, grads, 9, 3)
    got = corners([mine] * 3)
    got, *grads = lax.optimization_barrier((got, *grads))
    total = swap_order(jnp.concatenate([mine, *got], axis=0), side, pair, 0)
    return (total, *grads)


def local_any(out_grad, routes, gate_values, layer_input, w_gate, w_up, w_down):
    experts = w_gate.shape[0]
    me = lax.axis_index("expert")
    rows_in = lax.all_gather(layer_input, "expert", tiled=True)
    grads_in = lax.all_gather(out_grad, "expert", tiled=True)
    table = lax.all_gather(route_table(routes, gate_values), "expert")
    table = lax.dynamic_slice_in_dim(table, me * experts, experts, 1).transpose(1, 2, 0, 3)
    slot, weight = table[:, 0], table[:, 1]
    rows, act, slope = forward([rows_in], slot, w_gate, w_up)
    gate_grad, up_grad = hidden_grads([grads_in], slot, weight, act, slope, w_down)
    groups = (tuple(range(slot.shape[1])),)
    (sums,) = input_sums(back_matrix(slot), gate_grad, up_grad, w_gate, w_up, groups, 0, 1)
    blocks = experts * layer_input.shape[1] // FEATURE_TILE
    grads = weight_grads(rows, gate_grad, up_grad, None, 0, blocks)
    own = lax.psum_scatter(sums, "expert", scatter_dimension=0, tiled=True)
    return (lax.psum(own, "dp"), *grads)


def solution(mesh):
    near = mesh.shape["dp"] == 8 and mesh.shape["expert"] == 4
    placed = (
        P("expert", None),
        P("expert", None),
        P("expert", None),
        P("expert", None),
        P("expert", None, "dp"),
        P("expert", None, "dp"),
        P("expert", None, "dp"),
    )
    return jax.shard_map(
        local_near if near else local_any,
        mesh=mesh,
        in_specs=placed,
        out_specs=(P("expert", None), P("expert", None, "dp"), P("expert", None, "dp")),
        check_vma=False,
    )
```
